128 devices in a mesh: pipe: 4 (over x), dp: 32 (over z, y, core).
Axes of the slice: x: 4, y: 4, z: 4, core: 2. Of those that a mesh axis runs over, the one named last changes fastest.
Arguments:
- tokens: bfloat16 [4096, 1024], P('dp'), may hold values from -6 to 6
- cotangent: bfloat16 [4096, 1024], P('dp'), may hold values from -6 to 6
- live_counts: int32 [64], P('dp'), may hold values from 32 to 64, as said below
- segments: int32 [4096], P('dp'), may hold values from 0 to 255, never falling along the last dimension, each value on 1 to 64 neighbouring positions
- attn_input: bfloat16 [4, 1024, 3072], P('pipe', None, 'dp'), may hold values from -0.1875 to 0.1875
- attn_output: bfloat16 [4, 1024, 1024], P('pipe', None, 'dp'), may hold values from -0.1875 to 0.1875
- feed_up: bfloat16 [4, 1024, 4096], P('pipe', None, 'dp'), may hold values from -0.1875 to 0.1875
- feed_down: bfloat16 [4, 4096, 1024], P('pipe', None, 'dp'), may hold values from -0.09375 to 0.09375
- norm_gains: bfloat16 [4, 3, 1024], P('pipe', None, 'dp'), may hold values from 0.5 to 1.5
- vector_bias: bfloat16 [4, 7, 1024], P('pipe', None, 'dp'), may hold values from -2 to 2
- mid_gain: bfloat16 [4, 4096], P('pipe', 'dp'), may hold values from 0.5 to 1.5
- mid_bias: bfloat16 [4, 2, 4096], P('pipe', None, 'dp'), may hold values from -2 to 2
- head_scale: bfloat16 [4, 16], P('pipe'), may hold values from 0.25 to 1.75
Outputs:
- section_outputs: bfloat16 [4, 4096, 1024], P('pipe', 'dp')
- input_grads: bfloat16 [4, 4096, 1024], P('pipe', 'dp')
- grad_attn_input: float32 [4, 1024, 3072], P('pipe', None, 'dp')
- grad_attn_output: float32 [4, 1024, 1024], P('pipe', None, 'dp')
- grad_feed_up: float32 [4, 1024, 4096], P('pipe', None, 'dp')
- grad_feed_down: float32 [4, 4096, 1024], P('pipe', None, 'dp')
- grad_norm_gains: float32 [4, 3, 1024], P('pipe', None, 'dp')
- grad_vector_bias: float32 [4, 7, 1024], P('pipe', None, 'dp')
- grad_mid_gain: float32 [4, 4096], P('pipe', 'dp')
- grad_mid_bias: float32 [4, 2, 4096], P('pipe', None, 'dp')
- grad_head_scale: float32 [4, 16], P('pipe')
The draws below stay inside these ranges and needn't reach their ends.
Inputs may be any that keep to these rules, and one draw needn't show every extreme that they name: `live_counts`: some pack holds 64 live tokens.
All inputs are finite; a program needn't handle non-finite values.
Results may differ from the reference program's by a relative error of at most 0.035.
Values may be sent and summed in bfloat16 or wider, within the bound.
A program may use at most 960 MiB of HBM per device.

```python
import math
import jax
import jax.numpy as jnp
import numpy as np
from jax import lax

D = 1024
HEADS = 16
FF = 4096
LAYERS = 4
PACK = 64
TOKENS = 4096


def draw_live_counts(key, part):
    key = jax.random.fold_in(key, 7)
    key_values, key_shuffle = jax.random.split(key)
    count_packs = TOKENS // PACK
    values = jax.random.randint(key_values, (count_packs,), PACK // 2, PACK + 1)
    shuffled = jax.random.permutation(key_shuffle, count_packs)
    values = values.at[shuffled[0]].set(PACK)
    values = values.at[shuffled[1]].set(PACK // 2)
    return values.astype(jnp.int32)


def block_scale(rng, shape, shards, low, largest):
    loudness, own = 1.0, jax.random.fold_in(rng, 6)
    for dim, shards_of in shards:
        draws = jnp.exp(jax.random.uniform(jax.random.fold_in(own, dim), (shards_of,), jnp.float32, low / len(shards), largest / len(shards)))
        loudness = loudness * jnp.repeat(draws, shape[dim] // shards_of).reshape([-1 if axis == dim else 1 for axis in range(len(shape))])
    return loudness


def profile(number_of, total, reach, slope):
    weights = [(1 << 20) // math.isqrt(rank ** slope) + 1 for rank in range(2, number_of + 1)]
    spare, given = total - reach - (number_of - 1), [1] * (number_of - 1)
    while spare > 0:
        candidates = [i for i in range(number_of - 1) if given[i] < reach]
        mass, left = sum([weights[i] for i in candidates]), spare
        for i in candidates:
            addition = min(reach - given[i], max(1, left * weights[i] // mass), spare)
            given[i] = given[i] + addition
            spare = spare - addition
    return np.array([reach] + given)


def uneven_parts(stream_key, count, total, bound, lean):
    if count == 2:
        one = jax.random.randint(stream_key, (), max(1, total - bound), min(bound, total - 1) + 1)
        return jnp.stack([one, total - one])
    tallies = jnp.asarray(profile(count, total, bound, lean), jnp.int32)
    couples = (count - 1) // 2
    giver, taker = tallies[1:1 + 2 * couples:2], tallies[2:2 + 2 * couples:2]
    room = jnp.minimum(giver - 1, bound - taker)
    passed = jax.random.randint(jax.random.fold_in(stream_key, 1), (couples,), 0, 1 << 20) % (room + 1)
    tallies = tallies.at[1:1 + 2 * couples:2].set(giver - passed).at[2:2 + 2 * couples:2].set(taker + passed)
    return tallies[jax.random.permutation(jax.random.fold_in(stream_key, 2), count)]


def noise(stream_key, dims, scale, limit, cuts=(), dtype=jnp.bfloat16):
    values = jax.random.normal(stream_key, dims, jnp.float32) * scale
    if len(cuts) > 0:
        values = block_scale(stream_key, dims, cuts, -0.22, 0.18) * values
    return jnp.clip(values, min=-limit, max=limit).astype(dtype)


def setup_inputs(seed: int = 0) -> dict:
    streams_of = jax.random.split(jax.random.key(seed), 14)
    tokens = noise(streams_of[0], (TOKENS, D), 1.0, 6.0, ((0, 32),))
    cotangent = noise(streams_of[1], (TOKENS, D), 1.0, 6.0, ((0, 32),))
    live_counts = draw_live_counts(jax.random.fold_in(streams_of[13], 71), 0)
    segments = jnp.searchsorted(jnp.cumsum(uneven_parts(streams_of[3], TOKENS * 4 // PACK, TOKENS, PACK, 0)), jnp.arange(TOKENS), side="right").astype(jnp.int32)
    attn_input = noise(streams_of[4], (LAYERS, D, 3 * D), D ** -0.5, 0.1875, ((0, 4), (2, 32)))
    attn_output = noise(streams_of[5], (LAYERS, D, D), D ** -0.5, 0.1875, ((0, 4), (2, 32)))
    feed_up = noise(streams_of[6], (LAYERS, D, FF), D ** -0.5, 0.1875, ((0, 4), (2, 32)))
    feed_down = noise(streams_of[7], (LAYERS, FF, D), FF ** -0.5, 0.09375, ((0, 4), (2, 32)))
    norm_gains = jnp.clip(1.0 + 0.1 * jax.random.normal(streams_of[8], (LAYERS, 3, D), jnp.float32), 0.5, 1.5).astype(jnp.bfloat16)
    vector_bias = noise(streams_of[9], (LAYERS, 7, D), 0.3, 2.0, ((0, 4), (2, 32)))
    mid_gain = jnp.clip(1.0 + 0.1 * jax.random.normal(streams_of[10], (LAYERS, FF), jnp.float32), 0.5, 1.5).astype(jnp.bfloat16)
    mid_bias = noise(streams_of[11], (LAYERS, 2, FF), 0.3, 2.0, ((0, 4), (2, 32)))
    head_scale = jnp.clip(1.0 + 0.15 * jax.random.normal(streams_of[12], (LAYERS, HEADS), jnp.float32), 0.25, 1.75).astype(jnp.bfloat16)
    return dict(tokens=tokens, cotangent=cotangent, live_counts=live_counts, segments=segments, attn_input=attn_input, attn_output=attn_output, feed_up=feed_up, feed_down=feed_down, norm_gains=norm_gains, vector_bias=vector_bias, mid_gain=mid_gain, mid_bias=mid_bias, head_scale=head_scale)


@jax.custom_vjp
def low(v):
    return lax.optimization_barrier(v.astype(jnp.bfloat16)).astype(jnp.float32)

@jax.custom_vjp
def low_back(v):
    return v

def low_keep(v):
    return (low(v), None)

def low_pass(kept, grad):
    return (grad,)

def back_keep(v):
    return (v, None)

def back_low(kept, grad):
    return (low(grad),)
low.defvjp(low_keep, low_pass)
low_back.defvjp(back_keep, back_low)
epsilon = 1e-05
highest = lax.Precision.HIGHEST

def norm_rows(values, gain_row, bias_row):
    center = values - lax.optimization_barrier(jnp.mean(values, axis=-1, keepdims=True))
    spread = lax.optimization_barrier(jnp.mean(center * center, axis=-1, keepdims=True))
    return center * lax.rsqrt(spread + epsilon) * gain_row + bias_row

def layer_apply(state, allowed, in_weight, out_weight, up_weight, down_weight, gains, biases, inner_gain, inner_bias, scales):
    num_packs, pack_rows, model_width = state.shape
    head_count = scales.shape[0]
    head_size = model_width // head_count
    normed = low(norm_rows(state, gains[0], biases[0]))
    qkv_bias = jnp.concatenate([biases[1], jnp.zeros_like(biases[1]), biases[2]])
    qkv_all = low_back(low(jnp.einsum('npd,de->npe', normed, in_weight, precision=highest) + qkv_bias))
    query_rows = qkv_all[..., :model_width].reshape(num_packs, pack_rows, head_count, head_size)
    key_rows = qkv_all[..., model_width:2 * model_width].reshape(num_packs, pack_rows, head_count, head_size)
    value_rows = qkv_all[..., 2 * model_width:].reshape(num_packs, pack_rows, head_count, head_size)
    scores = jnp.einsum('nqhd,nkhd->nhqk', query_rows, key_rows, precision=highest) * head_size ** (-0.5)
    scores = low_back(scores)
    scores = jnp.where(allowed[:, None], scores, -1000000000.0)
    top_score = lax.optimization_barrier(jnp.max(scores, axis=-1, keepdims=True))
    expo_scores = jnp.exp(scores - top_score)
    attn_probs = expo_scores / lax.optimization_barrier(jnp.sum(expo_scores, axis=-1, keepdims=True))
    mixed_heads = jnp.einsum('nhqk,nkhd->nqhd', low(attn_probs), value_rows, precision=highest)
    mixed_heads = low_back(mixed_heads)
    scaled = low((mixed_heads * scales[:, None]).reshape(num_packs, pack_rows, model_width))
    attn_rows = low_back(jnp.einsum('npd,de->npe', scaled, out_weight, precision=highest) + biases[3])
    middle = state + norm_rows(attn_rows, gains[1], biases[4])
    normed_two = low(norm_rows(middle, gains[2], biases[5]))
    hidden = low_back(jnp.einsum('npd,df->npf', normed_two, up_weight, precision=highest) + inner_bias[0])
    inner = low(norm_rows(jax.nn.gelu(hidden), inner_gain, inner_bias[1]))
    return middle + jnp.einsum('npf,fd->npd', inner, down_weight, precision=highest) + biases[6]

def reference(tokens, cotangent, live_counts, segments, attn_input, attn_output, feed_up, feed_down, norm_gains, vector_bias, mid_gain, mid_bias, head_scale):
    num_packs = TOKENS // PACK
    start = tokens.astype(jnp.float32).reshape(num_packs, PACK, D)
    seg_rows = segments.reshape(num_packs, PACK)
    positions = jnp.arange(PACK)
    causal = positions[:, None] >= positions[None, :]
    allowed = causal[None] & (seg_rows[:, :, None] == seg_rows[:, None, :])
    live_mask = (positions[None, :] < live_counts[:, None]).astype(jnp.float32)
    params = tuple((p.astype(jnp.float32) for p in (attn_input, attn_output, feed_up, feed_down, norm_gains, vector_bias, mid_gain, mid_bias, head_scale)))
    probes = jnp.zeros((LAYERS - 1, num_packs, PACK, D), jnp.float32)

    def forward(first, weights, probe_rows):
        state = low_back(first)
        layer_outs = []
        for layer_id in range(LAYERS):
            picked = [w[layer_id] for w in weights]
            state = low(layer_apply(state, allowed, *picked))
            layer_outs.append(state)
            if layer_id + 1 < LAYERS:
                state = low_back(state + probe_rows[layer_id])
        return (state, jnp.stack(layer_outs))
    final_state, pullback, layer_outs = jax.vjp(forward, start, params, probes, has_aux=True)
    grad_seed_rows = cotangent.astype(jnp.float32).reshape(num_packs, PACK, D) * live_mask[..., None]
    grad_start, grad_params, grad_probes = pullback(grad_seed_rows)
    section_outputs = layer_outs.reshape(LAYERS, TOKENS, D).astype(jnp.bfloat16)
    input_grads = jnp.concatenate([grad_start[None], grad_probes], axis=0).reshape(LAYERS, TOKENS, D).astype(jnp.bfloat16)
    return (section_outputs, input_grads, grad_params[0], grad_params[1], grad_params[2], grad_params[3], grad_params[4], grad_params[5], grad_params[6], grad_params[7], grad_params[8])
```

```python
import functools

import jax
import jax.numpy as jnp
from jax import lax
from jax.experimental import pallas as pl
from jax.experimental.pallas import tpu as pltpu
from jax.sharding import PartitionSpec as P

MESH = pl.DeviceIdType.MESH
EPS = 1e-05
F32, BF16 = jnp.float32, jnp.bfloat16
VMEM_LIMIT = 60 * 1024 * 1024

S, A, B, C, D = range(5)
ROWS = (16, 96, 32, 128, 32)
COLS = (128, 1024, 1024, 1024, 4096)
TYPES = (F32, BF16, BF16, BF16, BF16)
TOK, WIDTH, FF, QKV = 128, 1024, 4096, 3072
OFFS = (0, 3, 1, 2)


class Place:
    def __init__(self):
        self.s = lax.axis_index("pipe")
        d = lax.axis_index("dp")
        self.d = d
        self.c = d % 2
        y, z = (d // 2) % 4, d // 8
        self.f = y + self.c * (z - y)
        self.g = z + self.c * (y - z)
        self.sf = 2 + 6 * self.c
        self.sg = 8 - 6 * self.c
        self.sib = d + 1 - 2 * self.c

    def dp(self, of, og):
        return ((self.f + of) % 4) * self.sf + ((self.g + og) % 4) * self.sg + self.c

    def sib_dp(self, of, og):
        return ((self.g + of) % 4) * self.sg + ((self.f + og) % 4) * self.sf + 1 - self.c

    def barrier(self, along_pipe):
        sem = pltpu.get_barrier_semaphore()
        near = [self.dp(1, 0), self.dp(3, 0), self.dp(0, 1), self.dp(0, 3), self.sib]
        for to in near:
            pl.semaphore_signal(sem, inc=1, device_id=(self.s, to), device_id_type=MESH)
        if along_pipe:
            for by in (1, 3):
                pl.semaphore_signal(sem, inc=1, device_id=((self.s + by) % 4, self.d), device_id_type=MESH)
        pl.semaphore_wait(sem, 7 if along_pipe else 5)


def part(ref, rows, d, half):
    if half is None:
        return ref.at[pl.ds(pl.multiple_of(d * rows, rows), rows)]
    h = rows // 2
    return ref.at[pl.ds(pl.multiple_of(d * rows + half * h, h), h)]


def remote(src, dst, send, recv, s, to):
    return pltpu.make_async_remote_copy(
        src_ref=src, dst_ref=dst, send_sem=send, recv_sem=recv, device_id=(s, to), device_id_type=MESH
    )


class Gather:
    def __init__(self, place, bufs, send, recv):
        self.p, self.bufs, self.send, self.recv = place, bufs, send, recv
        self.open = []

    def put(self, k, slot, d, half, to):
        ref = part(self.bufs[k], ROWS[k], d, half)
        copy = remote(ref, ref, self.send.at[k, slot], self.recv.at[k, slot], self.p.s, to)
        copy.start()
        self.open.append(copy)

    def got(self, k, slot, d, half):
        ref = part(self.bufs[k], ROWS[k], d, half)
        remote(ref, ref, self.send.at[k, slot], self.recv.at[k, slot], self.p.s, self.p.sib).wait_recv()

    def spread(self, k, j):
        p = self.p
        d = p.dp(OFFS[j], 0)
        self.put(k, 4 + 4 * j, d, None, p.dp(0, 1))
        self.put(k, 5 + 4 * j, d, None, p.dp(0, 3))
        self.put(k, 20 + 4 * j, d, None, p.sib)

    def first(self, k):
        p = self.p
        self.put(k, 0, p.d, None, p.dp(1, 0))
        self.put(k, 1, p.d, None, p.dp(3, 0))
        self.spread(k, 0)

    def ring(self, k):
        p = self.p
        left, right = p.dp(3, 0), p.dp(1, 0)
        self.got(k, 0, left, None)
        self.put(k, 2, left, 0, right)
        self.spread(k, 1)
        self.got(k, 1, right, None)
        self.put(k, 3, right, 1, left)
        self.spread(k, 2)

    def far(self, k):
        d = self.p.dp(2, 0)
        self.got(k, 2, d, 0)
        self.got(k, 3, d, 1)
        self.spread(k, 3)

    def second(self, k):
        p = self.p
        for j in range(4):
            low, high = p.dp(OFFS[j], 3), p.dp(OFFS[j], 1)
            self.got(k, 4 + 4 * j, low, None)
            self.put(k, 6 + 4 * j, low, 0, p.dp(0, 1))
            self.put(k, 21 + 4 * j, low, None, p.sib)
            self.got(k, 5 + 4 * j, high, None)
            self.put(k, 7 + 4 * j, high, 1, p.dp(0, 3))
            self.put(k, 22 + 4 * j, high, None, p.sib)

    def last(self, k):
        p = self.p
        for j in range(4):
            d = p.dp(OFFS[j], 2)
            self.got(k, 6 + 4 * j, d, 0)
            self.got(k, 7 + 4 * j, d, 1)
            self.put(k, 23 + 4 * j, d, None, p.sib)

    def whole(self, k):
        for j in range(4):
            for i in range(4):
                self.got(k, 20 + 4 * j + i, self.p.sib_dp(OFFS[j], OFFS[i]), None)

    def close(self):
        for copy in self.open:
            copy.wait_send()

    def run(self, order):
        n = len(order)
        for t in range(n + 2):
            if t == 0:
                self.first(order[0])
            if t + 1 < n:
                self.first(order[t + 1])
            if t < n:
                self.ring(order[t])
            if 0 <= t - 1 < n:
                self.far(order[t - 1])
                self.second(order[t - 1])
            if 0 <= t - 2 < n:
                self.last(order[t - 2])


def dot(a, b, ca, cb):
    return lax.dot_general(a, b, (((ca,), (cb,)), ((), ())), preferred_element_type=F32)


def centered(x):
    c = x - jnp.mean(x, axis=-1, keepdims=True)
    r = lax.rsqrt(jnp.mean(c * c, axis=-1, keepdims=True) + EPS)
    return c, r


def norm(x, gain, bias):
    c, r = centered(x)
    return c * r * gain + bias


def norm_back(x, gain, gy):
    c, r = centered(x)
    hat = c * r
    gh = gy * gain
    gx = r * (gh - jnp.mean(gh, axis=-1, keepdims=True) - hat * jnp.mean(gh * hat, axis=-1, keepdims=True))
    return gx, gy * hat


def rows_of(i, n):
    return pl.ds(pl.multiple_of(i * n, n), n)


def col_sum(x):
    return jnp.sum(x, axis=0, keepdims=True)


K0, K1 = 0.7978845608028654, 0.044715


def gelu(x):
    return 0.5 * x * (1.0 + jnp.tanh(K0 * (x + K1 * x * x * x)))


def gelu_both(x):
    t = jnp.tanh(K0 * (x + K1 * x * x * x))
    u = 0.5 * x * (1.0 + t)
    du = 0.5 * (1.0 + t) + 0.5 * x * (1.0 - t * t) * K0 * (1.0 + 3.0 * K1 * x * x)
    return u, du


def head_masks():
    lane = lax.broadcasted_iota(jnp.int32, (1, 128), 1)
    even = jnp.where(lane < 64, 1.0, 0.0)
    return even.astype(BF16), (1.0 - even).astype(BF16)


def two_rows(x, even, odd):
    return jnp.concatenate([x * even, x * odd], axis=0)


def matmul_loop(width, tile, unroll=1):
    def run(body):
        def step(i, carry):
            body(pl.ds(pl.multiple_of(i * tile, tile), tile))
            return carry

        lax.fori_loop(0, width // tile, step, 0, unroll=unroll)

    return run


def each(count, unroll=1):
    def run(body):
        def step(i, carry):
            body(i)
            return carry

        lax.fori_loop(0, count, step, 0, unroll=unroll)

    return run


def forward(z_ref, w, pd, pm, hs_ref, segc_ref, segr_ref, keep, send_out):
    wa, wb, wc, wd = w

    @each(4)
    def _(i):
        r = rows_of(i, 32)
        keep["a1"][r, :] = norm(z_ref[r, :].astype(F32), pd[0:1, :], pd[3:4, :]).astype(BF16)

    a1 = keep["a1"]
    for third in range(3):
        bias_row = (4, None, 5)[third]

        @matmul_loop(WIDTH, 256, 2)
        def _(cols, third=third, bias_row=bias_row):
            at = pl.ds(pl.multiple_of(third * WIDTH + cols.start, 256), 256)
            acc = dot(a1[...], wa[at, :], 1, 1)
            if bias_row is not None:
                acc = acc + pd[bias_row : bias_row + 1, cols]
            keep["qkv"][:, at] = acc.astype(BF16)

    qkv = keep["qkv"]
    row = lax.broadcasted_iota(jnp.int32, (TOK, TOK), 0)
    col = lax.broadcasted_iota(jnp.int32, (TOK, TOK), 1)
    ok = (segc_ref[...] == segr_ref[...]) & (col <= row) & (row // 64 == col // 64)
    okf = jnp.where(ok, 1.0, 0.0)
    even, odd = head_masks()

    @each(8, 2)
    def _(p):
        cols = pl.ds(pl.multiple_of(p * 128, 128), 128)
        q = qkv[:, cols]
        k = qkv[:, pl.ds(pl.multiple_of(WIDTH + p * 128, 128), 128)]
        v = qkv[:, pl.ds(pl.multiple_of(2 * WIDTH + p * 128, 128), 128)]
        sc = dot(two_rows(q, even, odd), k, 1, 1) * 0.125
        okk = jnp.concatenate([okf, okf], axis=0) > 0.5
        sc = jnp.where(okk, sc, -1000000000.0)
        e = jnp.exp(sc - jnp.max(sc, axis=-1, keepdims=True))
        pr = e / jnp.sum(e, axis=-1, keepdims=True)
        keep["p"][rows_of(p, 256), :] = pr
        pb = pr.astype(BF16)
        both = jnp.concatenate([pb[:TOK], pb[TOK:]], axis=1)
        mixed = dot(both, two_rows(v, even, odd), 1, 0)
        keep["mixed"][:, cols] = mixed
        keep["scaled"][:, cols] = (mixed * hs_ref[:, cols]).astype(BF16)

    @matmul_loop(WIDTH, 256, 2)
    def _(cols):
        keep["attn"][:, cols] = dot(keep["scaled"][...], wb[cols, :], 1, 1) + pd[6:7, cols]

    @each(4)
    def _(i):
        r = rows_of(i, 32)
        z2 = z_ref[r, :].astype(F32) + norm(keep["attn"][r, :], pd[1:2, :], pd[7:8, :])
        keep["z2"][r, :] = z2
        keep["a2"][r, :] = norm(z2, pd[2:3, :], pd[8:9, :]).astype(BF16)

    @matmul_loop(FF, 256, 2)
    def _(cols):
        keep["hid"][:, cols] = dot(keep["a2"][...], wc[cols, :], 1, 1) + pm[11:12, cols]

    @each(8)
    def _(i):
        r = rows_of(i, 16)
        keep["mid"][r, :] = norm(gelu(keep["hid"][r, :]), pm[10:11, :], pm[12:13, :]).astype(BF16)

    for n in range(4):
        cols = slice(n * 256, (n + 1) * 256)
        acc = dot(keep["mid"][...], wd[cols, :], 1, 1)
        keep["out"][:, cols] = (keep["z2"][:, cols] + acc + pd[9:10, cols]).astype(BF16)
        send_out(n)


def backward(g_ref, w, pd, pm, hs_ref, kept, out, tmp, wait_w, send_out):
    wa, wb, wc, wd = w
    gd, gm = out["gd"], out["gm"]
    gd[...] = jnp.zeros_like(gd)
    gm[...] = jnp.zeros_like(gm)
    wait_w(D)

    @matmul_loop(FF, 256, 2)
    def _(cols):
        tmp["ff"][:, cols] = dot(g_ref[...], wd[:, cols], 1, 0)

    gd[9:10, :] = col_sum(g_ref[...].astype(F32))

    @each(8)
    def _(i):
        r = rows_of(i, 16)
        gmid = tmp["ff"][r, :]
        u, du = gelu_both(kept["hid"][r, :])
        gu, gg = norm_back(u, pm[10:11, :], gmid)
        gh = (gu * du).astype(BF16)
        out["ghid"][r, :] = gh
        gm[10:11, :] += col_sum(gg)
        gm[12:13, :] += col_sum(gmid)
        gm[11:12, :] += col_sum(gh.astype(F32))

    wait_w(C)

    @matmul_loop(WIDTH, 256, 1)
    def _(cols):
        tmp["w"][:, cols] = dot(out["ghid"][...], wc[:, cols], 1, 0)

    @each(4)
    def _(i):
        r = rows_of(i, 32)
        ga2 = tmp["w"][r, :]
        gz, gg = norm_back(kept["z2"][r, :], pd[2:3, :], ga2)
        gd[2:3, :] += col_sum(gg)
        gd[8:9, :] += col_sum(ga2)
        gz = gz + g_ref[r, :].astype(F32)
        tmp["gz2"][r, :] = gz
        gat, gg = norm_back(kept["attn"][r, :], pd[1:2, :], gz)
        gd[1:2, :] += col_sum(gg)
        gd[7:8, :] += col_sum(gz)
        gat = gat.astype(BF16)
        out["gattn"][r, :] = gat
        gd[6:7, :] += col_sum(gat.astype(F32))

    wait_w(B)
    even, odd = head_masks()

    @each(8, 2)
    def _(p):
        cols = pl.ds(pl.multiple_of(p * 128, 128), 128)
        kcols = pl.ds(pl.multiple_of(WIDTH + p * 128, 128), 128)
        vcols = pl.ds(pl.multiple_of(2 * WIDTH + p * 128, 128), 128)
        gs = dot(out["gattn"][...], wb[:, cols], 1, 0)
        tmp["hs"][:, cols] = col_sum(gs * kept["mixed"][:, cols])
        gmx = (gs * hs_ref[:, cols]).astype(BF16)
        q, k, v = kept["qkv"][:, cols], kept["qkv"][:, kcols], kept["qkv"][:, vcols]
        gmx2 = two_rows(gmx, even, odd)
        gp = dot(gmx2, v, 1, 1)
        pr = kept["p"][rows_of(p, 256), :]
        gsc = (pr * (gp - jnp.sum(pr * gp, axis=-1, keepdims=True))).astype(BF16)
        both = jnp.concatenate([gsc[:TOK], gsc[TOK:]], axis=1)
        gq = dot(both, two_rows(k, even, odd), 1, 0) * 0.125
        gk = dot(gsc, two_rows(q, even, odd), 0, 0) * 0.125
        gv = dot(pr.astype(BF16), gmx2, 0, 0)
        gq, gk, gv = gq.astype(BF16), gk.astype(BF16), gv.astype(BF16)
        out["gqkv"][:, cols] = gq
        out["gqkv"][:, kcols] = gk
        out["gqkv"][:, vcols] = gv
        gd[4:5, cols] = col_sum(gq.astype(F32))
        gd[5:6, cols] = col_sum(gv.astype(F32))

    wait_w(A)

    @matmul_loop(WIDTH, 256, 1)
    def _(cols):
        tmp["w"][:, cols] = dot(out["gqkv"][...], wa[:, cols], 1, 0)

    for i in range(4):
        r = slice(i * 32, (i + 1) * 32)
        ga1 = tmp["w"][r, :]
        gz, gg = norm_back(kept["zin"][r, :].astype(F32), pd[0:1, :], ga1)
        gd[0:1, :] += col_sum(gg)
        gd[3:4, :] += col_sum(ga1)
        out["gz"][r, :] = (gz + tmp["gz2"][r, :]).astype(BF16)
        send_out(i)

    ind = jnp.where(
        lax.broadcasted_iota(jnp.int32, (WIDTH, 128), 0) // 64 == lax.broadcasted_iota(jnp.int32, (WIDTH, 128), 1), 1.0, 0.0
    )
    hsum = lax.dot_general(
        jnp.broadcast_to(tmp["hs"][...], (8, WIDTH)), ind, (((1,), (0,)), ((), ())),
        precision=lax.Precision.HIGHEST, preferred_element_type=F32,
    )
    is13 = lax.broadcasted_iota(jnp.int32, (16, 128), 0) == 13
    out["gh"][...] = jnp.where(is13, jnp.concatenate([hsum, hsum], axis=0), 0.0)


KEEP = dict(
    zin=((TOK, WIDTH), BF16), a1=((TOK, WIDTH), BF16), qkv=((TOK, QKV), BF16), p=((8 * 256, TOK), F32),
    mixed=((TOK, WIDTH), F32), scaled=((TOK, WIDTH), BF16), attn=((TOK, WIDTH), F32), z2=((TOK, WIDTH), F32),
    a2=((TOK, WIDTH), BF16), hid=((TOK, FF), F32), mid=((TOK, FF), BF16), out=((TOK, WIDTH), BF16),
)
GRADS = dict(
    gin=((TOK, WIDTH), BF16), ghid=((TOK, FF), BF16), gattn=((TOK, WIDTH), BF16), gqkv=((TOK, QKV), BF16),
    gz=((TOK, WIDTH), BF16), gd=((16, WIDTH), F32), gm=((16, FF), F32), gh=((16, 128), F32),
)
WCLASS = (A, B, C, D)


def kernel_forward(*refs):
    own, refs = refs[:5], refs[5:]
    (tok, segc, segr, hs), refs = refs[:4], refs[4:]
    keep = dict(zip(KEEP, refs))
    refs = refs[len(KEEP) :]
    whbm, refs = refs[:4], refs[4:]
    (pd_out, pm_out), refs = refs[:2], refs[2:]
    bufs, refs = refs[:5], refs[5:]
    zin, send, recv, own_sem, xsend, xrecv, wsem = refs
    place = Place()
    loads = [
        pltpu.make_async_copy(own[k], part(bufs[k], ROWS[k], place.d, None), own_sem.at[k]) for k in range(5)
    ]
    for copy in loads:
        copy.start()
    place.barrier(True)
    for copy in loads:
        copy.wait()
    gather = Gather(place, bufs, send, recv)
    gather.run((S, A, B, C, D))
    for k in range(5):
        gather.whole(k)
    stores = [pltpu.make_async_copy(bufs[k], whbm[k - 1], wsem.at[k - 1]) for k in WCLASS]
    for copy in stores:
        copy.start()
    for q in range(8):
        at = slice(q * 128, (q + 1) * 128)
        acc = bufs[S][64 * q : 64 * q + 16, :]
        for j in range(1, 4):
            acc = acc + bufs[S][64 * q + 16 * j : 64 * q + 16 * j + 16, :]
        pd_out[:, at] = acc
    for q in range(32):
        pm_out[:, q * 128 : (q + 1) * 128] = bufs[S][16 * q : 16 * q + 16, :]

    def x_copy(n):
        cols = pl.ds(n * 256, 256)
        return remote(
            keep["out"].at[:, cols], zin.at[:, cols], xsend.at[n], xrecv.at[n], (place.s + 1) % 4, place.d
        )

    @pl.when(place.s == 0)
    def _():
        zin[...] = tok[...]

    @pl.when(place.s > 0)
    def _():
        for n in range(4):
            x_copy(n).wait_recv()

    keep["zin"][...] = zin[...]

    def send_out(n):
        @pl.when(place.s < 3)
        def _():
            x_copy(n).start()

    forward(zin, [bufs[k] for k in WCLASS], pd_out, pm_out, hs, segc, segr, keep, send_out)

    @pl.when(place.s < 3)
    def _():
        for n in range(4):
            x_copy(n).wait_send()

    gather.close()
    for copy in stores:
        copy.wait()


def kernel_backward(*refs):
    whbm, refs = refs[:4], refs[4:]
    kept = dict(zip(KEEP, refs))
    refs = refs[len(KEEP) :]
    (cot, pd, pm, hs), refs = refs[:4], refs[4:]
    out = dict(zip(GRADS, refs))
    refs = refs[len(GRADS) :]
    w, refs = refs[:4], refs[4:]
    gin, t_w, t_gz2, t_ff, t_hs, wsem, xsend, xrecv = refs
    place = Place()
    loads = {k: pltpu.make_async_copy(whbm[k - 1], w[k - 1], wsem.at[k - 1]) for k in (D, C, B, A)}
    for k in (D, C, B, A):
        loads[k].start()
    sem = pltpu.get_barrier_semaphore()
    for by in (1, 3):
        pl.semaphore_signal(sem, inc=1, device_id=((place.s + by) % 4, place.d), device_id_type=MESH)
    pl.semaphore_wait(sem, 2)

    def x_copy(i):
        r = pl.ds(i * 32, 32)
        return remote(out["gz"].at[r], gin.at[r], xsend.at[i], xrecv.at[i], (place.s + 3) % 4, place.d)

    @pl.when(place.s == 3)
    def _():
        gin[...] = cot[...]

    @pl.when(place.s < 3)
    def _():
        for i in range(4):
            x_copy(i).wait_recv()

    out["gin"][...] = gin[...]

    def send_out(i):
        @pl.when(place.s > 0)
        def _():
            x_copy(i).start()

    backward(
        gin, w, pd, pm, hs, kept, out, dict(w=t_w, gz2=t_gz2, ff=t_ff, hs=t_hs), lambda k: loads[k].wait(), send_out
    )

    @pl.when(place.s > 0)
    def _():
        for i in range(4):
            x_copy(i).wait_send()


class Scatter:
    def __init__(self, place, dw, sib, h1, f1, h2, f2, sem_send, sem_recv):
        self.p, self.dw, self.sib_buf = place, dw, sib
        self.h1, self.f1, self.h2, self.f2 = h1, f1, h2, f2
        self.send, self.recv = sem_send, sem_recv
        self.open = []


    def go(self, k, slot, src, dst, to):
        copy = remote(src, dst, self.send.at[k, slot], self.recv.at[k, slot], self.p.s, to)
        copy.start()
        self.open.append(copy)

    def got(self, k, slot, dst):
        remote(dst, dst, self.send.at[k, slot], self.recv.at[k, slot], self.p.s, self.p.sib).wait_recv()

    def block(self, k, of, og, half=None):
        return part(self.dw[k], ROWS[k], self.p.dp(of, og), half)

    def to_sibling(self, k):
        p = self.p
        for i in (3, 1, 2, 0):
            for j in (3, 1, 2, 0):
                slot = i * 4 + j
                src = part(self.dw[k], ROWS[k], p.sib_dp(OFFS[j], OFFS[i]), None)
                self.go(k, slot, src, part(self.sib_buf[k], ROWS[k], slot, None), p.sib)

    def add(self, k, dst, srcs, rows, store=None):
        cols = min(COLS[k], 1024)
        step = 16 if rows % 16 == 0 else 8
        steps_r, steps_c = rows // step, COLS[k] // cols

        def body(t, carry):
            r = pl.ds(pl.multiple_of((t // steps_c) * step, step), step)
            c = pl.ds(pl.multiple_of((t % steps_c) * cols, cols), cols)
            acc = dst[r, c].astype(F32)
            for src in srcs:
                acc = acc + src[r, c].astype(F32)
            if store is None:
                dst[r, c] = acc.astype(dst.dtype)
            else:
                store[r, c] = acc
            return carry

        lax.fori_loop(0, steps_r * steps_c, body, 0)

    def halves(self, k):
        p = self.p
        for j in (3, 1, 2, 0):
            slot = 3 * 4 + j
            here = part(self.sib_buf[k], ROWS[k], slot, None)
            self.got(k, slot, here)
            self.add(k, self.block(k, OFFS[j], 2), [here], ROWS[k])
            self.go(k, 16 + j, self.block(k, OFFS[j], 2, 0), part(self.h1[k], ROWS[k] // 2, j, None), p.dp(0, 1))
            self.go(k, 20 + j, self.block(k, OFFS[j], 2, 1), part(self.h1[k], ROWS[k] // 2, 4 + j, None), p.dp(0, 3))

    def wholes(self, k):
        p = self.p
        h = ROWS[k] // 2
        for j in (3, 1, 2, 0):
            for i, near, side in ((2, 1, 0), (1, 3, 1)):
                slot = i * 4 + j
                here = part(self.sib_buf[k], ROWS[k], slot, None)
                self.got(k, slot, here)
                hslot = 16 + 4 * side + j
                half = part(self.h1[k], h, 4 * side + j, None)
                self.got(k, hslot, half)
                blk = self.block(k, OFFS[j], near)
                self.add(k, blk.at[pl.ds(side * h, h)], [here.at[pl.ds(side * h, h)], half], h)
                self.add(k, blk.at[pl.ds((1 - side) * h, h)], [here.at[pl.ds((1 - side) * h, h)]], h)
                self.go(k, 24 + 4 * side + j, blk, part(self.f1[k], ROWS[k], 4 * side + j, None), p.dp(0, near))

    def settle(self, k, j):
        slot = j
        here = part(self.sib_buf[k], ROWS[k], slot, None)
        self.got(k, slot, here)
        srcs = [here]
        for side in range(2):
            src = part(self.f1[k], ROWS[k], 4 * side + j, None)
            self.got(k, 24 + 4 * side + j, src)
            srcs.append(src)
        self.add(k, self.block(k, OFFS[j], 0), srcs, ROWS[k])

    def far(self, k):
        p = self.p
        h = ROWS[k] // 2
        self.settle(k, 3)
        self.go(k, 32, self.block(k, 2, 0, 0), part(self.h2[k], h, 0, None), p.dp(1, 0))
        self.go(k, 33, self.block(k, 2, 0, 1), part(self.h2[k], h, 1, None), p.dp(3, 0))
        self.settle(k, 1)
        self.settle(k, 2)
        self.settle(k, 0)

    def near(self, k):
        p = self.p
        h = ROWS[k] // 2
        for near, side in ((1, 0), (3, 1)):
            half = part(self.h2[k], h, side, None)
            self.got(k, 32 + side, half)
            blk = self.block(k, near, 0)
            self.add(k, blk.at[pl.ds(side * h, h)], [half], h)
            self.go(k, 34 + side, blk, part(self.f2[k], ROWS[k], side, None), p.dp(near, 0))

    def last(self, k, out):
        srcs = []
        for side in range(2):
            src = part(self.f2[k], ROWS[k], side, None)
            self.got(k, 34 + side, src)
            srcs.append(src)
        self.add(k, self.block(k, 0, 0), srcs, ROWS[k], store=out)

    def close(self):
        for copy in self.open:
            copy.wait_send()


def kernel_grads(a1, scaled, a2, mid, gin, ghid, gattn, gqkv, gd, gm, gh, *refs):
    outs, refs = refs[:5], refs[5:]
    dw, refs = refs[:5], refs[5:]
    sib, refs = refs[:5], refs[5:]
    h1, refs = refs[:5], refs[5:]
    f1, refs = refs[:5], refs[5:]
    h2, refs = refs[:5], refs[5:]
    f2, refs = refs[:5], refs[5:]
    send, recv = refs
    place = Place()
    place.barrier(False)
    scatter = Scatter(place, dw, sib, h1, f1, h2, f2, send, recv)
    pairs = {A: (gqkv, a1), B: (gattn, scaled), C: (ghid, a2), D: (gin, mid)}

    def product(k):
        if k == S:

            @each(32)
            def _(d):
                at = pl.ds(pl.multiple_of((d // 4) * 128, 128), 128)
                own = pl.ds(pl.multiple_of(d * 128, 128), 128)
                dw[S][rows_of(d, 16), :] = gd[:, at] + gm[:, own] + gh[...]

            return
        g, a = pairs[k]
        rows, cols = 32 * ROWS[k], COLS[k]

        @each(rows // 512)
        def _(m):
            gt = g[:, pl.ds(pl.multiple_of(m * 512, 512), 512)].T

            @each(cols // 256)
            def _(n):
                at = pl.ds(pl.multiple_of(n * 256, 256), 256)
                dw[k][rows_of(m, 512), at] = dot(gt, a[:, at], 1, 0).astype(BF16)

    order = (D, C, B, A, S)
    n = len(order)
    for t in range(n + 4):
        if t < n:
            product(order[t])
            scatter.to_sibling(order[t])
        if 0 <= t - 1 < n:
            scatter.halves(order[t - 1])
        if 0 <= t - 2 < n:
            scatter.wholes(order[t - 2])
        if 0 <= t - 3 < n:
            scatter.far(order[t - 3])
            scatter.near(order[t - 3])
        if 0 <= t - 4 < n:
            scatter.last(order[t - 4], outs[order[t - 4]])
    scatter.close()


def vmem(shape, dtype):
    return pltpu.VMEM(shape, dtype)


VSPEC = pl.BlockSpec(memory_space=pltpu.VMEM)
ASPEC = pl.BlockSpec(memory_space=pl.ANY)
DMA = pltpu.SemaphoreType.DMA


def params(cid):
    return pltpu.CompilerParams(collective_id=cid, has_side_effects=True, vmem_limit_bytes=VMEM_LIMIT)


def struct(pair):
    return jax.ShapeDtypeStruct(*pair)


WSTRUCT = [((32 * ROWS[k], COLS[k]), BF16) for k in WCLASS]


def run_forward(own, tok, segc, segr, hs):
    outs = list(KEEP.values()) + WSTRUCT + [((16, WIDTH), F32), ((16, FF), F32)]
    return pl.pallas_call(
        kernel_forward,
        out_shape=[struct(o) for o in outs],
        in_specs=[ASPEC] * 5 + [VSPEC] * 4,
        out_specs=[VSPEC] * len(KEEP) + [ASPEC] * 4 + [VSPEC] * 2,
        scratch_shapes=[vmem((32 * ROWS[k], COLS[k]), TYPES[k]) for k in range(5)]
        + [vmem((TOK, WIDTH), BF16), DMA((5, 36)), DMA((5, 36)), DMA((5,)), DMA((4,)), DMA((4,)), DMA((4,))],
        compiler_params=params(1),
        name="gather_forward",
    )(*own, tok, segc, segr, hs)


def run_backward(weights, kept, cot, pd, pm, hs):
    return pl.pallas_call(
        kernel_backward,
        out_shape=[struct(o) for o in GRADS.values()],
        in_specs=[ASPEC] * 4 + [VSPEC] * (len(KEEP) + 4),
        out_specs=[VSPEC] * len(GRADS),
        scratch_shapes=[vmem(*w) for w in WSTRUCT]
        + [vmem((TOK, WIDTH), BF16), vmem((TOK, WIDTH), F32), vmem((TOK, WIDTH), F32), vmem((TOK, FF), F32)]
        + [vmem((1, WIDTH), F32), DMA((4,)), DMA((4,)), DMA((4,))],
        compiler_params=params(2),
        name="backward_chain",
    )(*weights, *kept, cot, pd, pm, hs)


def run_grads(*args):
    five = range(5)
    return pl.pallas_call(
        kernel_grads,
        out_shape=[jax.ShapeDtypeStruct((ROWS[k], COLS[k]), F32) for k in five],
        in_specs=[VSPEC] * 11,
        out_specs=[VSPEC] * 5,
        scratch_shapes=[vmem((32 * ROWS[k], COLS[k]), TYPES[k]) for k in five]
        + [vmem((16 * ROWS[k], COLS[k]), TYPES[k]) for k in five]
        + [vmem((8 * (ROWS[k] // 2), COLS[k]), TYPES[k]) for k in five]
        + [vmem((8 * ROWS[k], COLS[k]), TYPES[k]) for k in five]
        + [vmem((2 * (ROWS[k] // 2), COLS[k]), TYPES[k]) for k in five]
        + [vmem((2 * ROWS[k], COLS[k]), TYPES[k]) for k in five]
        + [DMA((5, 36)), DMA((5, 36))],
        compiler_params=params(3),
        name="grads_scatter",
    )(*args)


def body(
    tokens, cotangent, live_counts, segments, attn_input, attn_output, feed_up, feed_down,
    norm_gains, vector_bias, mid_gain, mid_bias, head_scale,
):
    d = lax.axis_index("dp")
    thin = jnp.concatenate([norm_gains[0], vector_bias[0]], axis=0).astype(F32)
    lane = d % 4
    spots = (jnp.arange(4) == lane).astype(F32)
    thin = (spots[None, :, None] * thin[:, None, :]).reshape(10, 128)
    small = jnp.concatenate(
        [thin, mid_gain[0][None].astype(F32), mid_bias[0].astype(F32), jnp.zeros((3, 128), F32)], axis=0
    )
    own = [small, attn_input[0].T, attn_output[0].T, feed_up[0].T, feed_down[0].T]
    hs = jnp.repeat(head_scale[0].astype(F32), 64)[None]
    live = jnp.repeat(live_counts, 64)
    place = jnp.arange(TOK) % 64
    cot = jnp.where((place < live)[:, None], cotangent, jnp.zeros_like(cotangent))
    fwd = run_forward(own, tokens, segments[:, None], segments[None, :], hs)
    kept = fwd[: len(KEEP)]
    weights = fwd[len(KEEP) : len(KEEP) + 4]
    pd, pm = fwd[len(KEEP) + 4 :]
    named = dict(zip(KEEP, kept))
    grads = run_backward(weights, kept, cot, pd, pm, hs)
    gn = dict(zip(GRADS, grads))
    sums = run_grads(
        named["a1"], named["scaled"], named["a2"], named["mid"], gn["gin"], gn["ghid"], gn["gattn"], gn["gqkv"],
        gn["gd"], gn["gm"], gn["gh"],
    )
    gs = lax.dynamic_slice(sums[S], (0, 32 * lane), (10, 32))
    return (
        named["out"][None],
        gn["gz"][None],
        sums[A].T[None],
        sums[B].T[None],
        sums[C].T[None],
        sums[D].T[None],
        gs[:3][None],
        gs[3:][None],
        sums[S][10:11],
        sums[S][11:13][None],
        sums[S][13:14, :16],
    )


def solution(mesh):
    return jax.shard_map(
        body,
        mesh=mesh,
        in_specs=(
            P("dp", None), P("dp", None), P("dp"), P("dp"),
            P("pipe", None, "dp"), P("pipe", None, "dp"), P("pipe", None, "dp"), P("pipe", None, "dp"),
            P("pipe", None, "dp"), P("pipe", None, "dp"), P("pipe", "dp"), P("pipe", None, "dp"), P("pipe", None),
        ),
        out_specs=(
            P("pipe", "dp", None), P("pipe", "dp", None),
            P("pipe", None, "dp"), P("pipe", None, "dp"), P("pipe", None, "dp"), P("pipe", None, "dp"),
            P("pipe", None, "dp"), P("pipe", None, "dp"), P("pipe", "dp"), P("pipe", None, "dp"), P("pipe", None),
        ),
        check_vma=False,
    )
```

```python
import jax
import jax.numpy as jnp
from jax import lax
from jax.experimental import pallas as pl
from jax.experimental.pallas import tpu as pltpu
from jax.sharding import PartitionSpec as P

MESH = pl.DeviceIdType.MESH
EPS = 1e-05
F32, BF16 = jnp.float32, jnp.bfloat16
VMEM_LIMIT = 61800 * 1024

TOK, WIDTH, FF, QKV = 128, 1024, 4096, 3072
IN, OUT, UP, DOWN, UNITS = 0, 6, 8, 16, 24
SMALL = "small"
GATHER = (SMALL, (IN, 6), (OUT, 2), (UP, 8), (DOWN, 8))
SCATTER = ((DOWN, 4), (DOWN + 4, 4), (UP, 4), (UP + 4, 4), (IN, 4), (IN + 4, 4), SMALL)
SHARE = 3
OFFS = (0, 3, 1, 2)


class Place:
    def __init__(self):
        self.s = lax.axis_index("pipe")
        d = lax.axis_index("dp")
        self.d = d
        self.c = d % 2
        y, z = (d // 2) % 4, d // 8
        self.f = y + self.c * (z - y)
        self.g = z + self.c * (y - z)
        self.sf = 2 + 6 * self.c
        self.sg = 8 - 6 * self.c
        self.sib = d + 1 - 2 * self.c

    def dp(self, of, og):
        return ((self.f + of) % 4) * self.sf + ((self.g + og) % 4) * self.sg + self.c

    def sib_dp(self, of, og):
        return ((self.g + of) % 4) * self.sg + ((self.f + og) % 4) * self.sf + 1 - self.c

    def barrier(self):
        sem = pltpu.get_barrier_semaphore()
        near = [self.dp(1, 0), self.dp(3, 0), self.dp(0, 1), self.dp(0, 3), self.sib]
        near = [(self.s, to) for to in near] + [((self.s + by) % 4, self.d) for by in (1, 3)]
        for to in near:
            pl.semaphore_signal(sem, inc=1, device_id=to, device_id_type=MESH)
        pl.semaphore_wait(sem, len(near))


def remote(src, dst, send, recv, s, to):
    return pltpu.make_async_remote_copy(
        src_ref=src, dst_ref=dst, send_sem=send, recv_sem=recv, device_id=(s, to), device_id_type=MESH
    )


def piece_block(whole, small, piece, d, half=None):
    if piece is SMALL:
        return small.at[d] if half is None else small.at[d, pl.ds(8 * half, 8)]
    u, n = piece
    return whole.at[d, pl.ds(u, n)] if half is None else whole.at[d, pl.ds(u + half * (n // 2), n // 2)]


class Gather:
    def __init__(self, place, whole, small, send, recv):
        self.p, self.whole_ref, self.small = place, whole, small
        self.send, self.recv = send, recv
        self.open = []

    def ref(self, k, d, half):
        return piece_block(self.whole_ref, self.small, GATHER[k], d, half)

    def put(self, k, slot, d, half, to):
        ref = self.ref(k, d, half)
        copy = remote(ref, ref, self.send.at[k, slot], self.recv.at[k, slot], self.p.s, to)
        copy.start()
        self.open.append(copy)

    def got(self, k, slot, d, half):
        ref = self.ref(k, d, half)
        remote(ref, ref, self.send.at[k, slot], self.recv.at[k, slot], self.p.s, self.p.sib).wait_recv()

    def spread(self, k, j):
        p = self.p
        d = p.dp(OFFS[j], 0)
        self.put(k, 4 + 4 * j, d, None, p.dp(0, 1))
        self.put(k, 5 + 4 * j, d, None, p.dp(0, 3))
        self.put(k, 20 + 4 * j, d, None, p.sib)

    def first(self, k):
        p = self.p
        self.put(k, 0, p.d, None, p.dp(1, 0))
        self.put(k, 1, p.d, None, p.dp(3, 0))
        self.spread(k, 0)

    def ring(self, k):
        p = self.p
        left, right = p.dp(3, 0), p.dp(1, 0)
        self.got(k, 0, left, None)
        self.put(k, 2, left, 0, right)
        self.spread(k, 1)
        self.got(k, 1, right, None)
        self.put(k, 3, right, 1, left)
        self.spread(k, 2)

    def far(self, k):
        d = self.p.dp(2, 0)
        self.got(k, 2, d, 0)
        self.got(k, 3, d, 1)
        self.spread(k, 3)

    def second(self, k):
        p = self.p
        for j in range(4):
            low, high = p.dp(OFFS[j], 3), p.dp(OFFS[j], 1)
            self.got(k, 4 + 4 * j, low, None)
            self.put(k, 6 + 4 * j, low, 0, p.dp(0, 1))
            self.put(k, 21 + 4 * j, low, None, p.sib)
            self.got(k, 5 + 4 * j, high, None)
            self.put(k, 7 + 4 * j, high, 1, p.dp(0, 3))
            self.put(k, 22 + 4 * j, high, None, p.sib)

    def last(self, k):
        p = self.p
        for j in range(4):
            d = p.dp(OFFS[j], 2)
            self.got(k, 6 + 4 * j, d, 0)
            self.got(k, 7 + 4 * j, d, 1)
            self.put(k, 23 + 4 * j, d, None, p.sib)

    def whole(self, k):
        for j in range(4):
            for i in range(4):
                self.got(k, 20 + 4 * j + i, self.p.sib_dp(OFFS[j], OFFS[i]), None)

    def close(self):
        for copy in self.open:
            copy.wait_send()

    def run(self, ready):
        n, begun = len(GATHER), 0
        for t in range(n + 3):
            while begun < min(n, t + 3):
                self.first(begun)
                begun += 1
            if t < n:
                self.ring(t)
            if 0 <= t - 1 < n:
                self.far(t - 1)
            if 0 <= t - 2 < n:
                self.second(t - 2)
            if 0 <= t - 3 < n:
                self.last(t - 3)
                self.whole(t - 3)
                ready(t - 3)


def dot(a, b, ca, cb):
    return lax.dot_general(a, b, (((ca,), (cb,)), ((), ())), preferred_element_type=F32)


def centered(x):
    c = x - jnp.mean(x, axis=-1, keepdims=True)
    r = lax.rsqrt(jnp.mean(c * c, axis=-1, keepdims=True) + EPS)
    return c, r


def norm(x, gain, bias):
    c, r = centered(x)
    return c * r * gain + bias


def norm_back(x, gain, gy):
    c, r = centered(x)
    hat = c * r
    gh = gy * gain
    gx = r * (gh - jnp.mean(gh, axis=-1, keepdims=True) - hat * jnp.mean(gh * hat, axis=-1, keepdims=True))
    return gx, gy * hat


def rows_of(i, n):
    return pl.ds(pl.multiple_of(i * n, n), n)


def col_sum(x):
    return jnp.sum(x, axis=0, keepdims=True)


def row_sum(x):
    return dot(jnp.full((16, x.shape[0]), 1.0, BF16), x, 1, 0)[:1]


K0, K1 = 0.7978845608028654, 0.044715


def gelu(x):
    return 0.5 * x * (1.0 + jnp.tanh(K0 * (x + K1 * x * x * x)))


def gelu_both(x):
    t = jnp.tanh(K0 * (x + K1 * x * x * x))
    u = 0.5 * x * (1.0 + t)
    du = 0.5 * (1.0 + t) + 0.5 * x * (1.0 - t * t) * K0 * (1.0 + 3.0 * K1 * x * x)
    return u, du


def head_masks():
    lane = lax.broadcasted_iota(jnp.int32, (1, 128), 1)
    even = jnp.where(lane < 64, 1.0, 0.0)
    return even.astype(BF16), (1.0 - even).astype(BF16)


def two_rows(x, even, odd):
    return jnp.concatenate([x * even, x * odd], axis=0)


def each(count, unroll=1):
    def run(body):
        def step(i, carry):
            body(i)
            return carry

        lax.fori_loop(0, count, step, 0, unroll=unroll)

    return run


def stack(w, d0, nd, u, nu):
    return w[pl.ds(d0, nd), u : u + nu].reshape(nd * nu * 16, WIDTH)


def head_columns():
    col = lax.broadcasted_iota(jnp.int32, (128, WIDTH), 1)
    head = lax.broadcasted_iota(jnp.int32, (128, WIDTH), 0)
    return jnp.where(col // 64 == head, 1.0, 0.0)


class Layer:
    def __init__(self, w, r):
        self.w, self.r = w, r


    def first_norm(self):
        r, pd = self.r, self.r["pd"]

        @each(4, 2)
        def _(i):
            at = rows_of(i, 32)
            r["a1"][at, :] = norm(r["zin"][at, :].astype(F32), pd[0:1, :], pd[3:4, :]).astype(BF16)

    def qkv(self):
        r = self.r
        for c in range(4):
            at = slice(c * 768, (c + 1) * 768)
            acc = dot(r["a1"][...], stack(self.w, 8 * c, 8, IN, 6), 1, 1) + r["pq"][0:1, at]
            r["qkv"][:, at] = acc.astype(BF16)

    def attention(self):
        r, qkv = self.r, self.r["qkv"]
        even, odd = head_masks()

        @each(8, 4)
        def _(p):
            cols = rows_of(p, 128)
            q = qkv[:, cols]
            k = qkv[:, pl.ds(pl.multiple_of(WIDTH + p * 128, 128), 128)]
            v = qkv[:, pl.ds(pl.multiple_of(2 * WIDTH + p * 128, 128), 128)]
            ok = r["ok"][...]
            sc = dot(two_rows(q, even, odd), k, 1, 1) * 0.125
            sc = jnp.where(jnp.concatenate([ok, ok], axis=0) > 0.5, sc, -1000000000.0)
            e = jnp.exp(sc - jnp.max(sc, axis=-1, keepdims=True))
            pr = e / jnp.sum(e, axis=-1, keepdims=True)
            r["p"][rows_of(p, 256), :] = pr
            pb = pr.astype(BF16)
            both = jnp.concatenate([pb[:TOK], pb[TOK:]], axis=1)
            mixed = dot(both, two_rows(v, even, odd), 1, 0)
            r["mixed"][:, cols] = mixed
            r["scaled"][:, cols] = (mixed * r["hs"][0:1, cols]).astype(BF16)

    def project(self):
        r = self.r
        r["attn"][...] = dot(r["scaled"][...], stack(self.w, 0, 32, OUT, 2), 1, 1) + r["pd"][6:7, :]

    def middle_norms(self):
        r, pd = self.r, self.r["pd"]

        @each(4, 2)
        def _(i):
            at = rows_of(i, 32)
            z2 = r["zin"][at, :].astype(F32) + norm(r["attn"][at, :], pd[1:2, :], pd[7:8, :])
            r["z2"][at, :] = z2
            r["a2"][at, :] = norm(z2, pd[2:3, :], pd[8:9, :]).astype(BF16)

    def up(self):
        r = self.r

        @each(4)
        def _(c):
            cols = rows_of(c, 1024)
            r["ff"][:, cols] = dot(r["a2"][...], stack(self.w, 8 * c, 8, UP, 8), 1, 1) + r["pm"][11:12, cols]

    def inner_norm(self):
        r, pm = self.r, self.r["pm"]

        @each(8, 2)
        def _(i):
            at = rows_of(i, 16)
            r["mid"][at, :] = norm(gelu(r["ff"][at, :]), pm[10:11, :], pm[12:13, :]).astype(BF16)

    def down(self, send_out):
        r = self.r
        for n in range(4):
            cols = slice(n * 256, (n + 1) * 256)
            acc = r["z2"][:, cols] + r["pd"][9:10, cols]
            for q in range(4):
                w = stack(self.w, 8 * n, 8, DOWN + 2 * q, 2)
                acc = acc + dot(r["mid"][:, q * 1024 : (q + 1) * 1024], w, 1, 1)
            r["out"][:, cols] = acc.astype(BF16)
            send_out(n)

    def prepare(self):
        r = self.r

        @each(8, 2)
        def _(i):
            at = rows_of(i, 16)
            u, du = gelu_both(r["ff"][at, :])
            c, s = centered(u)
            r["hat"][at, :] = (c * s).astype(BF16)
            r["slope"][at, :] = (du * s).astype(BF16)

        for name in ("gd", "gm"):
            r[name][...] = jnp.zeros_like(r[name])


    def back_down(self):
        r = self.r
        for q in range(4):
            w = stack(self.w, 0, 32, DOWN + 2 * q, 2)
            r["ff"][:, q * 1024 : (q + 1) * 1024] = dot(r["gin"][...], w, 1, 0)

    def back_inner(self):
        r, pm = self.r, self.r["pm"]

        @each(8, 2)
        def _(i):
            at = rows_of(i, 16)
            gh = r["ff"][at, :] * pm[10:11, :]
            hat = r["hat"][at, :].astype(F32)
            m1 = jnp.mean(gh, axis=-1, keepdims=True)
            m2 = jnp.mean(gh * hat, axis=-1, keepdims=True)
            r["ghid"][at, :] = ((gh - m1 - hat * m2) * r["slope"][at, :].astype(F32)).astype(BF16)

    def back_up(self):
        r = self.r
        r["tw"][...] = dot(r["ghid"][...], stack(self.w, 0, 32, UP, 8), 1, 0)

    def back_middle(self):
        r, gd, pd = self.r, self.r["gd"], self.r["pd"]

        @each(4, 2)
        def _(i):
            at = rows_of(i, 32)
            ga2 = r["tw"][at, :]
            gz, gg = norm_back(r["z2"][at, :], pd[2:3, :], ga2)
            gd[2:3, :] += col_sum(gg)
            gd[8:9, :] += col_sum(ga2)
            gz = gz + r["gin"][at, :].astype(F32)
            r["gz2"][at, :] = gz
            gat, gg = norm_back(r["attn"][at, :], pd[1:2, :], gz)
            gd[1:2, :] += col_sum(gg)
            gd[7:8, :] += col_sum(gz)
            r["gattn"][at, :] = gat.astype(BF16)

    def back_project(self):
        r = self.r
        r["tw"][...] = dot(r["gattn"][...], stack(self.w, 0, 32, OUT, 2), 1, 0)

    def back_attention(self):
        r = self.r
        even, odd = head_masks()

        @each(8, 4)
        def _(p):
            cols = rows_of(p, 128)
            kcols = pl.ds(pl.multiple_of(WIDTH + p * 128, 128), 128)
            vcols = pl.ds(pl.multiple_of(2 * WIDTH + p * 128, 128), 128)
            gs = r["tw"][:, cols]
            r["gh"][0:1, cols] = col_sum(gs * r["mixed"][:, cols])
            gmx = (gs * r["hs"][0:1, cols]).astype(BF16)
            q, k, v = r["qkv"][:, cols], r["qkv"][:, kcols], r["qkv"][:, vcols]
            gmx2 = two_rows(gmx, even, odd)
            gp = dot(gmx2, v, 1, 1)
            pr = r["p"][rows_of(p, 256), :]
            gsc = (pr * (gp - jnp.sum(pr * gp, axis=-1, keepdims=True))).astype(BF16)
            both = jnp.concatenate([gsc[:TOK], gsc[TOK:]], axis=1)
            r["gqkv"][:, cols] = (dot(both, two_rows(k, even, odd), 1, 0) * 0.125).astype(BF16)
            r["gqkv"][:, kcols] = (dot(gsc, two_rows(q, even, odd), 0, 0) * 0.125).astype(BF16)
            r["gqkv"][:, vcols] = dot(pr.astype(BF16), gmx2, 0, 0).astype(BF16)

    def back_qkv(self):
        r = self.r
        r["tw"][...] = dot(r["gqkv"][...], stack(self.w, 0, 32, IN, 6), 1, 0)

    def back_first(self, send_out):
        r, gd, pd = self.r, self.r["gd"], self.r["pd"]
        for i in range(4):
            at = slice(i * 32, (i + 1) * 32)
            ga1 = r["tw"][at, :]
            gz, gg = norm_back(r["zin"][at, :].astype(F32), pd[0:1, :], ga1)
            r["gz"][at, :] = (gz + r["gz2"][at, :]).astype(BF16)
            send_out(i)
            gd[0:1, :] += col_sum(gg)
            gd[3:4, :] += col_sum(ga1)

    def inner_sums(self):
        r, gm = self.r, self.r["gm"]

        @each(8)
        def _(i):
            at = rows_of(i, 16)
            g = r["ff"][at, :]
            gm[10:11, :] += col_sum(g * r["hat"][at, :].astype(F32))
            gm[12:13, :] += col_sum(g)

        gm[11:12, :] = row_sum(r["ghid"][...])

    def other_sums(self):
        r, gd = self.r, self.r["gd"]
        gd[9:10, :] = row_sum(r["gin"][...])
        gd[6:7, :] = row_sum(r["gattn"][...])
        gd[4:5, :] = row_sum(r["gqkv"][:, :WIDTH])
        gd[5:6, :] = row_sum(r["gqkv"][:, 2 * WIDTH :])


    def grad_down(self):
        r = self.r

        @each(4)
        def _(c):
            gt = r["gin"][:, rows_of(c, 256)].T
            for q in range(4):
                g = dot(gt, r["mid"][:, q * 1024 : (q + 1) * 1024], 1, 0).astype(BF16)
                self.w[pl.ds(8 * c, 8), DOWN + 2 * q : DOWN + 2 * q + 2] = g.reshape(8, 2, 16, WIDTH)

    def grad_up(self):
        r = self.r

        @each(8)
        def _(c):
            gt = r["ghid"][:, rows_of(c, 512)].T
            g = dot(gt, r["a2"][...], 1, 0).astype(BF16)
            self.w[pl.ds(4 * c, 4), UP : UP + 8] = g.reshape(4, 8, 16, WIDTH)

    def grad_attention(self):
        r = self.r

        @each(8)
        def _(c):
            gt = r["gqkv"][:, rows_of(c, 384)].T
            g = dot(gt, r["a1"][...], 1, 0).astype(BF16)
            self.w[pl.ds(4 * c, 4), IN : IN + 6] = g.reshape(4, 6, 16, WIDTH)

        @each(2)
        def _(c):
            gt = r["gattn"][:, rows_of(c, 512)].T
            g = dot(gt, r["scaled"][...], 1, 0).astype(BF16)
            self.w[pl.ds(16 * c, 16), OUT : OUT + 2] = g.reshape(16, 2, 16, WIDTH)

    def grad_small(self, small):
        r = self.r
        hsum = lax.dot_general(
            jnp.broadcast_to(r["gh"][0:1, :], (8, WIDTH)), head_columns(), (((1,), (1,)), ((), ())),
            precision=lax.Precision.HIGHEST, preferred_element_type=F32,
        )
        is13 = lax.broadcasted_iota(jnp.int32, (16, 128), 0) == 13
        heads = jnp.where(is13, jnp.concatenate([hsum, hsum], axis=0), 0.0)
        for d in range(32):
            a, b = (d // 4) * 128, d * 128
            small[d] = r["gd"][:, a : a + 128] + r["gm"][:, b : b + 128] + heads


class Scatter:
    def __init__(self, place, grads, small, sib, ssib, land, sland, send, recv):
        self.p, self.grads, self.small = place, grads, small
        self.sib, self.ssib, self.land, self.sland = sib, ssib, land, sland
        self.send, self.recv = send, recv
        self.open = []

    def go(self, k, slot, src, dst, to):
        copy = remote(src, dst, self.send.at[k, slot], self.recv.at[k, slot], self.p.s, to)
        copy.start()
        self.open.append(copy)

    def got(self, k, slot, dst):
        remote(dst, dst, self.send.at[k, slot], self.recv.at[k, slot], self.p.s, self.p.sib).wait_recv()

    def block(self, k, of, og, half=None):
        return piece_block(self.grads, self.small, SCATTER[k], self.p.dp(of, og), half)

    def from_sib(self, k, slot, half=None):
        return piece_block(self.sib, self.ssib, SCATTER[k], slot, half)

    def landing(self, k, kind, slot):
        if SCATTER[k] is SMALL:
            ref = self.sland[kind].at[slot]
        else:
            ref = self.land[kind].at[k % SHARE, slot]
        return ref

    def to_sibling(self, k):
        p = self.p
        for i in (3, 1, 2, 0):
            for j in (3, 1, 2, 0):
                src = piece_block(self.grads, self.small, SCATTER[k], p.sib_dp(OFFS[j], OFFS[i]))
                self.go(k, i * 4 + j, src, self.from_sib(k, i * 4 + j), p.sib)

    def add(self, k, dst, srcs, store=None):
        out = dst if store is None else store
        if SCATTER[k] is SMALL:
            out[...] = dst[...] + sum(src[...] for src in srcs)
            return
        for u in range(dst.shape[0]):
            acc = dst[u].astype(F32)
            for src in srcs:
                acc = acc + src[u].astype(F32)
            out[u] = acc.astype(out.dtype)

    def halves(self, k):
        p = self.p
        for j in (3, 1, 2, 0):
            slot = 3 * 4 + j
            here = self.from_sib(k, slot)
            self.got(k, slot, here)
            self.add(k, self.block(k, OFFS[j], 2), [here])
            self.go(k, 16 + j, self.block(k, OFFS[j], 2, 0), self.landing(k, 0, j), p.dp(0, 1))
            self.go(k, 20 + j, self.block(k, OFFS[j], 2, 1), self.landing(k, 0, 4 + j), p.dp(0, 3))

    def wholes(self, k):
        p = self.p
        for j in (3, 1, 2, 0):
            for i, side in ((2, 0), (1, 1)):
                self.got(k, i * 4 + j, self.from_sib(k, i * 4 + j))
                self.got(k, 16 + 4 * side + j, self.landing(k, 0, 4 * side + j))
            for i, near, side in ((2, 1, 0), (1, 3, 1)):
                slot = i * 4 + j
                self.add(
                    k, self.block(k, OFFS[j], near, side), [self.from_sib(k, slot, side), self.landing(k, 0, 4 * side + j)]
                )
                self.add(k, self.block(k, OFFS[j], near, 1 - side), [self.from_sib(k, slot, 1 - side)])
            for near, side in ((1, 0), (3, 1)):
                self.go(
                    k, 24 + 4 * side + j, self.block(k, OFFS[j], near), self.landing(k, 1, 4 * side + j), p.dp(0, near)
                )

    def settle(self, k, j):
        here = self.from_sib(k, j)
        self.got(k, j, here)
        srcs = [here]
        for side in range(2):
            src = self.landing(k, 1, 4 * side + j)
            self.got(k, 24 + 4 * side + j, src)
            srcs.append(src)
        self.add(k, self.block(k, OFFS[j], 0), srcs)

    def far(self, k):
        p = self.p
        self.settle(k, 3)
        self.go(k, 32, self.block(k, 2, 0, 0), self.landing(k, 2, 0), p.dp(1, 0))
        self.go(k, 33, self.block(k, 2, 0, 1), self.landing(k, 2, 1), p.dp(3, 0))
        for j in (1, 2, 0):
            self.settle(k, j)

    def near(self, k):
        p = self.p
        for side in range(2):
            self.got(k, 32 + side, self.landing(k, 2, side))
        for near, side in ((1, 0), (3, 1)):
            self.add(k, self.block(k, near, 0, side), [self.landing(k, 2, side)])
        for near, side in ((1, 0), (3, 1)):
            self.go(k, 34 + side, self.block(k, near, 0), self.landing(k, 3, side), p.dp(near, 0))

    def last(self, k, total, small_total):
        srcs = []
        for side in range(2):
            src = self.landing(k, 3, side)
            self.got(k, 34 + side, src)
            srcs.append(src)
        if SCATTER[k] is SMALL:
            store = small_total
        else:
            u, n = SCATTER[k]
            store = total.at[pl.ds(u, n)]
        self.add(k, self.block(k, 0, 0), srcs, store=store)

    def close(self):
        for copy in self.open:
            copy.wait_send()


HELD = dict(
    pd=((16, WIDTH), F32), pm=((16, FF), F32), pq=((1, QKV), F32), hs=((8, WIDTH), F32), ok=((TOK, TOK), F32),
    zin=((TOK, WIDTH), BF16), a1=((TOK, WIDTH), BF16), qkv=((TOK, QKV), BF16), p=((8 * 256, TOK), F32),
    mixed=((TOK, WIDTH), F32), scaled=((TOK, WIDTH), BF16), attn=((TOK, WIDTH), F32), z2=((TOK, WIDTH), F32),
    a2=((TOK, WIDTH), BF16), ff=((TOK, FF), F32), hat=((TOK, FF), BF16), slope=((TOK, FF), BF16), mid=((TOK, FF), BF16),
    gin=((TOK, WIDTH), BF16), ghid=((TOK, FF), BF16), gattn=((TOK, WIDTH), BF16), gqkv=((TOK, QKV), BF16),
    tw=((TOK, WIDTH), F32), gz2=((TOK, WIDTH), F32), gd=((16, WIDTH), F32), gm=((16, FF), F32), gh=((8, WIDTH), F32),
)
LANDING = ((8, 2), (8, 4), (2, 2), (2, 4))


def kernel(*refs):
    (tok, cot, live, seg, own_in, own_out, own_up, own_down, gains, vecs, mgain, mbias, hscale), refs = refs[:13], refs[13:]
    (out, gz, total, small_total), refs = refs[:4], refs[4:]
    (w, small, sib, ssib), refs = refs[:4], refs[4:]
    land, sland, refs = refs[:4], refs[4:8], refs[8:]
    r = dict(zip(HELD, refs), out=out, gz=gz)
    gsend, grecv, own_sem, xsend, xrecv, bsend, brecv, ssend, srecv = refs[len(HELD) :]
    place = Place()
    layer = Layer(w, r)

    loads = [
        pltpu.make_async_copy(own_in, w.at[place.d, pl.ds(IN, 6)], own_sem.at[0]),
        pltpu.make_async_copy(own_out, w.at[place.d, pl.ds(OUT, 2)], own_sem.at[1]),
    ] + [
        pltpu.make_async_copy(
            own_down.at[:, :, pl.ds(q * 1024, 1024)], w.at[place.d, pl.ds(DOWN + 2 * q, 2)], own_sem.at[2 + q]
        )
        for q in range(4)
    ]
    for copy in loads:
        copy.start()
    token_load = pltpu.make_async_copy(tok, r["zin"], own_sem.at[6])
    cot_load = pltpu.make_async_copy(cot, r["gin"], own_sem.at[7])

    @pl.when(place.s == 0)
    def _():
        token_load.start()

    @pl.when(place.s == 3)
    def _():
        cot_load.start()

    w[place.d, UP : UP + 8] = own_up[...].T.reshape(8, 16, WIDTH)
    mine = lax.broadcasted_iota(jnp.int32, (1, 128), 1) // 32 == place.d % 4

    def spot(x):
        x = x.astype(F32)
        return jnp.where(mine, jnp.concatenate([x, x, x, x], axis=1), 0.0)

    small[place.d, 0:3] = spot(gains[...])
    small[place.d, 3:10] = spot(vecs[...])
    small[place.d, 10:11] = mgain[...].astype(F32)
    small[place.d, 11:13] = mbias[...].astype(F32)
    small[place.d, 13:16] = jnp.zeros((3, 128), F32)
    place.barrier()
    for copy in loads:
        copy.wait()

    def forward_copy(n):
        cols = pl.ds(n * 256, 256)
        return remote(
            out.at[:, cols], r["zin"].at[:, cols], xsend.at[n], xrecv.at[n], (place.s + 1) % 4, place.d
        )

    def send_forward(n):
        @pl.when(place.s < 3)
        def _():
            forward_copy(n).start()

    gather = Gather(place, w, small, gsend, grecv)

    def setup():
        for q in range(8):
            r["pd"][:, q * 128 : (q + 1) * 128] = small[4 * q] + small[4 * q + 1] + small[4 * q + 2] + small[4 * q + 3]
        for q in range(32):
            r["pm"][:, q * 128 : (q + 1) * 128] = small[q]
        r["pq"][:, :WIDTH] = r["pd"][4:5, :]
        r["pq"][:, WIDTH : 2 * WIDTH] = jnp.zeros((1, WIDTH), F32)
        r["pq"][:, 2 * WIDTH :] = r["pd"][5:6, :]
        heads = jnp.concatenate([hscale[...].astype(F32), jnp.zeros((1, 112), F32)], axis=1)
        r["hs"][...] = lax.dot_general(
            jnp.broadcast_to(heads, (8, 128)), head_columns(), (((1,), (0,)), ((), ())),
            precision=lax.Precision.HIGHEST, preferred_element_type=F32,
        )
        row = lax.broadcasted_iota(jnp.int32, (TOK, TOK), 0)
        col = lax.broadcasted_iota(jnp.int32, (TOK, TOK), 1)
        seg_key = jnp.broadcast_to(seg[...].astype(F32), (TOK, TOK))
        ok = (seg_key == seg_key.T) & (col <= row) & (row // 64 == col // 64)
        r["ok"][...] = jnp.where(ok, 1.0, 0.0)

    def ready(k):
        if k == 0:
            setup()

        @pl.when(place.s == 0)
        def _():
            if k == 0:
                token_load.wait()
                layer.first_norm()
            elif k == 1:
                layer.qkv()
                layer.attention()
            elif k == 2:
                layer.project()
                layer.middle_norms()
            elif k == 3:
                layer.up()
                layer.inner_norm()
            else:
                layer.down(send_forward)

    gather.run(ready)

    @pl.when(place.s > 0)
    def _():
        for n in range(4):
            forward_copy(n).wait_recv()
        layer.first_norm()
        layer.qkv()
        layer.attention()
        layer.project()
        layer.middle_norms()
        layer.up()
        layer.inner_norm()
        layer.down(send_forward)

    layer.prepare()
    gather.close()

    @pl.when(place.s < 3)
    def _():
        for n in range(4):
            forward_copy(n).wait_send()

    def backward_copy(i):
        at = pl.ds(i * 32, 32)
        return remote(gz.at[at], r["gin"].at[at], bsend.at[i], brecv.at[i], (place.s + 3) % 4, place.d)

    def send_backward(i):
        @pl.when(place.s > 0)
        def _():
            backward_copy(i).start()

    @pl.when(place.s == 3)
    def _():
        cot_load.wait()

        @each(4)
        def _(i):
            at = rows_of(i, 32)
            row = lax.broadcasted_iota(jnp.int32, (32, WIDTH), 0) + 32 * i
            alive = row % 64 < jnp.where(row < 64, live[0], live[1])
            r["gin"][at, :] = jnp.where(alive, r["gin"][at, :].astype(F32), 0.0).astype(BF16)

    @pl.when(place.s < 3)
    def _():
        for i in range(4):
            backward_copy(i).wait_recv()

    @pl.when(place.s > 0)
    def _():
        layer.back_down()
        layer.back_inner()
        layer.back_up()
        layer.back_middle()
        layer.back_project()
        layer.back_attention()
        layer.back_qkv()
        layer.back_first(send_backward)

    def first_section(*phases):
        @pl.when(place.s == 0)
        def _():
            for phase in phases:
                phase()

    scatter = Scatter(place, w, small, sib, ssib, land, sland, ssend, srecv)
    n = len(SCATTER)

    def flow(t):
        if 0 <= t - 1 < n:
            scatter.halves(t - 1)
        if 0 <= t - 2 < n:
            scatter.wholes(t - 2)
        if 0 <= t - 3 < n:
            scatter.far(t - 3)
        if 0 <= t - 4 < n:
            scatter.near(t - 4)
        if 0 <= t - 5 < n:
            scatter.last(t - 5, total, small_total)

    first_section(layer.back_down)
    layer.grad_down()
    scatter.to_sibling(0)
    scatter.to_sibling(1)
    first_section(layer.back_inner, layer.back_up)
    flow(1)
    layer.grad_up()
    scatter.to_sibling(2)
    scatter.to_sibling(3)
    flow(2)
    first_section(layer.back_middle, layer.back_project)
    flow(3)
    first_section(layer.back_attention)
    flow(4)
    first_section(layer.back_qkv, lambda: layer.back_first(send_backward))
    layer.grad_attention()
    scatter.to_sibling(4)
    scatter.to_sibling(5)
    flow(5)
    layer.inner_sums()
    layer.other_sums()
    layer.grad_small(small)
    scatter.to_sibling(6)
    for t in range(6, n + 5):
        flow(t)
    scatter.close()

    @pl.when(place.s > 0)
    def _():
        for i in range(4):
            backward_copy(i).wait_send()


VSPEC = pl.BlockSpec(memory_space=pltpu.VMEM)
ASPEC = pl.BlockSpec(memory_space=pl.ANY)
SSPEC = pl.BlockSpec(memory_space=pltpu.SMEM)
DMA = pltpu.SemaphoreType.DMA


def run_layers(*args):
    g, s = (len(GATHER), 36), (len(SCATTER), 36)
    return pl.pallas_call(
        kernel,
        out_shape=[
            jax.ShapeDtypeStruct((TOK, WIDTH), BF16),
            jax.ShapeDtypeStruct((TOK, WIDTH), BF16),
            jax.ShapeDtypeStruct((UNITS, 16, WIDTH), F32),
            jax.ShapeDtypeStruct((16, 128), F32),
        ],
        in_specs=[ASPEC, ASPEC, SSPEC, VSPEC, ASPEC, ASPEC, VSPEC, ASPEC, VSPEC, VSPEC, VSPEC, VSPEC, VSPEC],
        out_specs=[VSPEC] * 4,
        scratch_shapes=[
            pltpu.VMEM((32, UNITS, 16, WIDTH), BF16),
            pltpu.VMEM((32, 16, 128), F32),
            pltpu.VMEM((16, UNITS, 16, WIDTH), BF16),
            pltpu.VMEM((16, 16, 128), F32),
        ]
        + [pltpu.VMEM((SHARE, slots, units, 16, WIDTH), BF16) for slots, units in LANDING]
        + [pltpu.VMEM((slots, 4 * units, 128), F32) for slots, units in LANDING]
        + [pltpu.VMEM(*v) for v in HELD.values()]
        + [DMA(g), DMA(g), DMA((8,)), DMA((4,)), DMA((4,)), DMA((4,)), DMA((4,)), DMA(s), DMA(s)],
        compiler_params=pltpu.CompilerParams(collective_id=1, has_side_effects=True, vmem_limit_bytes=VMEM_LIMIT),
        name="layers",
    )(*args)


def finish_kernel(out, gz, total, small, out2, gz2, g_in, g_out, g_up, g_down, g_gains, g_vecs, g_mgain, g_mbias, g_heads):
    out2[...] = out[...]
    gz2[...] = gz[...]
    g_in[...] = total[IN : IN + 6]
    g_out[...] = total[OUT : OUT + 2]
    for q in range(4):
        g_down[:, :, q * 1024 : (q + 1) * 1024] = total[DOWN + 2 * q : DOWN + 2 * q + 2]
    g_up[...] = total[UP : UP + 8].reshape(128, WIDTH).T
    lane = lax.axis_index("dp") % 4
    thin = jnp.zeros((10, 32), F32)
    for j in range(4):
        thin = jnp.where(lane == j, small[0:10, 32 * j : 32 * (j + 1)], thin)
    for i in range(3):
        g_gains[i] = thin[i : i + 1]
    for i in range(7):
        g_vecs[i] = thin[3 + i : 4 + i]
    g_mgain[...] = small[10:11, :]
    g_mbias[...] = small[11:13, :]
    g_heads[...] = small[13:14, :16]


def finish(*args):
    f = jax.ShapeDtypeStruct
    return pl.pallas_call(
        finish_kernel,
        out_shape=[
            f((TOK, WIDTH), BF16), f((TOK, WIDTH), BF16), f((6, 16, WIDTH), F32), f((2, 16, WIDTH), F32),
            f((WIDTH, 128), F32), f((2, 16, FF), F32), f((3, 1, 32), F32), f((7, 1, 32), F32), f((1, 128), F32),
            f((2, 128), F32), f((1, 16), F32),
        ],
        in_specs=[VSPEC] * 4,
        out_specs=[VSPEC] * 11,
        name="finish",
    )(*args)


def body(
    tokens, cotangent, live_counts, segments, attn_input, attn_output, feed_up, feed_down,
    norm_gains, vector_bias, mid_gain, mid_bias, head_scale,
):
    res = run_layers(
        tokens, cotangent, live_counts, segments[None, :], attn_input[0].T.reshape(6, 16, WIDTH),
        attn_output[0].T.reshape(2, 16, WIDTH), feed_up[0], feed_down[0].T.reshape(2, 16, FF), norm_gains[0],
        vector_bias[0], mid_gain, mid_bias[0], head_scale,
    )
    out, gz, g_in, g_out, g_up, g_down, g_gains, g_vecs, g_mgain, g_mbias, g_heads = finish(*res)
    return (
        out[None],
        gz[None],
        g_in.reshape(96, WIDTH).T[None],
        g_out.reshape(32, WIDTH).T[None],
        g_up[None],
        g_down.reshape(32, FF).T[None],
        g_gains.transpose(1, 0, 2),
        g_vecs.transpose(1, 0, 2),
        g_mgain,
        g_mbias[None],
        g_heads,
    )


def solution(mesh):
    return jax.shard_map(
        body,
        mesh=mesh,
        in_specs=(
            P("dp", None), P("dp", None), P("dp"), P("dp"),
            P("pipe", None, "dp"), P("pipe", None, "dp"), P("pipe", None, "dp"), P("pipe", None, "dp"),
            P("pipe", None, "dp"), P("pipe", None, "dp"), P("pipe", "dp"), P("pipe", None, "dp"), P("pipe", None),
        ),
        out_specs=(
            P("pipe", "dp", None), P("pipe", "dp", None),
            P("pipe", None, "dp"), P("pipe", None, "dp"), P("pipe", None, "dp"), P("pipe", None, "dp"),
            P("pipe", None, "dp"), P("pipe", None, "dp"), P("pipe", "dp"), P("pipe", None, "dp"), P("pipe", None),
        ),
        check_vma=False,
    )
```

```python
import jax
import jax.numpy as jnp
from jax import lax
from jax.experimental import pallas as pl
from jax.experimental.pallas import tpu as pltpu
from jax.sharding import PartitionSpec as P

MESH = pl.DeviceIdType.MESH
EPS = 1e-05
F32, BF16 = jnp.float32, jnp.bfloat16
VMEM_LIMIT = 61840 * 1024

TOK, WIDTH, FF, QKV = 128, 1024, 4096, 3072
IN, OUT, UP, DOWN, UNITS = 0, 6, 8, 16, 24
SMALL = "small"
GATHER = (SMALL, (IN, 6), (OUT, 2), (UP, 8), (DOWN + 4, 4), (DOWN, 4))
SCATTER = ((DOWN + 4, 4), (UP, 4), (UP + 4, 4), (IN, 4), SMALL, (IN + 4, 4), (DOWN, 4))
LENT = (DOWN, 4)
LATE, HELP = 5, 6
AWAY, AID = 6, 7
DESK = (DOWN + 4, 4)
X_OWN, X_GIVE, X_SUMS, X_BACK = 0, 1, 5, 8
BACK_GROUPS = (
    ((1, 0), (2, 0), (3, 0)),
    ((0, 1), (0, 2), (1, 1), (1, 2)),
    ((2, 1), (2, 2), (3, 1), (3, 2)),
    ((0, 3), (1, 3), (2, 3), (3, 3)),
)
SHARE = 3
OFFS = (0, 3, 1, 2)


class Place:
    def __init__(self):
        self.s = lax.axis_index("pipe")
        d = lax.axis_index("dp")
        self.d = d
        self.c = d % 2
        y, z = (d // 2) % 4, d // 8
        self.f = y + self.c * (z - y)
        self.g = z + self.c * (y - z)
        self.sf = 2 + 6 * self.c
        self.sg = 8 - 6 * self.c
        self.sib = d + 1 - 2 * self.c

    def dp(self, of, og):
        return ((self.f + of) % 4) * self.sf + ((self.g + og) % 4) * self.sg + self.c

    def sib_dp(self, of, og):
        return ((self.g + of) % 4) * self.sg + ((self.f + og) % 4) * self.sf + 1 - self.c

    def greet(self):
        sem = pltpu.get_barrier_semaphore()
        near = [self.dp(1, 0), self.dp(3, 0), self.dp(0, 1), self.dp(0, 3), self.sib]
        near = [(self.s, to) for to in near] + [((self.s + by) % 4, self.d) for by in (1, 3)]
        for to in near:
            pl.semaphore_signal(sem, inc=1, device_id=to, device_id_type=MESH)

    def barrier(self):
        pl.semaphore_wait(pltpu.get_barrier_semaphore(), 7)


class Work:
    def __init__(self):
        self.items = []

    def add(self, slice_of_work, when=None, tag=None):
        self.items.append((slice_of_work, when, tag))

    def pop(self, count=1):
        for _ in range(min(count, len(self.items))):
            slice_of_work, when, _ = self.items.pop(0)
            if when is None:
                slice_of_work()
            else:
                pl.when(when)(slice_of_work)

    def until(self, tag):
        while any(tag == item[2] for item in self.items):
            self.pop()

    def drain(self):
        self.pop(len(self.items))


def remote(src, dst, send, recv, s, to):
    return pltpu.make_async_remote_copy(
        src_ref=src, dst_ref=dst, send_sem=send, recv_sem=recv, device_id=(s, to), device_id_type=MESH
    )


def piece_block(whole, small, piece, d, half=None):
    if piece is SMALL:
        return small.at[d] if half is None else small.at[d, pl.ds(8 * half, 8)]
    u, n = piece
    return whole.at[d, pl.ds(u, n)] if half is None else whole.at[d, pl.ds(u + half * (n // 2), n // 2)]


def blocks(whole, small, piece, count, first=0):
    if piece is SMALL:
        return small.at[pl.ds(first, count)]
    return whole.at[pl.ds(first, count), pl.ds(*piece)]


class Gather:
    def __init__(self, place, whole, small, lent, send, recv, xsend, xrecv):
        self.p, self.whole_ref, self.small, self.lent = place, whole, small, lent
        self.send, self.recv, self.xsend, self.xrecv = send, recv, xsend, xrecv
        self.work = Work()

    def ref(self, k, d, half=None):
        if k == HELP:
            u, n = LENT
            at = pl.ds(u, n) if half is None else pl.ds(u + half * (n // 2), n // 2)
            return self.lent.at[d // 2, at]
        return piece_block(self.whole_ref, self.small, GATHER[k], d, half)

    def put(self, k, slot, d, half, to):
        ref = self.ref(k, d, half)
        remote(ref, ref, self.send.at[k], self.recv.at[k, slot], self.p.s, to).start()

    def got(self, k, slot, d):
        ref = self.ref(k, d)
        remote(ref, ref, self.send.at[k], self.recv.at[k, slot], self.p.s, self.p.sib).wait_recv()

    def hand(self, k, j, i):
        p = self.p
        d = p.dp(OFFS[j], OFFS[i])
        if k != HELP:
            self.put(k, 15, d, None, p.sib)
        elif (j, i) != (0, 0):
            self.give(j, i).start()

    def give(self, j, i):
        p = self.p
        d = p.dp(OFFS[j], OFFS[i])
        group = next(g for g, group in enumerate(BACK_GROUPS) if (j, i) in group)
        return remote(
            self.ref(HELP, d), self.ref(LATE, d), self.xsend.at[1], self.xrecv.at[X_GIVE + group], (p.s + 1) % 4, p.d
        )

    def lend(self):
        p = self.p
        return remote(
            self.ref(LATE, p.d), self.ref(HELP, p.d), self.xsend.at[0], self.xrecv.at[X_OWN], (p.s + 3) % 4, p.d
        )

    def spread(self, k, j):
        p = self.p
        d = p.dp(OFFS[j], 0)
        self.put(k, 3 + 3 * j, d, None, p.dp(0, 1))
        self.put(k, 4 + 3 * j, d, None, p.dp(0, 3))
        self.hand(k, j, 0)

    def first(self, k):
        p = self.p
        self.put(k, 0, p.d, None, p.dp(1, 0))
        self.put(k, 1, p.d, None, p.dp(3, 0))
        self.spread(k, 0)

    def ring(self, k):
        p = self.p
        left, right = p.dp(3, 0), p.dp(1, 0)
        self.got(k, 0, left)
        self.put(k, 2, left, 0, right)
        self.spread(k, 1)
        self.got(k, 1, right)
        self.put(k, 2, right, 1, left)
        self.spread(k, 2)

    def far(self, k):
        self.got(k, 2, self.p.dp(2, 0))
        self.spread(k, 3)

    def second(self, k, j):
        p = self.p
        low, high = p.dp(OFFS[j], 3), p.dp(OFFS[j], 1)
        self.got(k, 3 + 3 * j, low)
        self.put(k, 5 + 3 * j, low, 0, p.dp(0, 1))
        self.hand(k, j, 1)
        self.got(k, 4 + 3 * j, high)
        self.put(k, 5 + 3 * j, high, 1, p.dp(0, 3))
        self.hand(k, j, 2)

    def last(self, k, j):
        self.got(k, 5 + 3 * j, self.p.dp(OFFS[j], 2))
        self.hand(k, j, 3)

    def relay(self, group):
        p = self.p
        ref = self.many(LATE, len(BACK_GROUPS[group]))
        remote(ref, ref, self.xsend.at[1], self.xrecv.at[X_GIVE + group], p.s, p.sib).wait_recv()
        for j, i in BACK_GROUPS[group]:
            self.hand(LATE, j, i)

    def many(self, k, count):
        if k == HELP:
            return blocks(self.lent, None, LENT, count)
        return blocks(self.whole_ref, self.small, GATHER[k], count)

    def whole(self, k):
        ref = self.many(k, 16)
        remote(ref, ref, self.send.at[k], self.recv.at[k, 15], self.p.s, self.p.sib).wait_recv()

    def close(self):
        p = self.p

        def sent(k, count):
            ref = self.many(k, count)
            remote(ref, ref, self.send.at[k], self.recv.at[k, 15], p.s, p.sib).wait_send()

        for k in range(len(GATHER)):
            if k != LATE:
                sent(k, 31)

        @pl.when(p.s > 0)
        def _():
            sent(LATE, 31)

        @pl.when(p.s == 0)
        def _():
            sent(LATE, 16)
            self.lend().wait_send()

        @pl.when(p.s == 3)
        def _():
            sent(HELP, 15)
            ref = self.many(HELP, 15)
            remote(ref, ref, self.xsend.at[1], self.xrecv.at[X_GIVE], p.s, p.sib).wait_send()

    def run(self, own, ready):
        n, begun = len(GATHER), 0
        s = self.p.s

        def stage(step, k):
            if k == LATE:
                pl.when(s > 0)(lambda: step(k))
            elif 0 <= k < n:
                step(k)

        own(LATE)

        @pl.when(s == 0)
        def _():
            self.lend().start()
            self.hand(LATE, 0, 0)

        @pl.when(s == 3)
        def _():
            self.lend().wait_recv()
            for step in (self.first, self.ring, self.far):
                step(HELP)
            for j in range(4):
                self.second(HELP, j)
            for j in range(4):
                self.last(HELP, j)

        for t in range(n + 3):
            while begun < min(n, t + 3):
                if begun != LATE:
                    own(begun)
                stage(self.first, begun)
                begun += 1
            stage(self.ring, t)
            self.work.pop()
            stage(self.far, t - 1)
            self.work.pop()
            for j in range(4):
                stage(lambda k, j=j: self.second(k, j), t - 2)
                self.work.pop()
            for j in range(4):
                stage(lambda k, j=j: self.last(k, j), t - 3)
                self.work.pop()
            if 4 <= t < 8:
                pl.when(s == 0)(lambda t=t: self.relay(t - 4))

            self.work.pop()
            if t >= 3:
                self.whole(t - 3)
                ready(t - 3)
        self.work.drain()


def dot(a, b, ca, cb):
    return lax.dot_general(a, b, (((ca,), (cb,)), ((), ())), preferred_element_type=F32)


def centered(x):
    c = x - jnp.mean(x, axis=-1, keepdims=True)
    r = lax.rsqrt(jnp.mean(c * c, axis=-1, keepdims=True) + EPS)
    return c, r


def norm(x, gain, bias):
    c, r = centered(x)
    return c * r * gain + bias


def norm_back(x, gain, gy):
    c, r = centered(x)
    hat = c * r
    gh = gy * gain
    gx = r * (gh - jnp.mean(gh, axis=-1, keepdims=True) - hat * jnp.mean(gh * hat, axis=-1, keepdims=True))
    return gx, gy * hat


def rows_of(i, n):
    return pl.ds(pl.multiple_of(i * n, n), n)


def col_sum(x):
    return jnp.sum(x, axis=0, keepdims=True)


def row_sum(x):
    return dot(jnp.full((16, x.shape[0]), 1.0, BF16), x, 1, 0)[:1]


K0, K1 = 0.7978845608028654, 0.044715


def gelu(x):
    return 0.5 * x * (1.0 + jnp.tanh(K0 * (x + K1 * x * x * x)))


def gelu_both(x):
    t = jnp.tanh(K0 * (x + K1 * x * x * x))
    u = 0.5 * x * (1.0 + t)
    du = 0.5 * (1.0 + t) + 0.5 * x * (1.0 - t * t) * K0 * (1.0 + 3.0 * K1 * x * x)
    return u, du


def head_masks():
    lane = lax.broadcasted_iota(jnp.int32, (1, 128), 1)
    even = jnp.where(lane < 64, 1.0, 0.0)
    return even.astype(BF16), (1.0 - even).astype(BF16)


def two_rows(x, even, odd):
    return jnp.concatenate([x * even, x * odd], axis=0)


def each(count, unroll=1):
    def run(body):
        def step(i, carry):
            body(i)
            return carry

        lax.fori_loop(0, count, step, 0, unroll=unroll)

    return run


def stack(w, d0, nd, u, nu, cols=slice(0, WIDTH)):
    return w[pl.ds(d0, nd), u : u + nu, :, cols].reshape(nd * nu * 16, cols.stop - cols.start)


def head_columns():
    col = lax.broadcasted_iota(jnp.int32, (128, WIDTH), 1)
    head = lax.broadcasted_iota(jnp.int32, (128, WIDTH), 0)
    return jnp.where(col // 64 == head, 1.0, 0.0)


class Layer:
    def __init__(self, w, r):
        self.w, self.r = w, r


    def first_norm(self):
        r, pd = self.r, self.r["pd"]

        @each(4, 2)
        def _(i):
            at = rows_of(i, 32)
            r["a1"][at, :] = norm(r["zin"][at, :].astype(F32), pd[0:1, :], pd[3:4, :]).astype(BF16)

    def qkv(self, first=0, count=4):
        r = self.r
        for c in range(first, first + count):
            at = slice(c * 768, (c + 1) * 768)
            acc = dot(r["a1"][...], stack(self.w, 8 * c, 8, IN, 6), 1, 1) + r["pq"][0:1, at]
            r["qkv"][:, at] = acc.astype(BF16)

    def attention(self, first=0, count=8):
        r, qkv = self.r, self.r["qkv"]
        even, odd = head_masks()

        @each(count, min(count, 4))
        def _(p):
            p = p + first
            cols = rows_of(p, 128)
            q = qkv[:, cols]
            k = qkv[:, pl.ds(pl.multiple_of(WIDTH + p * 128, 128), 128)]
            v = qkv[:, pl.ds(pl.multiple_of(2 * WIDTH + p * 128, 128), 128)]
            ok = r["ok"][...]
            sc = dot(two_rows(q, even, odd), k, 1, 1) * 0.125
            sc = jnp.where(jnp.concatenate([ok, ok], axis=0) > 0.5, sc, -1000000000.0)
            e = jnp.exp(sc - jnp.max(sc, axis=-1, keepdims=True))
            pr = e / jnp.sum(e, axis=-1, keepdims=True)
            r["p"][rows_of(p, 256), :] = pr
            pb = pr.astype(BF16)
            both = jnp.concatenate([pb[:TOK], pb[TOK:]], axis=1)
            mixed = dot(both, two_rows(v, even, odd), 1, 0)
            r["mixed"][:, cols] = mixed
            r["scaled"][:, cols] = (mixed * r["hs"][0:1, cols]).astype(BF16)

    def project(self):
        r = self.r
        r["attn"][...] = dot(r["scaled"][...], stack(self.w, 0, 32, OUT, 2), 1, 1) + r["pd"][6:7, :]

    def middle_norms(self):
        r, pd = self.r, self.r["pd"]

        @each(4, 2)
        def _(i):
            at = rows_of(i, 32)
            z2 = r["zin"][at, :].astype(F32) + norm(r["attn"][at, :], pd[1:2, :], pd[7:8, :])
            r["z2"][at, :] = z2
            r["a2"][at, :] = norm(z2, pd[2:3, :], pd[8:9, :]).astype(BF16)

    def up(self, first=0, count=4):
        r = self.r

        @each(count)
        def _(c):
            c = c + first
            cols = rows_of(c, 1024)
            r["ff"][:, cols] = dot(r["a2"][...], stack(self.w, 8 * c, 8, UP, 8), 1, 1) + r["pm"][11:12, cols]

    def inner_norm(self, first=0, count=8):
        r, pm = self.r, self.r["pm"]

        @each(count, 2)
        def _(i):
            i = i + first
            at = rows_of(i, 16)
            r["mid"][at, :] = norm(gelu(r["ff"][at, :]), pm[10:11, :], pm[12:13, :]).astype(BF16)

    def down(self, send_out):
        r = self.r
        for n in range(4):
            cols = slice(n * 256, (n + 1) * 256)
            acc = r["z2"][:, cols] + r["pd"][9:10, cols]
            for q in range(4):
                w = stack(self.w, 8 * n, 8, DOWN + 2 * q, 2)
                acc = acc + dot(r["mid"][:, q * 1024 : (q + 1) * 1024], w, 1, 1)
            r["out"][:, cols] = acc.astype(BF16)
            send_out(n)

    def prepare(self):
        r = self.r

        @each(8, 2)
        def _(i):
            at = rows_of(i, 16)
            u, du = gelu_both(r["ff"][at, :])
            c, s = centered(u)
            r["hat"][at, :] = (c * s).astype(BF16)
            r["slope"][at, :] = (du * s).astype(BF16)

        for name in ("gd", "gm"):
            r[name][...] = jnp.zeros_like(r[name])


    def back_down(self, *chunks):
        r = self.r
        for q in chunks:
            w = stack(self.w, 0, 32, DOWN + 2 * q, 2)
            r["ff"][:, q * 1024 : (q + 1) * 1024] = dot(r["gin"][...], w, 1, 0)

    def back_inner(self, first=0, count=8):
        r, pm = self.r, self.r["pm"]

        @each(count, 2)
        def _(i):
            i = i + first
            at = rows_of(i, 16)
            gh = r["ff"][at, :] * pm[10:11, :]
            hat = r["hat"][at, :].astype(F32)
            m1 = jnp.mean(gh, axis=-1, keepdims=True)
            m2 = jnp.mean(gh * hat, axis=-1, keepdims=True)
            r["ghid"][at, :] = ((gh - m1 - hat * m2) * r["slope"][at, :].astype(F32)).astype(BF16)

    def back_up(self, cols=slice(0, WIDTH)):
        r = self.r
        r["tw"][:, cols] = dot(r["ghid"][...], stack(self.w, 0, 32, UP, 8, cols), 1, 0)

    def back_middle(self):
        r, gd, pd = self.r, self.r["gd"], self.r["pd"]

        @each(4, 2)
        def _(i):
            at = rows_of(i, 32)
            ga2 = r["tw"][at, :]
            gz, gg = norm_back(r["z2"][at, :], pd[2:3, :], ga2)
            gd[2:3, :] += col_sum(gg)
            gd[8:9, :] += col_sum(ga2)
            gz = gz + r["gin"][at, :].astype(F32)
            r["gz2"][at, :] = gz
            gat, gg = norm_back(r["attn"][at, :], pd[1:2, :], gz)
            gd[1:2, :] += col_sum(gg)
            gd[7:8, :] += col_sum(gz)
            r["gattn"][at, :] = gat.astype(BF16)

    def back_project(self):
        r = self.r
        r["tw"][...] = dot(r["gattn"][...], stack(self.w, 0, 32, OUT, 2), 1, 0)

    def back_attention(self, first=0, count=8):
        r = self.r
        even, odd = head_masks()

        @each(count, min(count, 4))
        def _(p):
            p = p + first
            cols = rows_of(p, 128)
            kcols = pl.ds(pl.multiple_of(WIDTH + p * 128, 128), 128)
            vcols = pl.ds(pl.multiple_of(2 * WIDTH + p * 128, 128), 128)
            gs = r["tw"][:, cols]
            r["gh"][0:1, cols] = col_sum(gs * r["mixed"][:, cols])
            gmx = (gs * r["hs"][0:1, cols]).astype(BF16)
            q, k, v = r["qkv"][:, cols], r["qkv"][:, kcols], r["qkv"][:, vcols]
            gmx2 = two_rows(gmx, even, odd)
            gp = dot(gmx2, v, 1, 1)
            pr = r["p"][rows_of(p, 256), :]
            gsc = (pr * (gp - jnp.sum(pr * gp, axis=-1, keepdims=True))).astype(BF16)
            both = jnp.concatenate([gsc[:TOK], gsc[TOK:]], axis=1)
            r["gqkv"][:, cols] = (dot(both, two_rows(k, even, odd), 1, 0) * 0.125).astype(BF16)
            r["gqkv"][:, kcols] = (dot(gsc, two_rows(q, even, odd), 0, 0) * 0.125).astype(BF16)
            r["gqkv"][:, vcols] = dot(pr.astype(BF16), gmx2, 0, 0).astype(BF16)

    def back_qkv(self, cols=slice(0, WIDTH)):
        r = self.r
        r["tw"][:, cols] = dot(r["gqkv"][...], stack(self.w, 0, 32, IN, 6, cols), 1, 0)

    def back_first(self, send_out):
        r, gd, pd = self.r, self.r["gd"], self.r["pd"]
        for i in range(4):
            at = slice(i * 32, (i + 1) * 32)
            ga1 = r["tw"][at, :]
            gz, gg = norm_back(r["zin"][at, :].astype(F32), pd[0:1, :], ga1)
            r["gz"][at, :] = (gz + r["gz2"][at, :]).astype(BF16)
            send_out(i)
            gd[0:1, :] += col_sum(gg)
            gd[3:4, :] += col_sum(ga1)

    def inner_sums(self):
        r, gm = self.r, self.r["gm"]

        @each(8)
        def _(i):
            at = rows_of(i, 16)
            g = r["ff"][at, :]
            gm[10:11, :] += col_sum(g * r["hat"][at, :].astype(F32))
            gm[12:13, :] += col_sum(g)

        gm[11:12, :] = row_sum(r["ghid"][...])

    def other_sums(self):
        r, gd = self.r, self.r["gd"]
        gd[9:10, :] = row_sum(r["gin"][...])
        gd[6:7, :] = row_sum(r["gattn"][...])
        gd[4:5, :] = row_sum(r["gqkv"][:, :WIDTH])
        gd[5:6, :] = row_sum(r["gqkv"][:, 2 * WIDTH :])


    def grad_down(self, *chunks):
        r = self.r

        @each(4)
        def _(c):
            gt = r["gin"][:, rows_of(c, 256)].T
            for q in chunks:
                g = dot(gt, r["mid"][:, q * 1024 : (q + 1) * 1024], 1, 0).astype(BF16)
                self.w[pl.ds(8 * c, 8), DOWN + 2 * q : DOWN + 2 * q + 2] = g.reshape(8, 2, 16, WIDTH)

    def grad_up(self, c):
        r = self.r
        g = dot(r["ghid"][:, c * 512 : (c + 1) * 512].T, r["a2"][...], 1, 0).astype(BF16)
        self.w[pl.ds(4 * c, 4), UP : UP + 8] = g.reshape(4, 8, 16, WIDTH)

    def grad_in(self, c):
        r = self.r
        g = dot(r["gqkv"][:, c * 384 : (c + 1) * 384].T, r["a1"][...], 1, 0).astype(BF16)
        self.w[pl.ds(4 * c, 4), IN : IN + 6] = g.reshape(4, 6, 16, WIDTH)

    def grad_out(self, c):
        r = self.r
        g = dot(r["gattn"][:, c * 512 : (c + 1) * 512].T, r["scaled"][...], 1, 0).astype(BF16)
        self.w[pl.ds(16 * c, 16), OUT : OUT + 2] = g.reshape(16, 2, 16, WIDTH)

    def grad_small(self, small):
        r = self.r
        hsum = lax.dot_general(
            jnp.broadcast_to(r["gh"][0:1, :], (8, WIDTH)), head_columns(), (((1,), (1,)), ((), ())),
            precision=lax.Precision.HIGHEST, preferred_element_type=F32,
        )
        is13 = lax.broadcasted_iota(jnp.int32, (16, 128), 0) == 13
        heads = jnp.where(is13, jnp.concatenate([hsum, hsum], axis=0), 0.0)
        for d in range(32):
            a, b = (d // 4) * 128, d * 128
            small[d] = r["gd"][:, a : a + 128] + r["gm"][:, b : b + 128] + heads


class Scatter:
    def __init__(self, place, grads, small, sib, ssib, land, sland, back, send, recv, xsend, xrecv):
        self.p, self.grads, self.small = place, grads, small
        self.sib, self.ssib, self.land, self.sland, self.back = sib, ssib, land, sland, back
        self.send, self.recv, self.xsend, self.xrecv = send, recv, xsend, xrecv
        self.work = Work()

    def copy(self, k, slot, src, dst, to):
        return remote(src, dst, self.send.at[k], self.recv.at[k, slot], self.p.s, to)

    def go(self, k, slot, src, dst, to):
        self.copy(k, slot, src, dst, to).start()

    def got(self, k, slot, dst):
        self.copy(k, slot, dst, dst, self.p.sib).wait_recv()

    def block(self, k, of, og, half=None):
        d = self.p.dp(of, og)
        if k == AID:
            return piece_block(self.sib, None, DESK, d // 2, half)
        return piece_block(self.grads, self.small, SCATTER[k], d, half)

    def from_sib(self, k, slot, half=None):
        return piece_block(self.sib, self.ssib, SCATTER[k], slot, half)

    def landing(self, k, kind, slot):
        if k != AID and SCATTER[k] is SMALL:
            return self.sland[kind].at[slot]
        return self.land[kind].at[k % SHARE, slot]

    def landed(self, k, slot, kind, j=0):
        self.got(k, slot, self.landing(k, kind, pl.ds(2 * j, 2)))

    def to_sibling(self, k):
        p = self.p
        for i in (3, 1, 2, 0):
            for j in (3, 1, 2, 0):
                src = piece_block(self.grads, self.small, SCATTER[k], p.sib_dp(OFFS[j], OFFS[i]))
                self.go(k, 0 if i == 3 else 1, src, self.from_sib(k, i * 4 + j), p.sib)

    def lent_sum(self, i, j):
        p = self.p
        return remote(
            self.block(AWAY, OFFS[j], OFFS[i]), self.block(AID, OFFS[j], OFFS[i]), self.xsend.at[2],
            self.xrecv.at[X_SUMS + (2, 1, 1, 0)[i]], (p.s + 3) % 4, p.d,
        )

    def lend(self):
        for i in (3, 1, 2, 0):
            if i in (3, 1):
                self.arrived(AWAY, i == 3)
            for j in (3, 1, 2, 0):
                self.add(AWAY, self.block(AWAY, OFFS[j], OFFS[i]), [self.from_sib(AWAY, i * 4 + j)])
                self.lent_sum(i, j).start()

    def returned(self):
        p = self.p
        return remote(
            self.block(AID, 0, 0), self.back, self.xsend.at[3], self.xrecv.at[X_BACK], (p.s + 1) % 4, p.d
        )

    def arrived(self, k, far):
        first, count = (12, 4) if far else (0, 12)
        self.got(k, 0 if far else 1, blocks(self.sib, self.ssib, SCATTER[k], count, first))

    def lent_arrived(self, group):
        ref = blocks(self.sib, None, DESK, (4, 8, 4)[group])
        remote(ref, ref, self.xsend.at[2], self.xrecv.at[X_SUMS + group], self.p.s, self.p.sib).wait_recv()

    def add(self, k, dst, srcs, store=None):
        out = dst if store is None else store
        if store is None and not srcs:
            return
        if k != AID and SCATTER[k] is SMALL:
            out[...] = dst[...] + sum(src[...] for src in srcs)
            return
        for u in range(dst.shape[0]):
            acc = dst[u].astype(F32)
            for src in srcs:
                acc = acc + src[u].astype(F32)
            out[u] = acc.astype(out.dtype)

    def halves(self, k, j):
        p = self.p
        srcs = []
        if k == AID:
            if j == 3:
                self.lent_arrived(0)
        else:
            if j == 3:
                self.arrived(k, True)
            srcs = [self.from_sib(k, 12 + j)]
        self.add(k, self.block(k, OFFS[j], 2), srcs)
        for side, to in enumerate((p.dp(0, 1), p.dp(0, 3))):
            self.go(k, 2 + j, self.block(k, OFFS[j], 2, side), self.landing(k, 0, 2 * j + side), to)

    def wholes(self, k, j):
        p = self.p
        if j == 3:
            if k == AID:
                self.lent_arrived(1)
            else:
                self.arrived(k, False)
        self.landed(k, 2 + j, 0, j)
        for i, near, side in ((2, 1, 0), (1, 3, 1)):
            for half in range(2):
                srcs = [] if k == AID else [self.from_sib(k, i * 4 + j, half)]
                if half == side:
                    srcs.append(self.landing(k, 0, 2 * j + side))
                self.add(k, self.block(k, OFFS[j], near, half), srcs)
        for near, side in ((1, 0), (3, 1)):
            self.go(k, 6 + j, self.block(k, OFFS[j], near), self.landing(k, 1, 2 * j + side), p.dp(0, near))

    def far(self, k, j):
        p = self.p
        srcs = []
        if k != AID:
            srcs.append(self.from_sib(k, j))
        elif j == 3:
            self.lent_arrived(2)
        self.landed(k, 6 + j, 1, j)
        srcs += [self.landing(k, 1, 2 * j + side) for side in range(2)]
        self.add(k, self.block(k, OFFS[j], 0), srcs)
        if j == 3:
            self.go(k, 10, self.block(k, 2, 0, 0), self.landing(k, 2, 0), p.dp(1, 0))
            self.go(k, 10, self.block(k, 2, 0, 1), self.landing(k, 2, 1), p.dp(3, 0))

    def near(self, k):
        p = self.p
        self.landed(k, 10, 2)
        for near, side in ((1, 0), (3, 1)):
            self.add(k, self.block(k, near, 0, side), [self.landing(k, 2, side)])
        for near, side in ((1, 0), (3, 1)):
            self.go(k, 11, self.block(k, near, 0), self.landing(k, 3, side), p.dp(near, 0))

    def last(self, k, total, small_total):
        self.landed(k, 11, 3)
        srcs = [self.landing(k, 3, side) for side in range(2)]
        if k == AID:
            self.add(k, self.block(k, 0, 0), srcs)
            self.returned().start()
        elif SCATTER[k] is SMALL:
            self.add(k, self.block(k, 0, 0), srcs, store=small_total)
        else:
            u, n = SCATTER[k]
            self.add(k, self.block(k, 0, 0), srcs, store=total.at[pl.ds(u, n)])

    def aid(self):
        for step in (self.halves, self.wholes, self.far):
            for j in (3, 1, 2, 0):
                step(AID, j)
        self.near(AID)
        self.last(AID, None, None)

    def close(self):
        p = self.p

        def sent(k, count):
            if k == AID:
                ref = blocks(self.sib, None, DESK, count)
            else:
                ref = blocks(self.grads, self.small, SCATTER[k], count)
            self.copy(k, 0, ref, ref, p.sib).wait_send()

        for k in range(len(SCATTER)):
            if k != AWAY:
                sent(k, 31)

        @pl.when(p.s > 0)
        def _():
            sent(AWAY, 31)

        @pl.when(p.s == 0)
        def _():
            sent(AWAY, 16)
            ref = blocks(self.grads, None, LENT, 16)
            remote(ref, ref, self.xsend.at[2], self.xrecv.at[X_SUMS], p.s, p.sib).wait_send()

        @pl.when(p.s == 3)
        def _():
            sent(AID, 15)
            self.returned().wait_send()


HELD = dict(
    pd=((16, WIDTH), F32), pm=((16, FF), F32), pq=((1, QKV), F32), hs=((8, WIDTH), F32), ok=((TOK, TOK), F32),
    zin=((TOK, WIDTH), BF16), a1=((TOK, WIDTH), BF16), qkv=((TOK, QKV), BF16), p=((8 * 256, TOK), F32),
    mixed=((TOK, WIDTH), F32), scaled=((TOK, WIDTH), BF16), attn=((TOK, WIDTH), F32), z2=((TOK, WIDTH), F32),
    a2=((TOK, WIDTH), BF16), ff=((TOK, FF), F32), hat=((TOK, FF), BF16), slope=((TOK, FF), BF16), mid=((TOK, FF), BF16),
    gin=((TOK, WIDTH), BF16), ghid=((TOK, FF), BF16), gattn=((TOK, WIDTH), BF16), gqkv=((TOK, QKV), BF16),
    tw=((TOK, WIDTH), F32), gz2=((TOK, WIDTH), F32), gd=((16, WIDTH), F32), gm=((16, FF), F32), gh=((8, WIDTH), F32),
)
LANDING = ((8, 2), (8, 4), (2, 2), (2, 4))


def kernel(*refs):
    (tok, cot, live, seg, own_in, own_out, own_up, own_down, gains, vecs, mgain, mbias, hscale), refs = refs[:13], refs[13:]
    (out, gz, total, small_total), refs = refs[:4], refs[4:]
    (w, small, sib, ssib), refs = refs[:4], refs[4:]
    land, sland, refs = refs[:4], refs[4:8], refs[8:]
    back, refs = refs[0], refs[1:]
    r = dict(zip(HELD, refs), out=out, gz=gz)
    gsend, grecv, own_sem, xsend, xrecv, bsend, brecv, ssend, srecv, hsend, hrecv, sib_ok, lent_ok = refs[len(HELD) :]
    place = Place()
    layer = Layer(w, r)
    place.greet()

    loads = [
        pltpu.make_async_copy(
            own_down.at[:, :, pl.ds(q * 1024, 1024)], w.at[place.d, pl.ds(DOWN + 2 * q, 2)], own_sem.at[q]
        )
        for q in range(4)
    ] + [
        pltpu.make_async_copy(own_in, w.at[place.d, pl.ds(IN, 6)], own_sem.at[4]),
        pltpu.make_async_copy(own_out, w.at[place.d, pl.ds(OUT, 2)], own_sem.at[5]),
    ]
    for copy in loads:
        copy.start()
    token_load = pltpu.make_async_copy(tok, r["zin"], own_sem.at[6])
    cot_load = pltpu.make_async_copy(cot, r["gin"], own_sem.at[7])

    @pl.when(place.s == 0)
    def _():
        token_load.start()

    @pl.when(place.s == 3)
    def _():
        cot_load.start()

    mine = lax.broadcasted_iota(jnp.int32, (1, 128), 1) // 32 == place.d % 4

    def spot(x):
        x = x.astype(F32)
        return jnp.where(mine, jnp.concatenate([x, x, x, x], axis=1), 0.0)

    small[place.d, 0:3] = spot(gains[...])
    small[place.d, 3:10] = spot(vecs[...])
    small[place.d, 10:11] = mgain[...].astype(F32)
    small[place.d, 11:13] = mbias[...].astype(F32)
    small[place.d, 13:16] = jnp.zeros((3, 128), F32)
    place.barrier()

    def own(k):
        if k == 3:
            w[place.d, UP : UP + 8] = own_up[...].T.reshape(8, 16, WIDTH)
        for copy in {1: loads[4:5], 2: loads[5:6], 4: loads[2:4], 5: loads[:2]}.get(k, ()):
            copy.wait()

    def forward_copy(n):
        cols = pl.ds(n * 256, 256)
        return remote(
            out.at[:, cols], r["zin"].at[:, cols], xsend.at[n], xrecv.at[n], (place.s + 1) % 4, place.d
        )

    def send_forward(n):
        @pl.when(place.s < 3)
        def _():
            forward_copy(n).start()

    gather = Gather(place, w, small, sib, gsend, grecv, hsend, hrecv)

    def setup():
        for q in range(8):
            r["pd"][:, q * 128 : (q + 1) * 128] = small[4 * q] + small[4 * q + 1] + small[4 * q + 2] + small[4 * q + 3]
        for q in range(32):
            r["pm"][:, q * 128 : (q + 1) * 128] = small[q]
        r["pq"][:, :WIDTH] = r["pd"][4:5, :]
        r["pq"][:, WIDTH : 2 * WIDTH] = jnp.zeros((1, WIDTH), F32)
        r["pq"][:, 2 * WIDTH :] = r["pd"][5:6, :]
        heads = jnp.concatenate([hscale[...].astype(F32), jnp.zeros((1, 112), F32)], axis=1)
        r["hs"][...] = lax.dot_general(
            jnp.broadcast_to(heads, (8, 128)), head_columns(), (((1,), (0,)), ((), ())),
            precision=lax.Precision.HIGHEST, preferred_element_type=F32,
        )
        row = lax.broadcasted_iota(jnp.int32, (TOK, TOK), 0)
        col = lax.broadcasted_iota(jnp.int32, (TOK, TOK), 1)
        seg_key = jnp.broadcast_to(seg[...].astype(F32), (TOK, TOK))
        ok = (seg_key == seg_key.T) & (col <= row) & (row // 64 == col // 64)
        r["ok"][...] = jnp.where(ok, 1.0, 0.0)

    begins = place.s == 0

    def ready(k):
        work = gather.work
        if k == 0:
            setup()

            @pl.when(begins)
            def _():
                token_load.wait()
                layer.first_norm()
        elif k == 1:
            for c in range(4):
                work.add(lambda c=c: layer.qkv(c, 1), begins)
            for c in range(4):
                work.add(lambda c=c: layer.attention(2 * c, 2), begins)
        elif k == 2:
            work.add(layer.project, begins)
            work.add(layer.middle_norms, begins)
        elif k == 3:
            for c in range(4):
                work.add(lambda c=c: layer.up(c, 1), begins)
            for c in range(2):
                work.add(lambda c=c: layer.inner_norm(4 * c, 4), begins)

    gather.run(own, ready)

    @pl.when(begins)
    def _():
        layer.down(send_forward)

    @pl.when(place.s > 0)
    def _():
        for n in range(4):
            forward_copy(n).wait_recv()
        layer.first_norm()
        layer.qkv()
        layer.attention()
        layer.project()
        layer.middle_norms()
        layer.up()
        layer.inner_norm()
        layer.down(send_forward)

    layer.prepare()
    gather.close()
    pl.semaphore_signal(sib_ok, inc=1, device_id=(place.s, place.sib), device_id_type=MESH)

    @pl.when(place.s < 3)
    def _():
        for n in range(4):
            forward_copy(n).wait_send()

    def backward_copy(i):
        at = pl.ds(i * 32, 32)
        return remote(gz.at[at], r["gin"].at[at], bsend.at[i], brecv.at[i], (place.s + 3) % 4, place.d)

    def send_backward(i):
        @pl.when(place.s > 0)
        def _():
            backward_copy(i).start()

    @pl.when(place.s == 3)
    def _():
        cot_load.wait()

        @each(4)
        def _(i):
            at = rows_of(i, 32)
            row = lax.broadcasted_iota(jnp.int32, (32, WIDTH), 0) + 32 * i
            alive = row % 64 < jnp.where(row < 64, live[0], live[1])
            r["gin"][at, :] = jnp.where(alive, r["gin"][at, :].astype(F32), 0.0).astype(BF16)

    @pl.when(place.s < 3)
    def _():
        for i in range(4):
            backward_copy(i).wait_recv()

    @pl.when(place.s > 0)
    def _():
        layer.back_down(0, 1, 2, 3)
        layer.back_inner()
        layer.back_up()
        layer.back_middle()
        layer.back_project()
        layer.back_attention()
        layer.back_qkv()
        layer.back_first(send_backward)

    def first_section(*phases):
        @pl.when(place.s == 0)
        def _():
            for phase in phases:
                phase()

    scatter = Scatter(place, w, small, sib, ssib, land, sland, back, ssend, srecv, hsend, hrecv)
    n = len(SCATTER)

    def stage(step, k, slices=1):
        if k == AWAY:
            pl.when(place.s > 0)(lambda: step(k))
        elif 0 <= k < n:
            step(k)
            scatter.work.pop(slices)

    def flow(t):
        for late, step in enumerate((scatter.halves, scatter.wholes, scatter.far)):
            for j in (3, 1, 2, 0):
                stage(lambda k, j=j, step=step: step(k, j), t - 1 - late)
        stage(scatter.near, t - 4)
        stage(lambda k: scatter.last(k, total, small_total), t - 5)

    work = scatter.work
    halfs = (slice(0, 512), slice(512, 1024))
    for c in range(2):
        work.add(lambda c=c: layer.back_inner(4 * c, 4), begins)
    for half in halfs:
        work.add(lambda half=half: layer.back_up(half), begins)
    for c in range(8):
        work.add(lambda c=c: layer.grad_up(c))
    work.add(lambda: scatter.to_sibling(1))
    work.add(lambda: scatter.to_sibling(2), tag="up")
    work.add(layer.back_middle, begins)
    work.add(layer.back_project, begins)
    for c in range(4):
        work.add(lambda c=c: layer.back_attention(2 * c, 2), begins)
    for half in halfs:
        work.add(lambda half=half: layer.back_qkv(half), begins)
    work.add(lambda: layer.back_first(send_backward), begins)
    for c in range(8):
        work.add(lambda c=c: layer.grad_in(c))
    for c in range(2):
        work.add(lambda c=c: layer.grad_out(c))
    work.add(lambda: scatter.to_sibling(3))
    work.add(lambda: scatter.to_sibling(5), tag="in")
    work.add(layer.inner_sums)
    work.add(layer.other_sums)
    work.add(lambda: layer.grad_small(small))
    work.add(lambda: scatter.to_sibling(4), tag="small")

    first_section(lambda: layer.back_down(2, 3))
    layer.grad_down(2, 3)
    pl.semaphore_wait(sib_ok, 1)
    scatter.to_sibling(0)
    first_section(lambda: layer.back_down(0, 1))
    layer.grad_down(0, 1)
    scatter.to_sibling(AWAY)
    flow(1)

    @pl.when(begins)
    def _():
        pl.semaphore_wait(lent_ok, 1)
        scatter.lend()

    work.until("up")
    flow(2)
    flow(3)

    @pl.when(place.s == 3)
    def _():
        pl.semaphore_signal(lent_ok, inc=1, device_id=(0, place.d), device_id_type=MESH)

    work.until("in")
    flow(4)
    work.until("small")
    for t in range(5, n + 5):
        flow(t)
    pl.when(place.s == 3)(scatter.aid)

    @pl.when(place.s == 0)
    def _():
        scatter.returned().wait_recv()
        u, count = LENT
        total[u : u + count] = back[...].astype(F32)

    scatter.close()

    @pl.when(place.s > 0)
    def _():
        for i in range(4):
            backward_copy(i).wait_send()


VSPEC = pl.BlockSpec(memory_space=pltpu.VMEM)
ASPEC = pl.BlockSpec(memory_space=pl.ANY)
SSPEC = pl.BlockSpec(memory_space=pltpu.SMEM)
DMA = pltpu.SemaphoreType.DMA


def run_layers(*args):
    g, s = (len(GATHER) + 1, 16), (len(SCATTER) + 1, 12)
    return pl.pallas_call(
        kernel,
        out_shape=[
            jax.ShapeDtypeStruct((TOK, WIDTH), BF16),
            jax.ShapeDtypeStruct((TOK, WIDTH), BF16),
            jax.ShapeDtypeStruct((UNITS, 16, WIDTH), F32),
            jax.ShapeDtypeStruct((16, 128), F32),
        ],
        in_specs=[ASPEC, ASPEC, SSPEC, VSPEC, ASPEC, ASPEC, VSPEC, ASPEC, VSPEC, VSPEC, VSPEC, VSPEC, VSPEC],
        out_specs=[VSPEC] * 4,
        scratch_shapes=[
            pltpu.VMEM((32, UNITS, 16, WIDTH), BF16),
            pltpu.VMEM((32, 16, 128), F32),
            pltpu.VMEM((16, UNITS, 16, WIDTH), BF16),
            pltpu.VMEM((16, 16, 128), F32),
        ]
        + [pltpu.VMEM((SHARE, slots, units, 16, WIDTH), BF16) for slots, units in LANDING]
        + [pltpu.VMEM((slots, 4 * units, 128), F32) for slots, units in LANDING]
        + [pltpu.VMEM((LENT[1], 16, WIDTH), BF16)]
        + [pltpu.VMEM(*v) for v in HELD.values()]
        + [DMA(g[:1]), DMA(g), DMA((8,)), DMA((4,)), DMA((4,)), DMA((4,)), DMA((4,)), DMA(s[:1]), DMA(s), DMA((4,)), DMA((9,))]
        + [pltpu.SemaphoreType.REGULAR] * 2,
        compiler_params=pltpu.CompilerParams(collective_id=1, has_side_effects=True, vmem_limit_bytes=VMEM_LIMIT),
        name="layers",
    )(*args)


def finish_kernel(out, gz, total, small, out2, gz2, g_in, g_out, g_up, g_down, g_gains, g_vecs, g_mgain, g_mbias, g_heads):
    out2[...] = out[...]
    gz2[...] = gz[...]
    g_in[...] = total[IN : IN + 6]
    g_out[...] = total[OUT : OUT + 2]
    for q in range(4):
        g_down[:, :, q * 1024 : (q + 1) * 1024] = total[DOWN + 2 * q : DOWN + 2 * q + 2]
    g_up[...] = total[UP : UP + 8].reshape(128, WIDTH).T
    lane = lax.axis_index("dp") % 4
    thin = jnp.zeros((10, 32), F32)
    for j in range(4):
        thin = jnp.where(lane == j, small[0:10, 32 * j : 32 * (j + 1)], thin)
    for i in range(3):
        g_gains[i] = thin[i : i + 1]
    for i in range(7):
        g_vecs[i] = thin[3 + i : 4 + i]
    g_mgain[...] = small[10:11, :]
    g_mbias[...] = small[11:13, :]
    g_heads[...] = small[13:14, :16]


def finish(*args):
    f = jax.ShapeDtypeStruct
    return pl.pallas_call(
        finish_kernel,
        out_shape=[
            f((TOK, WIDTH), BF16), f((TOK, WIDTH), BF16), f((6, 16, WIDTH), F32), f((2, 16, WIDTH), F32),
            f((WIDTH, 128), F32), f((2, 16, FF), F32), f((3, 1, 32), F32), f((7, 1, 32), F32), f((1, 128), F32),
            f((2, 128), F32), f((1, 16), F32),
        ],
        in_specs=[VSPEC] * 4,
        out_specs=[VSPEC] * 11,
        name="finish",
    )(*args)


def body(
    tokens, cotangent, live_counts, segments, attn_input, attn_output, feed_up, feed_down,
    norm_gains, vector_bias, mid_gain, mid_bias, head_scale,
):
    res = run_layers(
        tokens, cotangent, live_counts, segments[None, :], attn_input[0].T.reshape(6, 16, WIDTH),
        attn_output[0].T.reshape(2, 16, WIDTH), feed_up[0], feed_down[0].T.reshape(2, 16, FF), norm_gains[0],
        vector_bias[0], mid_gain, mid_bias[0], head_scale,
    )
    out, gz, g_in, g_out, g_up, g_down, g_gains, g_vecs, g_mgain, g_mbias, g_heads = finish(*res)
    return (
        out[None],
        gz[None],
        g_in.reshape(96, WIDTH).T[None],
        g_out.reshape(32, WIDTH).T[None],
        g_up[None],
        g_down.reshape(32, FF).T[None],
        g_gains.transpose(1, 0, 2),
        g_vecs.transpose(1, 0, 2),
        g_mgain,
        g_mbias[None],
        g_heads,
    )


def solution(mesh):
    return jax.shard_map(
        body,
        mesh=mesh,
        in_specs=(
            P("dp", None), P("dp", None), P("dp"), P("dp"),
            P("pipe", None, "dp"), P("pipe", None, "dp"), P("pipe", None, "dp"), P("pipe", None, "dp"),
            P("pipe", None, "dp"), P("pipe", None, "dp"), P("pipe", "dp"), P("pipe", None, "dp"), P("pipe", None),
        ),
        out_specs=(
            P("pipe", "dp", None), P("pipe", "dp", None),
            P("pipe", None, "dp"), P("pipe", None, "dp"), P("pipe", None, "dp"), P("pipe", None, "dp"),
            P("pipe", None, "dp"), P("pipe", None, "dp"), P("pipe", "dp"), P("pipe", None, "dp"), P("pipe", None),
        ),
        check_vma=False,
    )
```

```python
import jax
import jax.numpy as jnp
from jax import lax
from jax.experimental import pallas as pl
from jax.experimental.pallas import tpu as pltpu
from jax.sharding import PartitionSpec as P

MESH = pl.DeviceIdType.MESH
EPS = 1e-05
F32, BF16 = jnp.float32, jnp.bfloat16
VMEM_LIMIT = 61840 * 1024

TOK, WIDTH, FF, QKV = 128, 1024, 4096, 3072
IN, OUT, UP, DOWN, UNITS = 0, 6, 8, 16, 24
SMALL = "small"
GATHER = (SMALL, (IN, 6), (OUT, 2), (UP, 8), (DOWN + 4, 4), (DOWN, 4))
SCATTER_STEPS = ((0,), (1,), (2,), (3,), (4, 5), (6,))
SCATTER = ((DOWN + 4, 4), (UP, 4), (UP + 4, 4), (IN, 4), SMALL, (IN + 4, 4), (DOWN, 4))
LENT = (DOWN, 4)
LATE, HELP = 5, 6
AWAY, AID = 6, 7
DESK = (DOWN + 4, 4)
X_OWN, X_GIVE, X_SUMS, X_BACK = 0, 1, 5, 8
BACK_GROUPS = (
    ((1, 0), (2, 0), (3, 0)),
    ((0, 1), (0, 2), (1, 1), (1, 2)),
    ((2, 1), (2, 2), (3, 1), (3, 2)),
    ((0, 3), (1, 3), (2, 3), (3, 3)),
)
SHARE = 3
OFFS = (0, 3, 1, 2)


class Place:
    def __init__(self):
        self.s = lax.axis_index("pipe")
        d = lax.axis_index("dp")
        self.d = d
        self.c = d % 2
        y, z = (d // 2) % 4, d // 8
        self.f = y + self.c * (z - y)
        self.g = z + self.c * (y - z)
        self.sf = 2 + 6 * self.c
        self.sg = 8 - 6 * self.c
        self.sib = d + 1 - 2 * self.c

    def dp(self, of, og):
        return ((self.f + of) % 4) * self.sf + ((self.g + og) % 4) * self.sg + self.c

    def sib_dp(self, of, og):
        return ((self.g + of) % 4) * self.sg + ((self.f + og) % 4) * self.sf + 1 - self.c

    def greet(self):
        sem = pltpu.get_barrier_semaphore()
        near = [self.dp(1, 0), self.dp(3, 0), self.dp(0, 1), self.dp(0, 3), self.sib]
        near = [(self.s, to) for to in near] + [((self.s + by) % 4, self.d) for by in (1, 3)]
        for to in near:
            pl.semaphore_signal(sem, inc=1, device_id=to, device_id_type=MESH)

    def barrier(self):
        pl.semaphore_wait(pltpu.get_barrier_semaphore(), 7)


class Work:
    def __init__(self):
        self.items = []

    def add(self, slice_of_work, when=None, tag=None):
        self.items.append((slice_of_work, when, tag))

    def pop(self, count=1):
        for _ in range(min(count, len(self.items))):
            slice_of_work, when, _ = self.items.pop(0)
            if when is None:
                slice_of_work()
            else:
                pl.when(when)(slice_of_work)

    def until(self, tag):
        while any(tag == item[2] for item in self.items):
            self.pop()

    def drain(self):
        self.pop(len(self.items))


def remote(src, dst, send, recv, s, to):
    return pltpu.make_async_remote_copy(
        src_ref=src, dst_ref=dst, send_sem=send, recv_sem=recv, device_id=(s, to), device_id_type=MESH
    )


def piece_block(whole, small, piece, d, half=None):
    if piece is SMALL:
        return small.at[d] if half is None else small.at[d, pl.ds(8 * half, 8)]
    u, n = piece
    return whole.at[d, pl.ds(u, n)] if half is None else whole.at[d, pl.ds(u + half * (n // 2), n // 2)]


def blocks(whole, small, piece, count, first=0):
    if piece is SMALL:
        return small.at[pl.ds(first, count)]
    return whole.at[pl.ds(first, count), pl.ds(*piece)]


class Gather:
    def __init__(self, place, whole, small, lent, send, recv, xsend, xrecv):
        self.p, self.whole_ref, self.small, self.lent = place, whole, small, lent
        self.send, self.recv, self.xsend, self.xrecv = send, recv, xsend, xrecv
        self.work = Work()

    def ref(self, k, d, half=None):
        if k == HELP:
            u, n = LENT
            at = pl.ds(u, n) if half is None else pl.ds(u + half * (n // 2), n // 2)
            return self.lent.at[d // 2, at]
        return piece_block(self.whole_ref, self.small, GATHER[k], d, half)

    def put(self, k, slot, d, half, to):
        ref = self.ref(k, d, half)
        remote(ref, ref, self.send.at[k], self.recv.at[k, slot], self.p.s, to).start()

    def got(self, k, slot, d):
        ref = self.ref(k, d)
        remote(ref, ref, self.send.at[k], self.recv.at[k, slot], self.p.s, self.p.sib).wait_recv()

    def hand(self, k, j, i):
        p = self.p
        d = p.dp(OFFS[j], OFFS[i])
        if k != HELP:
            self.put(k, 15, d, None, p.sib)
        elif (j, i) != (0, 0):
            self.give(j, i).start()

    def give(self, j, i):
        p = self.p
        d = p.dp(OFFS[j], OFFS[i])
        group = next(g for g, group in enumerate(BACK_GROUPS) if (j, i) in group)
        return remote(
            self.ref(HELP, d), self.ref(LATE, d), self.xsend.at[1], self.xrecv.at[X_GIVE + group], (p.s + 1) % 4, p.d
        )

    def lend(self):
        p = self.p
        return remote(
            self.ref(LATE, p.d), self.ref(HELP, p.d), self.xsend.at[0], self.xrecv.at[X_OWN], (p.s + 3) % 4, p.d
        )

    def spread(self, k, j):
        p = self.p
        d = p.dp(OFFS[j], 0)
        self.put(k, 3 + 3 * j, d, None, p.dp(0, 1))
        self.put(k, 4 + 3 * j, d, None, p.dp(0, 3))
        self.hand(k, j, 0)

    def first(self, k):
        p = self.p
        self.put(k, 0, p.d, None, p.dp(1, 0))
        self.put(k, 1, p.d, None, p.dp(3, 0))
        self.spread(k, 0)

    def ring(self, k):
        p = self.p
        left, right = p.dp(3, 0), p.dp(1, 0)
        self.got(k, 0, left)
        self.put(k, 2, left, 0, right)
        self.spread(k, 1)
        self.got(k, 1, right)
        self.put(k, 2, right, 1, left)
        self.spread(k, 2)

    def far(self, k):
        self.got(k, 2, self.p.dp(2, 0))
        self.spread(k, 3)

    def second(self, k, j):
        p = self.p
        low, high = p.dp(OFFS[j], 3), p.dp(OFFS[j], 1)
        self.got(k, 3 + 3 * j, low)
        self.put(k, 5 + 3 * j, low, 0, p.dp(0, 1))
        self.hand(k, j, 1)
        self.got(k, 4 + 3 * j, high)
        self.put(k, 5 + 3 * j, high, 1, p.dp(0, 3))
        self.hand(k, j, 2)

    def last(self, k, j):
        self.got(k, 5 + 3 * j, self.p.dp(OFFS[j], 2))
        self.hand(k, j, 3)

    def relay(self, group):
        p = self.p
        ref = self.many(LATE, len(BACK_GROUPS[group]))
        remote(ref, ref, self.xsend.at[1], self.xrecv.at[X_GIVE + group], p.s, p.sib).wait_recv()
        for j, i in BACK_GROUPS[group]:
            self.hand(LATE, j, i)

    def many(self, k, count):
        if k == HELP:
            return blocks(self.lent, None, LENT, count)
        return blocks(self.whole_ref, self.small, GATHER[k], count)

    def whole(self, k):
        ref = self.many(k, 16)
        remote(ref, ref, self.send.at[k], self.recv.at[k, 15], self.p.s, self.p.sib).wait_recv()

    def close(self):
        p = self.p

        def sent(k, count):
            ref = self.many(k, count)
            remote(ref, ref, self.send.at[k], self.recv.at[k, 15], p.s, p.sib).wait_send()

        for k in range(len(GATHER)):
            if k != LATE:
                sent(k, 31)

        @pl.when(p.s > 0)
        def _():
            sent(LATE, 31)

        @pl.when(p.s == 0)
        def _():
            sent(LATE, 16)
            self.lend().wait_send()

        @pl.when(p.s == 3)
        def _():
            sent(HELP, 15)
            ref = self.many(HELP, 15)
            remote(ref, ref, self.xsend.at[1], self.xrecv.at[X_GIVE], p.s, p.sib).wait_send()

    def run(self, own, ready):
        n, begun = len(GATHER), 0
        s = self.p.s

        def stage(step, k):
            if k == LATE:
                pl.when(s > 0)(lambda: step(k))
            elif 0 <= k < n:
                step(k)

        own(LATE)

        @pl.when(s == 0)
        def _():
            self.lend().start()
            self.hand(LATE, 0, 0)

        @pl.when(s == 3)
        def _():
            self.lend().wait_recv()
            for step in (self.first, self.ring, self.far):
                step(HELP)
            for j in range(4):
                self.second(HELP, j)
            for j in range(4):
                self.last(HELP, j)

        for t in range(n + 3):
            while begun < min(n, t + 3):
                if begun != LATE:
                    own(begun)
                stage(self.first, begun)
                begun += 1
            stage(self.ring, t)
            self.work.pop()
            stage(self.far, t - 1)
            self.work.pop()
            for j in range(4):
                stage(lambda k, j=j: self.second(k, j), t - 2)
                self.work.pop()
            for j in range(4):
                stage(lambda k, j=j: self.last(k, j), t - 3)
                self.work.pop()
            if 4 <= t < 8:
                pl.when(s == 0)(lambda t=t: self.relay(t - 4))

            self.work.pop()
            if t >= 3:
                self.whole(t - 3)
                ready(t - 3)
        self.work.drain()


def dot(a, b, ca, cb):
    return lax.dot_general(a, b, (((ca,), (cb,)), ((), ())), preferred_element_type=F32)


def centered(x):
    c = x - jnp.mean(x, axis=-1, keepdims=True)
    r = lax.rsqrt(jnp.mean(c * c, axis=-1, keepdims=True) + EPS)
    return c, r


def norm(x, gain, bias):
    c, r = centered(x)
    return c * r * gain + bias


def norm_back(x, gain, gy):
    c, r = centered(x)
    hat = c * r
    gh = gy * gain
    gx = r * (gh - jnp.mean(gh, axis=-1, keepdims=True) - hat * jnp.mean(gh * hat, axis=-1, keepdims=True))
    return gx, gy * hat


def rows_of(i, n):
    return pl.ds(pl.multiple_of(i * n, n), n)


def col_sum(x):
    return jnp.sum(x, axis=0, keepdims=True)


def row_sum(x):
    return dot(jnp.full((16, x.shape[0]), 1.0, BF16), x, 1, 0)[:1]


K0, K1 = 0.7978845608028654, 0.044715


def gelu(x):
    return 0.5 * x * (1.0 + jnp.tanh(K0 * (x + K1 * x * x * x)))


def gelu_both(x):
    t = jnp.tanh(K0 * (x + K1 * x * x * x))
    u = 0.5 * x * (1.0 + t)
    du = 0.5 * (1.0 + t) + 0.5 * x * (1.0 - t * t) * K0 * (1.0 + 3.0 * K1 * x * x)
    return u, du


def head_masks():
    lane = lax.broadcasted_iota(jnp.int32, (1, 128), 1)
    even = jnp.where(lane < 64, 1.0, 0.0)
    return even.astype(BF16), (1.0 - even).astype(BF16)


def two_rows(x, even, odd):
    return jnp.concatenate([x * even, x * odd], axis=0)


def each(count, unroll=1):
    def run(body):
        def step(i, carry):
            body(i)
            return carry

        lax.fori_loop(0, count, step, 0, unroll=unroll)

    return run


def stack(w, d0, nd, u, nu, cols=slice(0, WIDTH)):
    return w[pl.ds(d0, nd), u : u + nu, :, cols].reshape(nd * nu * 16, cols.stop - cols.start)


def head_columns():
    col = lax.broadcasted_iota(jnp.int32, (128, WIDTH), 1)
    head = lax.broadcasted_iota(jnp.int32, (128, WIDTH), 0)
    return jnp.where(col // 64 == head, 1.0, 0.0)


class Layer:
    def __init__(self, w, r):
        self.w, self.r = w, r


    def first_norm(self):
        r, pd = self.r, self.r["pd"]

        @each(4, 2)
        def _(i):
            at = rows_of(i, 32)
            r["a1"][at, :] = norm(r["zin"][at, :].astype(F32), pd[0:1, :], pd[3:4, :]).astype(BF16)

    def qkv(self, first=0, count=4):
        r = self.r
        for c in range(first, first + count):
            at = slice(c * 768, (c + 1) * 768)
            acc = dot(r["a1"][...], stack(self.w, 8 * c, 8, IN, 6), 1, 1) + r["pq"][0:1, at]
            r["qkv"][:, at] = acc.astype(BF16)

    def attention(self, first=0, count=8):
        r, qkv = self.r, self.r["qkv"]
        even, odd = head_masks()

        @each(count, min(count, 4))
        def _(p):
            p = p + first
            cols = rows_of(p, 128)
            q = qkv[:, cols]
            k = qkv[:, pl.ds(pl.multiple_of(WIDTH + p * 128, 128), 128)]
            v = qkv[:, pl.ds(pl.multiple_of(2 * WIDTH + p * 128, 128), 128)]
            ok = r["ok"][...]
            sc = dot(two_rows(q, even, odd), k, 1, 1) * 0.125
            sc = jnp.where(jnp.concatenate([ok, ok], axis=0) > 0.5, sc, -1000000000.0)
            e = jnp.exp(sc - jnp.max(sc, axis=-1, keepdims=True))
            pr = e / jnp.sum(e, axis=-1, keepdims=True)
            r["p"][rows_of(p, 256), :] = pr
            pb = pr.astype(BF16)
            both = jnp.concatenate([pb[:TOK], pb[TOK:]], axis=1)
            mixed = dot(both, two_rows(v, even, odd), 1, 0)
            r["mixed"][:, cols] = mixed
            r["scaled"][:, cols] = (mixed * r["hs"][0:1, cols]).astype(BF16)

    def project(self):
        r = self.r
        r["attn"][...] = dot(r["scaled"][...], stack(self.w, 0, 32, OUT, 2), 1, 1) + r["pd"][6:7, :]

    def middle_norms(self):
        r, pd = self.r, self.r["pd"]

        @each(4, 2)
        def _(i):
            at = rows_of(i, 32)
            z2 = r["zin"][at, :].astype(F32) + norm(r["attn"][at, :], pd[1:2, :], pd[7:8, :])
            r["z2"][at, :] = z2
            r["a2"][at, :] = norm(z2, pd[2:3, :], pd[8:9, :]).astype(BF16)

    def up(self, first=0, count=4):
        r = self.r

        @each(count)
        def _(c):
            c = c + first
            cols = rows_of(c, 1024)
            r["ff"][:, cols] = dot(r["a2"][...], stack(self.w, 8 * c, 8, UP, 8), 1, 1) + r["pm"][11:12, cols]

    def inner_norm(self, first=0, count=8):
        r, pm = self.r, self.r["pm"]

        @each(count, 2)
        def _(i):
            i = i + first
            at = rows_of(i, 16)
            r["mid"][at, :] = norm(gelu(r["ff"][at, :]), pm[10:11, :], pm[12:13, :]).astype(BF16)

    def down(self, send_out):
        r = self.r
        for n in range(4):
            cols = slice(n * 256, (n + 1) * 256)
            acc = r["z2"][:, cols] + r["pd"][9:10, cols]
            for q in range(4):
                w = stack(self.w, 8 * n, 8, DOWN + 2 * q, 2)
                acc = acc + dot(r["mid"][:, q * 1024 : (q + 1) * 1024], w, 1, 1)
            r["out"][:, cols] = acc.astype(BF16)
            send_out(n)

    def prepare(self):
        r = self.r

        @each(8, 2)
        def _(i):
            at = rows_of(i, 16)
            u, du = gelu_both(r["ff"][at, :])
            c, s = centered(u)
            r["hat"][at, :] = (c * s).astype(BF16)
            r["slope"][at, :] = (du * s).astype(BF16)

        for name in ("gd", "gm"):
            r[name][...] = jnp.zeros_like(r[name])


    def back_down(self, *chunks):
        r = self.r
        for q in chunks:
            w = stack(self.w, 0, 32, DOWN + 2 * q, 2)
            r["ff"][:, q * 1024 : (q + 1) * 1024] = dot(r["gin"][...], w, 1, 0)

    def back_inner(self, first=0, count=8):
        r, pm = self.r, self.r["pm"]

        @each(count, 2)
        def _(i):
            i = i + first
            at = rows_of(i, 16)
            gh = r["ff"][at, :] * pm[10:11, :]
            hat = r["hat"][at, :].astype(F32)
            m1 = jnp.mean(gh, axis=-1, keepdims=True)
            m2 = jnp.mean(gh * hat, axis=-1, keepdims=True)
            r["ghid"][at, :] = ((gh - m1 - hat * m2) * r["slope"][at, :].astype(F32)).astype(BF16)

    def back_up(self, cols=slice(0, WIDTH)):
        r = self.r
        r["tw"][:, cols] = dot(r["ghid"][...], stack(self.w, 0, 32, UP, 8, cols), 1, 0)

    def back_middle(self):
        r, gd, pd = self.r, self.r["gd"], self.r["pd"]

        @each(4, 2)
        def _(i):
            at = rows_of(i, 32)
            ga2 = r["tw"][at, :]
            gz, gg = norm_back(r["z2"][at, :], pd[2:3, :], ga2)
            gd[2:3, :] += col_sum(gg)
            gd[8:9, :] += col_sum(ga2)
            gz = gz + r["gin"][at, :].astype(F32)
            r["gz2"][at, :] = gz
            gat, gg = norm_back(r["attn"][at, :], pd[1:2, :], gz)
            gd[1:2, :] += col_sum(gg)
            gd[7:8, :] += col_sum(gz)
            r["gattn"][at, :] = gat.astype(BF16)

    def back_project(self):
        r = self.r
        r["tw"][...] = dot(r["gattn"][...], stack(self.w, 0, 32, OUT, 2), 1, 0)

    def back_attention(self, first=0, count=8):
        r = self.r
        even, odd = head_masks()

        @each(count, min(count, 4))
        def _(p):
            p = p + first
            cols = rows_of(p, 128)
            kcols = pl.ds(pl.multiple_of(WIDTH + p * 128, 128), 128)
            vcols = pl.ds(pl.multiple_of(2 * WIDTH + p * 128, 128), 128)
            gs = r["tw"][:, cols]
            r["gh"][0:1, cols] = col_sum(gs * r["mixed"][:, cols])
            gmx = (gs * r["hs"][0:1, cols]).astype(BF16)
            q, k, v = r["qkv"][:, cols], r["qkv"][:, kcols], r["qkv"][:, vcols]
            gmx2 = two_rows(gmx, even, odd)
            gp = dot(gmx2, v, 1, 1)
            pr = r["p"][rows_of(p, 256), :]
            gsc = (pr * (gp - jnp.sum(pr * gp, axis=-1, keepdims=True))).astype(BF16)
            both = jnp.concatenate([gsc[:TOK], gsc[TOK:]], axis=1)
            r["gqkv"][:, cols] = (dot(both, two_rows(k, even, odd), 1, 0) * 0.125).astype(BF16)
            r["gqkv"][:, kcols] = (dot(gsc, two_rows(q, even, odd), 0, 0) * 0.125).astype(BF16)
            r["gqkv"][:, vcols] = dot(pr.astype(BF16), gmx2, 0, 0).astype(BF16)

    def back_qkv(self, cols=slice(0, WIDTH)):
        r = self.r
        r["tw"][:, cols] = dot(r["gqkv"][...], stack(self.w, 0, 32, IN, 6, cols), 1, 0)

    def back_first(self, send_out):
        r, gd, pd = self.r, self.r["gd"], self.r["pd"]
        for i in range(4):
            at = slice(i * 32, (i + 1) * 32)
            ga1 = r["tw"][at, :]
            gz, gg = norm_back(r["zin"][at, :].astype(F32), pd[0:1, :], ga1)
            r["gz"][at, :] = (gz + r["gz2"][at, :]).astype(BF16)
            send_out(i)
            gd[0:1, :] += col_sum(gg)
            gd[3:4, :] += col_sum(ga1)

    def inner_sums(self):
        r, gm = self.r, self.r["gm"]

        @each(8)
        def _(i):
            at = rows_of(i, 16)
            g = r["ff"][at, :]
            gm[10:11, :] += col_sum(g * r["hat"][at, :].astype(F32))
            gm[12:13, :] += col_sum(g)

        gm[11:12, :] = row_sum(r["ghid"][...])

    def other_sums(self):
        r, gd = self.r, self.r["gd"]
        gd[9:10, :] = row_sum(r["gin"][...])
        gd[6:7, :] = row_sum(r["gattn"][...])
        gd[4:5, :] = row_sum(r["gqkv"][:, :WIDTH])
        gd[5:6, :] = row_sum(r["gqkv"][:, 2 * WIDTH :])


    def grad_down(self, *chunks):
        r = self.r

        @each(4)
        def _(c):
            gt = r["gin"][:, rows_of(c, 256)].T
            for q in chunks:
                g = dot(gt, r["mid"][:, q * 1024 : (q + 1) * 1024], 1, 0).astype(BF16)
                self.w[pl.ds(8 * c, 8), DOWN + 2 * q : DOWN + 2 * q + 2] = g.reshape(8, 2, 16, WIDTH)

    def grad_up(self, c):
        r = self.r
        g = dot(r["ghid"][:, c * 512 : (c + 1) * 512].T, r["a2"][...], 1, 0).astype(BF16)
        self.w[pl.ds(4 * c, 4), UP : UP + 8] = g.reshape(4, 8, 16, WIDTH)

    def grad_in(self, c):
        r = self.r
        g = dot(r["gqkv"][:, c * 384 : (c + 1) * 384].T, r["a1"][...], 1, 0).astype(BF16)
        self.w[pl.ds(4 * c, 4), IN : IN + 6] = g.reshape(4, 6, 16, WIDTH)

    def grad_out(self, c):
        r = self.r
        g = dot(r["gattn"][:, c * 512 : (c + 1) * 512].T, r["scaled"][...], 1, 0).astype(BF16)
        self.w[pl.ds(16 * c, 16), OUT : OUT + 2] = g.reshape(16, 2, 16, WIDTH)

    def grad_small(self, small):
        r = self.r
        hsum = lax.dot_general(
            jnp.broadcast_to(r["gh"][0:1, :], (8, WIDTH)), head_columns(), (((1,), (1,)), ((), ())),
            precision=lax.Precision.HIGHEST, preferred_element_type=F32,
        )
        is13 = lax.broadcasted_iota(jnp.int32, (16, 128), 0) == 13
        heads = jnp.where(is13, jnp.concatenate([hsum, hsum], axis=0), 0.0)
        for d in range(32):
            a, b = (d // 4) * 128, d * 128
            small[d] = r["gd"][:, a : a + 128] + r["gm"][:, b : b + 128] + heads


class Scatter:
    def __init__(self, place, grads, small, sib, ssib, land, sland, back, send, recv, xsend, xrecv):
        self.p, self.grads, self.small = place, grads, small
        self.sib, self.ssib, self.land, self.sland, self.back = sib, ssib, land, sland, back
        self.send, self.recv, self.xsend, self.xrecv = send, recv, xsend, xrecv
        self.work = Work()

    def copy(self, k, slot, src, dst, to):
        return remote(src, dst, self.send.at[k], self.recv.at[k, slot], self.p.s, to)

    def go(self, k, slot, src, dst, to):
        self.copy(k, slot, src, dst, to).start()

    def got(self, k, slot, dst):
        self.copy(k, slot, dst, dst, self.p.sib).wait_recv()

    def block(self, k, of, og, half=None):
        d = self.p.dp(of, og)
        if k == AID:
            return piece_block(self.sib, None, DESK, d // 2, half)
        return piece_block(self.grads, self.small, SCATTER[k], d, half)

    def from_sib(self, k, slot, half=None):
        return piece_block(self.sib, self.ssib, SCATTER[k], slot, half)

    def landing(self, k, kind, slot):
        if k != AID and SCATTER[k] is SMALL:
            return self.sland[kind].at[slot]
        step = next((t for t, ks in enumerate(SCATTER_STEPS) if k in ks), len(SCATTER_STEPS))
        return self.land[kind].at[step % SHARE, slot]

    def landed(self, k, slot, kind, j=0):
        self.got(k, slot, self.landing(k, kind, pl.ds(2 * j, 2)))

    def to_sibling(self, k):
        p = self.p
        for i in (3, 1, 2, 0):
            for j in (3, 1, 2, 0):
                src = piece_block(self.grads, self.small, SCATTER[k], p.sib_dp(OFFS[j], OFFS[i]))
                self.go(k, 0 if i == 3 else 1, src, self.from_sib(k, i * 4 + j), p.sib)

    def lent_sum(self, i, j):
        p = self.p
        return remote(
            self.block(AWAY, OFFS[j], OFFS[i]), self.block(AID, OFFS[j], OFFS[i]), self.xsend.at[2],
            self.xrecv.at[X_SUMS + (2, 1, 1, 0)[i]], (p.s + 3) % 4, p.d,
        )

    def lend(self):
        for i in (3, 1, 2, 0):
            if i in (3, 1):
                self.arrived(AWAY, i == 3)
            for j in (3, 1, 2, 0):
                self.add(AWAY, self.block(AWAY, OFFS[j], OFFS[i]), [self.from_sib(AWAY, i * 4 + j)])
                self.lent_sum(i, j).start()

    def returned(self):
        p = self.p
        return remote(
            self.block(AID, 0, 0), self.back, self.xsend.at[3], self.xrecv.at[X_BACK], (p.s + 1) % 4, p.d
        )

    def arrived(self, k, far):
        first, count = (12, 4) if far else (0, 12)
        self.got(k, 0 if far else 1, blocks(self.sib, self.ssib, SCATTER[k], count, first))

    def lent_arrived(self, group):
        ref = blocks(self.sib, None, DESK, (4, 8, 4)[group])
        remote(ref, ref, self.xsend.at[2], self.xrecv.at[X_SUMS + group], self.p.s, self.p.sib).wait_recv()

    def add(self, k, dst, srcs, store=None):
        out = dst if store is None else store
        if store is None and not srcs:
            return
        if k != AID and SCATTER[k] is SMALL:
            out[...] = dst[...] + sum(src[...] for src in srcs)
            return
        for u in range(dst.shape[0]):
            acc = dst[u].astype(F32)
            for src in srcs:
                acc = acc + src[u].astype(F32)
            out[u] = acc.astype(out.dtype)

    def halves(self, k, j):
        p = self.p
        srcs = []
        if k == AID:
            if j == 3:
                self.lent_arrived(0)
        else:
            if j == 3:
                self.arrived(k, True)
            srcs = [self.from_sib(k, 12 + j)]
        self.add(k, self.block(k, OFFS[j], 2), srcs)
        for side, to in enumerate((p.dp(0, 1), p.dp(0, 3))):
            self.go(k, 2 + j, self.block(k, OFFS[j], 2, side), self.landing(k, 0, 2 * j + side), to)

    def wholes(self, k, j):
        p = self.p
        if j == 3:
            if k == AID:
                self.lent_arrived(1)
            else:
                self.arrived(k, False)
        self.landed(k, 2 + j, 0, j)
        for i, near, side in ((2, 1, 0), (1, 3, 1)):
            for half in range(2):
                srcs = [] if k == AID else [self.from_sib(k, i * 4 + j, half)]
                if half == side:
                    srcs.append(self.landing(k, 0, 2 * j + side))
                self.add(k, self.block(k, OFFS[j], near, half), srcs)
        for near, side in ((1, 0), (3, 1)):
            self.go(k, 6 + j, self.block(k, OFFS[j], near), self.landing(k, 1, 2 * j + side), p.dp(0, near))

    def far(self, k, j):
        p = self.p
        srcs = []
        if k != AID:
            srcs.append(self.from_sib(k, j))
        elif j == 3:
            self.lent_arrived(2)
        self.landed(k, 6 + j, 1, j)
        srcs += [self.landing(k, 1, 2 * j + side) for side in range(2)]
        self.add(k, self.block(k, OFFS[j], 0), srcs)
        if j == 3:
            self.go(k, 10, self.block(k, 2, 0, 0), self.landing(k, 2, 0), p.dp(1, 0))
            self.go(k, 10, self.block(k, 2, 0, 1), self.landing(k, 2, 1), p.dp(3, 0))

    def near(self, k):
        p = self.p
        self.landed(k, 10, 2)
        for near, side in ((1, 0), (3, 1)):
            self.add(k, self.block(k, near, 0, side), [self.landing(k, 2, side)])
        for near, side in ((1, 0), (3, 1)):
            self.go(k, 11, self.block(k, near, 0), self.landing(k, 3, side), p.dp(near, 0))

    def last(self, k, total, small_total):
        self.landed(k, 11, 3)
        srcs = [self.landing(k, 3, side) for side in range(2)]
        if k == AID:
            self.add(k, self.block(k, 0, 0), srcs)
            self.returned().start()
        elif SCATTER[k] is SMALL:
            self.add(k, self.block(k, 0, 0), srcs, store=small_total)
        else:
            u, n = SCATTER[k]
            self.add(k, self.block(k, 0, 0), srcs, store=total.at[pl.ds(u, n)])

    def aid(self):
        for step in (self.halves, self.wholes, self.far):
            for j in (3, 1, 2, 0):
                step(AID, j)
        self.near(AID)
        self.last(AID, None, None)

    def close(self):
        p = self.p

        def sent(k, count):
            if k == AID:
                ref = blocks(self.sib, None, DESK, count)
            else:
                ref = blocks(self.grads, self.small, SCATTER[k], count)
            self.copy(k, 0, ref, ref, p.sib).wait_send()

        for k in range(len(SCATTER)):
            if k != AWAY:
                sent(k, 31)

        @pl.when(p.s > 0)
        def _():
            sent(AWAY, 31)

        @pl.when(p.s == 0)
        def _():
            sent(AWAY, 16)
            ref = blocks(self.grads, None, LENT, 16)
            remote(ref, ref, self.xsend.at[2], self.xrecv.at[X_SUMS], p.s, p.sib).wait_send()

        @pl.when(p.s == 3)
        def _():
            sent(AID, 15)
            self.returned().wait_send()


HELD = dict(
    pd=((16, WIDTH), F32), pm=((16, FF), F32), pq=((1, QKV), F32), hs=((8, WIDTH), F32), ok=((TOK, TOK), F32),
    zin=((TOK, WIDTH), BF16), a1=((TOK, WIDTH), BF16), qkv=((TOK, QKV), BF16), p=((8 * 256, TOK), F32),
    mixed=((TOK, WIDTH), F32), scaled=((TOK, WIDTH), BF16), attn=((TOK, WIDTH), F32), z2=((TOK, WIDTH), F32),
    a2=((TOK, WIDTH), BF16), ff=((TOK, FF), F32), hat=((TOK, FF), BF16), slope=((TOK, FF), BF16), mid=((TOK, FF), BF16),
    gin=((TOK, WIDTH), BF16), ghid=((TOK, FF), BF16), gattn=((TOK, WIDTH), BF16), gqkv=((TOK, QKV), BF16),
    tw=((TOK, WIDTH), F32), gz2=((TOK, WIDTH), F32), gd=((16, WIDTH), F32), gm=((16, FF), F32), gh=((8, WIDTH), F32),
)
LANDING = ((8, 2), (8, 4), (2, 2), (2, 4))


def kernel(*refs):
    (tok, cot, live, seg, own_in, own_out, own_up, own_down, gains, vecs, mgain, mbias, hscale), refs = refs[:13], refs[13:]
    (out, gz, total, small_total), refs = refs[:4], refs[4:]
    (w, small, sib, ssib), refs = refs[:4], refs[4:]
    land, sland, refs = refs[:4], refs[4:8], refs[8:]
    back, refs = refs[0], refs[1:]
    r = dict(zip(HELD, refs), out=out, gz=gz)
    gsend, grecv, own_sem, xsend, xrecv, bsend, brecv, ssend, srecv, hsend, hrecv, sib_ok, lent_ok = refs[len(HELD) :]
    place = Place()
    layer = Layer(w, r)
    place.greet()

    loads = [
        pltpu.make_async_copy(
            own_down.at[:, :, pl.ds(q * 1024, 1024)], w.at[place.d, pl.ds(DOWN + 2 * q, 2)], own_sem.at[q]
        )
        for q in range(4)
    ] + [
        pltpu.make_async_copy(own_in, w.at[place.d, pl.ds(IN, 6)], own_sem.at[4]),
        pltpu.make_async_copy(own_out, w.at[place.d, pl.ds(OUT, 2)], own_sem.at[5]),
    ]
    for copy in loads:
        copy.start()
    token_load = pltpu.make_async_copy(tok, r["zin"], own_sem.at[6])
    cot_load = pltpu.make_async_copy(cot, r["gin"], own_sem.at[7])

    @pl.when(place.s == 0)
    def _():
        token_load.start()

    @pl.when(place.s == 3)
    def _():
        cot_load.start()

    mine = lax.broadcasted_iota(jnp.int32, (1, 128), 1) // 32 == place.d % 4

    def spot(x):
        x = x.astype(F32)
        return jnp.where(mine, jnp.concatenate([x, x, x, x], axis=1), 0.0)

    small[place.d, 0:3] = spot(gains[...])
    small[place.d, 3:10] = spot(vecs[...])
    small[place.d, 10:11] = mgain[...].astype(F32)
    small[place.d, 11:13] = mbias[...].astype(F32)
    small[place.d, 13:16] = jnp.zeros((3, 128), F32)
    place.barrier()

    def own(k):
        if k == 3:
            w[place.d, UP : UP + 8] = own_up[...].T.reshape(8, 16, WIDTH)
        for copy in {1: loads[4:5], 2: loads[5:6], 4: loads[2:4], 5: loads[:2]}.get(k, ()):
            copy.wait()

    def forward_copy(n):
        cols = pl.ds(n * 256, 256)
        return remote(
            out.at[:, cols], r["zin"].at[:, cols], xsend.at[n], xrecv.at[n], (place.s + 1) % 4, place.d
        )

    def send_forward(n):
        @pl.when(place.s < 3)
        def _():
            forward_copy(n).start()

    gather = Gather(place, w, small, sib, gsend, grecv, hsend, hrecv)

    def setup():
        for q in range(8):
            r["pd"][:, q * 128 : (q + 1) * 128] = small[4 * q] + small[4 * q + 1] + small[4 * q + 2] + small[4 * q + 3]
        for q in range(32):
            r["pm"][:, q * 128 : (q + 1) * 128] = small[q]
        r["pq"][:, :WIDTH] = r["pd"][4:5, :]
        r["pq"][:, WIDTH : 2 * WIDTH] = jnp.zeros((1, WIDTH), F32)
        r["pq"][:, 2 * WIDTH :] = r["pd"][5:6, :]
        heads = jnp.concatenate([hscale[...].astype(F32), jnp.zeros((1, 112), F32)], axis=1)
        r["hs"][...] = lax.dot_general(
            jnp.broadcast_to(heads, (8, 128)), head_columns(), (((1,), (0,)), ((), ())),
            precision=lax.Precision.HIGHEST, preferred_element_type=F32,
        )
        row = lax.broadcasted_iota(jnp.int32, (TOK, TOK), 0)
        col = lax.broadcasted_iota(jnp.int32, (TOK, TOK), 1)
        seg_key = jnp.broadcast_to(seg[...].astype(F32), (TOK, TOK))
        ok = (seg_key == seg_key.T) & (col <= row) & (row // 64 == col // 64)
        r["ok"][...] = jnp.where(ok, 1.0, 0.0)

    begins = place.s == 0

    def ready(k):
        work = gather.work
        if k == 0:
            setup()

            @pl.when(begins)
            def _():
                token_load.wait()
                layer.first_norm()
        elif k == 1:
            for c in range(4):
                work.add(lambda c=c: layer.qkv(c, 1), begins)
            for c in range(4):
                work.add(lambda c=c: layer.attention(2 * c, 2), begins)
        elif k == 2:
            work.add(layer.project, begins)
            work.add(layer.middle_norms, begins)
        elif k == 3:
            for c in range(4):
                work.add(lambda c=c: layer.up(c, 1), begins)
            for c in range(2):
                work.add(lambda c=c: layer.inner_norm(4 * c, 4), begins)

    gather.run(own, ready)

    @pl.when(begins)
    def _():
        layer.down(send_forward)

    @pl.when(place.s == 3)
    def _():
        cot_load.wait()

        @each(4)
        def _(i):
            at = rows_of(i, 32)
            row = lax.broadcasted_iota(jnp.int32, (32, WIDTH), 0) + 32 * i
            alive = row % 64 < jnp.where(row < 64, live[0], live[1])
            r["gin"][at, :] = jnp.where(alive, r["gin"][at, :].astype(F32), 0.0).astype(BF16)

    @pl.when(place.s > 0)
    def _():
        for n in range(4):
            forward_copy(n).wait_recv()
        layer.first_norm()
        layer.qkv()
        layer.attention()
        layer.project()
        layer.middle_norms()
        layer.up()
        layer.inner_norm()
        layer.down(send_forward)

    layer.prepare()
    gather.close()
    pl.semaphore_signal(sib_ok, inc=1, device_id=(place.s, place.sib), device_id_type=MESH)

    @pl.when(place.s < 3)
    def _():
        for n in range(4):
            forward_copy(n).wait_send()

    def backward_copy(i):
        at = pl.ds(i * 32, 32)
        return remote(gz.at[at], r["gin"].at[at], bsend.at[i], brecv.at[i], (place.s + 3) % 4, place.d)

    def send_backward(i):
        @pl.when(place.s > 0)
        def _():
            backward_copy(i).start()

    @pl.when(place.s < 3)
    def _():
        for i in range(4):
            backward_copy(i).wait_recv()

    @pl.when(place.s > 0)
    def _():
        layer.back_down(0, 1, 2, 3)
        layer.back_inner()
        layer.back_up()
        layer.back_middle()
        layer.back_project()
        layer.back_attention()
        layer.back_qkv()
        layer.back_first(send_backward)

    def first_section(*phases):
        @pl.when(place.s == 0)
        def _():
            for phase in phases:
                phase()

    scatter = Scatter(place, w, small, sib, ssib, land, sland, back, ssend, srecv, hsend, hrecv)
    n = len(SCATTER_STEPS)

    def stage(step, t):
        for k in SCATTER_STEPS[t] if 0 <= t < n else ():
            if k == AWAY:
                pl.when(place.s > 0)(lambda k=k: step(k))
            else:
                step(k)
        scatter.work.pop()

    def flow(t):
        for late, step in enumerate((scatter.halves, scatter.wholes, scatter.far)):
            for j in (3, 1, 2, 0):
                stage(lambda k, j=j, step=step: step(k, j), t - 1 - late)
        stage(scatter.near, t - 4)
        stage(lambda k: scatter.last(k, total, small_total), t - 5)

    work = scatter.work
    halfs = (slice(0, 512), slice(512, 1024))
    for c in range(2):
        work.add(lambda c=c: layer.back_inner(4 * c, 4), begins)
    for half in halfs:
        work.add(lambda half=half: layer.back_up(half), begins)
    for c in range(8):
        work.add(lambda c=c: layer.grad_up(c))
    work.add(lambda: scatter.to_sibling(1))
    work.add(lambda: scatter.to_sibling(2), tag="up")
    work.add(layer.back_middle, begins)
    work.add(layer.back_project, begins)
    for c in range(4):
        work.add(lambda c=c: layer.back_attention(2 * c, 2), begins)
    for half in halfs:
        work.add(lambda half=half: layer.back_qkv(half), begins)
    work.add(lambda: layer.back_first(send_backward), begins)
    for c in range(8):
        work.add(lambda c=c: layer.grad_in(c))
    for c in range(2):
        work.add(lambda c=c: layer.grad_out(c))
    work.add(lambda: scatter.to_sibling(3))
    work.add(lambda: scatter.to_sibling(5), tag="in")
    work.add(layer.inner_sums)
    work.add(layer.other_sums)
    work.add(lambda: layer.grad_small(small))
    work.add(lambda: scatter.to_sibling(4), tag="small")

    first_section(lambda: layer.back_down(2, 3))
    layer.grad_down(2, 3)
    pl.semaphore_wait(sib_ok, 1)
    scatter.to_sibling(0)
    first_section(lambda: layer.back_down(0, 1))
    layer.grad_down(0, 1)
    scatter.to_sibling(AWAY)
    flow(1)

    @pl.when(begins)
    def _():
        pl.semaphore_wait(lent_ok, 1)
        scatter.lend()

    work.until("up")
    flow(2)
    flow(3)

    @pl.when(place.s == 3)
    def _():
        pl.semaphore_signal(lent_ok, inc=1, device_id=(0, place.d), device_id_type=MESH)

    work.until("in")
    flow(4)
    work.until("small")
    for t in range(5, n + 5):
        flow(t)
    pl.when(place.s == 3)(scatter.aid)

    @pl.when(place.s == 0)
    def _():
        scatter.returned().wait_recv()
        u, count = LENT
        total[u : u + count] = back[...].astype(F32)

    scatter.close()

    @pl.when(place.s > 0)
    def _():
        for i in range(4):
            backward_copy(i).wait_send()


VSPEC = pl.BlockSpec(memory_space=pltpu.VMEM)
ASPEC = pl.BlockSpec(memory_space=pl.ANY)
SSPEC = pl.BlockSpec(memory_space=pltpu.SMEM)
DMA = pltpu.SemaphoreType.DMA


def run_layers(*args):
    g, s = (len(GATHER) + 1, 16), (len(SCATTER) + 1, 12)
    return pl.pallas_call(
        kernel,
        out_shape=[
            jax.ShapeDtypeStruct((TOK, WIDTH), BF16),
            jax.ShapeDtypeStruct((TOK, WIDTH), BF16),
            jax.ShapeDtypeStruct((UNITS, 16, WIDTH), F32),
            jax.ShapeDtypeStruct((16, 128), F32),
        ],
        in_specs=[ASPEC, ASPEC, SSPEC, VSPEC, ASPEC, ASPEC, VSPEC, ASPEC, VSPEC, VSPEC, VSPEC, VSPEC, VSPEC],
        out_specs=[VSPEC] * 4,
        scratch_shapes=[
            pltpu.VMEM((32, UNITS, 16, WIDTH), BF16),
            pltpu.VMEM((32, 16, 128), F32),
            pltpu.VMEM((16, UNITS, 16, WIDTH), BF16),
            pltpu.VMEM((16, 16, 128), F32),
        ]
        + [pltpu.VMEM((SHARE, slots, units, 16, WIDTH), BF16) for slots, units in LANDING]
        + [pltpu.VMEM((slots, 4 * units, 128), F32) for slots, units in LANDING]
        + [pltpu.VMEM((LENT[1], 16, WIDTH), BF16)]
        + [pltpu.VMEM(*v) for v in HELD.values()]
        + [DMA(g[:1]), DMA(g), DMA((8,)), DMA((4,)), DMA((4,)), DMA((4,)), DMA((4,)), DMA(s[:1]), DMA(s), DMA((4,)), DMA((9,))]
        + [pltpu.SemaphoreType.REGULAR] * 2,
        compiler_params=pltpu.CompilerParams(collective_id=1, has_side_effects=True, vmem_limit_bytes=VMEM_LIMIT),
        name="layers",
    )(*args)


def finish_kernel(out, gz, total, small, out2, gz2, g_in, g_out, g_up, g_down, g_gains, g_vecs, g_mgain, g_mbias, g_heads):
    out2[...] = out[...]
    gz2[...] = gz[...]
    g_in[...] = total[IN : IN + 6]
    g_out[...] = total[OUT : OUT + 2]
    for q in range(4):
        g_down[:, :, q * 1024 : (q + 1) * 1024] = total[DOWN + 2 * q : DOWN + 2 * q + 2]
    g_up[...] = total[UP : UP + 8].reshape(128, WIDTH).T
    lane = lax.axis_index("dp") % 4
    thin = jnp.zeros((10, 32), F32)
    for j in range(4):
        thin = jnp.where(lane == j, small[0:10, 32 * j : 32 * (j + 1)], thin)
    for i in range(3):
        g_gains[i] = thin[i : i + 1]
    for i in range(7):
        g_vecs[i] = thin[3 + i : 4 + i]
    g_mgain[...] = small[10:11, :]
    g_mbias[...] = small[11:13, :]
    g_heads[...] = small[13:14, :16]


def finish(*args):
    f = jax.ShapeDtypeStruct
    return pl.pallas_call(
        finish_kernel,
        out_shape=[
            f((TOK, WIDTH), BF16), f((TOK, WIDTH), BF16), f((6, 16, WIDTH), F32), f((2, 16, WIDTH), F32),
            f((WIDTH, 128), F32), f((2, 16, FF), F32), f((3, 1, 32), F32), f((7, 1, 32), F32), f((1, 128), F32),
            f((2, 128), F32), f((1, 16), F32),
        ],
        in_specs=[VSPEC] * 4,
        out_specs=[VSPEC] * 11,
        name="finish",
    )(*args)


def body(
    tokens, cotangent, live_counts, segments, attn_input, attn_output, feed_up, feed_down,
    norm_gains, vector_bias, mid_gain, mid_bias, head_scale,
):
    res = run_layers(
        tokens, cotangent, live_counts, segments[None, :], attn_input[0].T.reshape(6, 16, WIDTH),
        attn_output[0].T.reshape(2, 16, WIDTH), feed_up[0], feed_down[0].T.reshape(2, 16, FF), norm_gains[0],
        vector_bias[0], mid_gain, mid_bias[0], head_scale,
    )
    out, gz, g_in, g_out, g_up, g_down, g_gains, g_vecs, g_mgain, g_mbias, g_heads = finish(*res)
    return (
        out[None],
        gz[None],
        g_in.reshape(96, WIDTH).T[None],
        g_out.reshape(32, WIDTH).T[None],
        g_up[None],
        g_down.reshape(32, FF).T[None],
        g_gains.transpose(1, 0, 2),
        g_vecs.transpose(1, 0, 2),
        g_mgain,
        g_mbias[None],
        g_heads,
    )


def solution(mesh):
    return jax.shard_map(
        body,
        mesh=mesh,
        in_specs=(
            P("dp", None), P("dp", None), P("dp"), P("dp"),
            P("pipe", None, "dp"), P("pipe", None, "dp"), P("pipe", None, "dp"), P("pipe", None, "dp"),
            P("pipe", None, "dp"), P("pipe", None, "dp"), P("pipe", "dp"), P("pipe", None, "dp"), P("pipe", None),
        ),
        out_specs=(
            P("pipe", "dp", None), P("pipe", "dp", None),
            P("pipe", None, "dp"), P("pipe", None, "dp"), P("pipe", None, "dp"), P("pipe", None, "dp"),
            P("pipe", None, "dp"), P("pipe", None, "dp"), P("pipe", "dp"), P("pipe", None, "dp"), P("pipe", None),
        ),
        check_vma=False,
    )
```

```python
import jax
import jax.numpy as jnp
from jax import lax
from jax.experimental import pallas as pl
from jax.experimental.pallas import tpu as pltpu
from jax.sharding import PartitionSpec as P

MESH = pl.DeviceIdType.MESH
EPS = 1e-05
F32, BF16 = jnp.float32, jnp.bfloat16
VMEM_LIMIT = 61840 * 1024

TOK, WIDTH, FF, QKV = 128, 1024, 4096, 3072
IN, OUT, UP, DOWN, UNITS = 0, 6, 8, 16, 24
SMALL = "small"
GATHER = (SMALL, (IN, 6), (OUT, 2), (UP, 8), (DOWN + 4, 4), (DOWN, 4))
SCATTER_STEPS = ((0,), (1,), (2,), (3,), (4, 5), (6,))
SCATTER = ((DOWN + 4, 4), (UP, 4), (UP + 4, 4), (IN, 4), SMALL, (IN + 4, 4), (DOWN, 4))
LENT = (DOWN, 4)
LATE, HELP = 5, 6
AWAY, AID = 6, 7
DESK = (DOWN + 4, 4)
X_OWN, X_GIVE, X_SUMS, X_BACK = 0, 1, 5, 8
BACK_GROUPS = (
    ((1, 0), (2, 0), (3, 0)),
    ((0, 1), (0, 2), (1, 1), (1, 2)),
    ((2, 1), (2, 2), (3, 1), (3, 2)),
    ((0, 3), (1, 3), (2, 3), (3, 3)),
)
SHARE = 3
OFFS = (0, 3, 1, 2)


class Place:
    def __init__(self):
        self.s = lax.axis_index("pipe")
        d = lax.axis_index("dp")
        self.d = d
        self.c = d % 2
        y, z = (d // 2) % 4, d // 8
        self.f = y + self.c * (z - y)
        self.g = z + self.c * (y - z)
        self.sf = 2 + 6 * self.c
        self.sg = 8 - 6 * self.c
        self.sib = d + 1 - 2 * self.c
        rows = [((self.f + i) % 4) * self.sf for i in range(4)]
        columns = [((self.g + i) % 4) * self.sg for i in range(4)]
        self.table = [[row + column + self.c for column in columns] for row in rows]
        self.flip = 1 - 2 * self.c

    def dp(self, of, og):
        return self.table[of % 4][og % 4]

    def sib_dp(self, of, og):
        return self.table[og % 4][of % 4] + self.flip

    def greet(self):
        sem = pltpu.get_barrier_semaphore()
        near = [self.dp(1, 0), self.dp(3, 0), self.dp(0, 1), self.dp(0, 3), self.sib]
        near = [(self.s, to) for to in near] + [((self.s + by) % 4, self.d) for by in (1, 3)]
        for to in near:
            pl.semaphore_signal(sem, inc=1, device_id=to, device_id_type=MESH)

    def barrier(self):
        pl.semaphore_wait(pltpu.get_barrier_semaphore(), 7)


class Work:
    def __init__(self):
        self.items = []

    def add(self, slice_of_work, when=None, tag=None):
        self.items.append((slice_of_work, when, tag))

    def pop(self, count=1):
        for _ in range(min(count, len(self.items))):
            slice_of_work, when, _ = self.items.pop(0)
            if when is None:
                slice_of_work()
            else:
                pl.when(when)(slice_of_work)

    def until(self, tag):
        while any(tag == item[2] for item in self.items):
            self.pop()

    def drain(self):
        self.pop(len(self.items))


def remote(src, dst, send, recv, s, to):
    return pltpu.make_async_remote_copy(
        src_ref=src, dst_ref=dst, send_sem=send, recv_sem=recv, device_id=(s, to), device_id_type=MESH
    )


def piece_block(whole, small, piece, d, half=None):
    if piece is SMALL:
        return small.at[d] if half is None else small.at[d, pl.ds(8 * half, 8)]
    u, n = piece
    return whole.at[d, pl.ds(u, n)] if half is None else whole.at[d, pl.ds(u + half * (n // 2), n // 2)]


def blocks(whole, small, piece, count, first=0):
    if piece is SMALL:
        return small.at[pl.ds(first, count)]
    return whole.at[pl.ds(first, count), pl.ds(*piece)]


class Gather:
    def __init__(self, place, whole, small, lent, send, recv, xsend, xrecv):
        self.p, self.whole_ref, self.small, self.lent = place, whole, small, lent
        self.send, self.recv, self.xsend, self.xrecv = send, recv, xsend, xrecv
        self.work = Work()

    def ref(self, k, d, half=None):
        if k == HELP:
            u, n = LENT
            at = pl.ds(u, n) if half is None else pl.ds(u + half * (n // 2), n // 2)
            return self.lent.at[d // 2, at]
        return piece_block(self.whole_ref, self.small, GATHER[k], d, half)

    def put(self, k, slot, d, half, to):
        ref = self.ref(k, d, half)
        remote(ref, ref, self.send.at[k], self.recv.at[k, slot], self.p.s, to).start()

    def got(self, k, slot, d):
        ref = self.ref(k, d)
        remote(ref, ref, self.send.at[k], self.recv.at[k, slot], self.p.s, self.p.sib).wait_recv()

    def hand(self, k, j, i):
        p = self.p
        d = p.dp(OFFS[j], OFFS[i])
        if k != HELP:
            self.put(k, 15, d, None, p.sib)
        elif (j, i) != (0, 0):
            self.give(j, i).start()

    def give(self, j, i):
        p = self.p
        d = p.dp(OFFS[j], OFFS[i])
        group = next(g for g, group in enumerate(BACK_GROUPS) if (j, i) in group)
        return remote(
            self.ref(HELP, d), self.ref(LATE, d), self.xsend.at[1], self.xrecv.at[X_GIVE + group], (p.s + 1) % 4, p.d
        )

    def lend(self):
        p = self.p
        return remote(
            self.ref(LATE, p.d), self.ref(HELP, p.d), self.xsend.at[0], self.xrecv.at[X_OWN], (p.s + 3) % 4, p.d
        )

    def spread(self, k, j):
        p = self.p
        d = p.dp(OFFS[j], 0)
        self.put(k, 3 + 3 * j, d, None, p.dp(0, 1))
        self.put(k, 4 + 3 * j, d, None, p.dp(0, 3))
        self.hand(k, j, 0)

    def first(self, k):
        p = self.p
        self.put(k, 0, p.d, None, p.dp(1, 0))
        self.put(k, 1, p.d, None, p.dp(3, 0))
        self.spread(k, 0)

    def ring(self, k):
        p = self.p
        left, right = p.dp(3, 0), p.dp(1, 0)
        self.got(k, 0, left)
        self.put(k, 2, left, 0, right)
        self.spread(k, 1)
        self.got(k, 1, right)
        self.put(k, 2, right, 1, left)
        self.spread(k, 2)

    def far(self, k):
        self.got(k, 2, self.p.dp(2, 0))
        self.spread(k, 3)

    def second(self, k, j):
        p = self.p
        low, high = p.dp(OFFS[j], 3), p.dp(OFFS[j], 1)
        self.got(k, 3 + 3 * j, low)
        self.put(k, 5 + 3 * j, low, 0, p.dp(0, 1))
        self.hand(k, j, 1)
        self.got(k, 4 + 3 * j, high)
        self.put(k, 5 + 3 * j, high, 1, p.dp(0, 3))
        self.hand(k, j, 2)

    def last(self, k, j):
        self.got(k, 5 + 3 * j, self.p.dp(OFFS[j], 2))
        self.hand(k, j, 3)

    def relay(self, group):
        p = self.p
        ref = self.many(LATE, len(BACK_GROUPS[group]))
        remote(ref, ref, self.xsend.at[1], self.xrecv.at[X_GIVE + group], p.s, p.sib).wait_recv()
        for j, i in BACK_GROUPS[group]:
            self.hand(LATE, j, i)

    def many(self, k, count):
        if k == HELP:
            return blocks(self.lent, None, LENT, count)
        return blocks(self.whole_ref, self.small, GATHER[k], count)

    def whole(self, k):
        ref = self.many(k, 16)
        remote(ref, ref, self.send.at[k], self.recv.at[k, 15], self.p.s, self.p.sib).wait_recv()

    def close(self):
        p = self.p

        def sent(k, count):
            ref = self.many(k, count)
            remote(ref, ref, self.send.at[k], self.recv.at[k, 15], p.s, p.sib).wait_send()

        for k in range(len(GATHER)):
            if k != LATE:
                sent(k, 31)

        @pl.when(p.s > 0)
        def _():
            sent(LATE, 31)

        @pl.when(p.s == 0)
        def _():
            sent(LATE, 16)
            self.lend().wait_send()

        @pl.when(p.s == 3)
        def _():
            sent(HELP, 15)
            ref = self.many(HELP, 15)
            remote(ref, ref, self.xsend.at[1], self.xrecv.at[X_GIVE], p.s, p.sib).wait_send()

    def run(self, own, ready):
        n, begun = len(GATHER), 0
        s = self.p.s

        def stage(step, k):
            if k == LATE:
                pl.when(s > 0)(lambda: step(k))
            elif 0 <= k < n:
                step(k)

        own(LATE)

        @pl.when(s == 0)
        def _():
            self.lend().start()
            self.hand(LATE, 0, 0)

        @pl.when(s == 3)
        def _():
            self.lend().wait_recv()
            for step in (self.first, self.ring, self.far):
                step(HELP)
            for j in range(4):
                self.second(HELP, j)
            for j in range(4):
                self.last(HELP, j)

        for t in range(n + 3):
            while begun < min(n, t + 3):
                if begun != LATE:
                    own(begun)
                stage(self.first, begun)
                begun += 1
            stage(self.ring, t)
            self.work.pop()
            stage(self.far, t - 1)
            self.work.pop()
            for j in range(4):
                stage(lambda k, j=j: self.second(k, j), t - 2)
                self.work.pop()
            for j in range(4):
                stage(lambda k, j=j: self.last(k, j), t - 3)
                self.work.pop()
            if 4 <= t < 8:
                pl.when(s == 0)(lambda t=t: self.relay(t - 4))

            self.work.pop()
            if t >= 3:
                self.whole(t - 3)
                ready(t - 3)
        self.work.drain()


def dot(a, b, ca, cb):
    return lax.dot_general(a, b, (((ca,), (cb,)), ((), ())), preferred_element_type=F32)


def centered(x):
    c = x - jnp.mean(x, axis=-1, keepdims=True)
    r = lax.rsqrt(jnp.mean(c * c, axis=-1, keepdims=True) + EPS)
    return c, r


def norm(x, gain, bias):
    c, r = centered(x)
    return c * r * gain + bias


def norm_back(x, gain, gy):
    c, r = centered(x)
    hat = c * r
    gh = gy * gain
    gx = r * (gh - jnp.mean(gh, axis=-1, keepdims=True) - hat * jnp.mean(gh * hat, axis=-1, keepdims=True))
    return gx, gy * hat


def rows_of(i, n):
    return pl.ds(pl.multiple_of(i * n, n), n)


def col_sum(x):
    return jnp.sum(x, axis=0, keepdims=True)


def row_sum(x):
    return dot(jnp.full((16, x.shape[0]), 1.0, BF16), x, 1, 0)[:1]


K0, K1 = 0.7978845608028654, 0.044715


def gelu(x):
    return 0.5 * x * (1.0 + jnp.tanh(K0 * (x + K1 * x * x * x)))


def gelu_both(x):
    t = jnp.tanh(K0 * (x + K1 * x * x * x))
    u = 0.5 * x * (1.0 + t)
    du = 0.5 * (1.0 + t) + 0.5 * x * (1.0 - t * t) * K0 * (1.0 + 3.0 * K1 * x * x)
    return u, du


def head_masks():
    lane = lax.broadcasted_iota(jnp.int32, (1, 128), 1)
    even = jnp.where(lane < 64, 1.0, 0.0)
    return even.astype(BF16), (1.0 - even).astype(BF16)


def two_rows(x, even, odd):
    return jnp.concatenate([x * even, x * odd], axis=0)


def each(count, unroll=1):
    def run(body):
        def step(i, carry):
            body(i)
            return carry

        lax.fori_loop(0, count, step, 0, unroll=unroll)

    return run


def stack(w, d0, nd, u, nu, cols=slice(0, WIDTH)):
    return w[pl.ds(d0, nd), u : u + nu, :, cols].reshape(nd * nu * 16, cols.stop - cols.start)


def head_columns():
    col = lax.broadcasted_iota(jnp.int32, (128, WIDTH), 1)
    head = lax.broadcasted_iota(jnp.int32, (128, WIDTH), 0)
    return jnp.where(col // 64 == head, 1.0, 0.0)


class Layer:
    def __init__(self, w, r):
        self.w, self.r = w, r


    def first_norm(self):
        r, pd = self.r, self.r["pd"]

        @each(4, 2)
        def _(i):
            at = rows_of(i, 32)
            r["a1"][at, :] = norm(r["zin"][at, :].astype(F32), pd[0:1, :], pd[3:4, :]).astype(BF16)

    def qkv(self, first=0, count=4):
        r = self.r

        @each(count, 4 if count == 4 else 1)
        def _(c):
            c = c + first
            at = rows_of(c, 768)
            acc = dot(r["a1"][...], stack(self.w, 8 * c, 8, IN, 6), 1, 1) + r["pq"][0:1, at]
            r["qkv"][:, at] = acc.astype(BF16)

    def attention(self, first=0, count=8):
        r, qkv = self.r, self.r["qkv"]
        even, odd = head_masks()

        @each(count, 4 if count == 8 else 1)
        def _(p):
            p = p + first
            cols = rows_of(p, 128)
            q = qkv[:, cols]
            k = qkv[:, pl.ds(pl.multiple_of(WIDTH + p * 128, 128), 128)]
            v = qkv[:, pl.ds(pl.multiple_of(2 * WIDTH + p * 128, 128), 128)]
            ok = r["ok"][...]
            sc = dot(two_rows(q, even, odd), k, 1, 1) * 0.125
            sc = jnp.where(jnp.concatenate([ok, ok], axis=0) > 0.5, sc, -1000000000.0)
            e = jnp.exp(sc - jnp.max(sc, axis=-1, keepdims=True))
            pr = e / jnp.sum(e, axis=-1, keepdims=True)
            r["p"][rows_of(p, 256), :] = pr
            pb = pr.astype(BF16)
            both = jnp.concatenate([pb[:TOK], pb[TOK:]], axis=1)
            mixed = dot(both, two_rows(v, even, odd), 1, 0)
            r["mixed"][:, cols] = mixed
            r["scaled"][:, cols] = (mixed * r["hs"][0:1, cols]).astype(BF16)

    def project(self):
        r = self.r
        r["attn"][...] = dot(r["scaled"][...], stack(self.w, 0, 32, OUT, 2), 1, 1) + r["pd"][6:7, :]

    def middle_norms(self):
        r, pd = self.r, self.r["pd"]

        @each(4, 2)
        def _(i):
            at = rows_of(i, 32)
            z2 = r["zin"][at, :].astype(F32) + norm(r["attn"][at, :], pd[1:2, :], pd[7:8, :])
            r["z2"][at, :] = z2
            r["a2"][at, :] = norm(z2, pd[2:3, :], pd[8:9, :]).astype(BF16)

    def up(self, first=0, count=4):
        r = self.r

        @each(count)
        def _(c):
            c = c + first
            cols = rows_of(c, 1024)
            r["ff"][:, cols] = dot(r["a2"][...], stack(self.w, 8 * c, 8, UP, 8), 1, 1) + r["pm"][11:12, cols]

    def inner_norm(self, first=0, count=8):
        r, pm = self.r, self.r["pm"]

        @each(count, 2)
        def _(i):
            i = i + first
            at = rows_of(i, 16)
            r["mid"][at, :] = norm(gelu(r["ff"][at, :]), pm[10:11, :], pm[12:13, :]).astype(BF16)

    def down(self, send_out):
        r = self.r
        for n in range(4):
            cols = slice(n * 256, (n + 1) * 256)
            acc = r["z2"][:, cols] + r["pd"][9:10, cols]
            for q in range(4):
                w = stack(self.w, 8 * n, 8, DOWN + 2 * q, 2)
                acc = acc + dot(r["mid"][:, q * 1024 : (q + 1) * 1024], w, 1, 1)
            r["out"][:, cols] = acc.astype(BF16)
            send_out(n)

    def prepare(self):
        r = self.r

        @each(8, 2)
        def _(i):
            at = rows_of(i, 16)
            u, du = gelu_both(r["ff"][at, :])
            c, s = centered(u)
            r["hat"][at, :] = (c * s).astype(BF16)
            r["slope"][at, :] = (du * s).astype(BF16)

        for name in ("gd", "gm"):
            r[name][...] = jnp.zeros_like(r[name])


    def back_down(self, *chunks):
        r = self.r
        for q in chunks:
            w = stack(self.w, 0, 32, DOWN + 2 * q, 2)
            r["ff"][:, q * 1024 : (q + 1) * 1024] = dot(r["gin"][...], w, 1, 0)

    def back_inner(self, first=0, count=8):
        r, pm = self.r, self.r["pm"]

        @each(count, 2)
        def _(i):
            i = i + first
            at = rows_of(i, 16)
            gh = r["ff"][at, :] * pm[10:11, :]
            hat = r["hat"][at, :].astype(F32)
            m1 = jnp.mean(gh, axis=-1, keepdims=True)
            m2 = jnp.mean(gh * hat, axis=-1, keepdims=True)
            r["ghid"][at, :] = ((gh - m1 - hat * m2) * r["slope"][at, :].astype(F32)).astype(BF16)

    def back_up(self, cols=slice(0, WIDTH)):
        r = self.r
        r["tw"][:, cols] = dot(r["ghid"][...], stack(self.w, 0, 32, UP, 8, cols), 1, 0)

    def back_middle(self):
        r, gd, pd = self.r, self.r["gd"], self.r["pd"]

        @each(4, 2)
        def _(i):
            at = rows_of(i, 32)
            ga2 = r["tw"][at, :]
            gz, gg = norm_back(r["z2"][at, :], pd[2:3, :], ga2)
            gd[2:3, :] += col_sum(gg)
            gd[8:9, :] += col_sum(ga2)
            gz = gz + r["gin"][at, :].astype(F32)
            r["gz2"][at, :] = gz
            gat, gg = norm_back(r["attn"][at, :], pd[1:2, :], gz)
            gd[1:2, :] += col_sum(gg)
            gd[7:8, :] += col_sum(gz)
            r["gattn"][at, :] = gat.astype(BF16)

    def back_project(self):
        r = self.r
        r["tw"][...] = dot(r["gattn"][...], stack(self.w, 0, 32, OUT, 2), 1, 0)

    def back_attention(self, first=0, count=8):
        r = self.r
        even, odd = head_masks()

        @each(count, 4 if count == 8 else 1)
        def _(p):
            p = p + first
            cols = rows_of(p, 128)
            kcols = pl.ds(pl.multiple_of(WIDTH + p * 128, 128), 128)
            vcols = pl.ds(pl.multiple_of(2 * WIDTH + p * 128, 128), 128)
            gs = r["tw"][:, cols]
            r["gh"][0:1, cols] = col_sum(gs * r["mixed"][:, cols])
            gmx = (gs * r["hs"][0:1, cols]).astype(BF16)
            q, k, v = r["qkv"][:, cols], r["qkv"][:, kcols], r["qkv"][:, vcols]
            gmx2 = two_rows(gmx, even, odd)
            gp = dot(gmx2, v, 1, 1)
            pr = r["p"][rows_of(p, 256), :]
            gsc = (pr * (gp - jnp.sum(pr * gp, axis=-1, keepdims=True))).astype(BF16)
            both = jnp.concatenate([gsc[:TOK], gsc[TOK:]], axis=1)
            r["gqkv"][:, cols] = (dot(both, two_rows(k, even, odd), 1, 0) * 0.125).astype(BF16)
            r["gqkv"][:, kcols] = (dot(gsc, two_rows(q, even, odd), 0, 0) * 0.125).astype(BF16)
            r["gqkv"][:, vcols] = dot(pr.astype(BF16), gmx2, 0, 0).astype(BF16)

    def back_qkv(self, cols=slice(0, WIDTH)):
        r = self.r
        r["tw"][:, cols] = dot(r["gqkv"][...], stack(self.w, 0, 32, IN, 6, cols), 1, 0)

    def back_first(self, send_out):
        r, gd, pd = self.r, self.r["gd"], self.r["pd"]
        for i in range(4):
            at = slice(i * 32, (i + 1) * 32)
            ga1 = r["tw"][at, :]
            gz, gg = norm_back(r["zin"][at, :].astype(F32), pd[0:1, :], ga1)
            r["gz"][at, :] = (gz + r["gz2"][at, :]).astype(BF16)
            send_out(i)
            gd[0:1, :] += col_sum(gg)
            gd[3:4, :] += col_sum(ga1)

    def inner_sums(self):
        r, gm = self.r, self.r["gm"]

        @each(8)
        def _(i):
            at = rows_of(i, 16)
            g = r["ff"][at, :]
            gm[10:11, :] += col_sum(g * r["hat"][at, :].astype(F32))
            gm[12:13, :] += col_sum(g)

        gm[11:12, :] = row_sum(r["ghid"][...])

    def other_sums(self):
        r, gd = self.r, self.r["gd"]
        gd[9:10, :] = row_sum(r["gin"][...])
        gd[6:7, :] = row_sum(r["gattn"][...])
        gd[4:5, :] = row_sum(r["gqkv"][:, :WIDTH])
        gd[5:6, :] = row_sum(r["gqkv"][:, 2 * WIDTH :])


    def grad_down(self, *chunks):
        r = self.r

        @each(4)
        def _(c):
            gt = r["gin"][:, rows_of(c, 256)].T
            for q in chunks:
                g = dot(gt, r["mid"][:, q * 1024 : (q + 1) * 1024], 1, 0).astype(BF16)
                self.w[pl.ds(8 * c, 8), DOWN + 2 * q : DOWN + 2 * q + 2] = g.reshape(8, 2, 16, WIDTH)

    def grad_up(self, first, count):
        r = self.r

        @each(count)
        def _(c):
            c = c + first
            g = dot(r["ghid"][:, rows_of(c, 512)].T, r["a2"][...], 1, 0).astype(BF16)
            self.w[pl.ds(4 * c, 4), UP : UP + 8] = g.reshape(4, 8, 16, WIDTH)

    def grad_in(self, first, count):
        r = self.r

        @each(count)
        def _(c):
            c = c + first
            g = dot(r["gqkv"][:, rows_of(c, 384)].T, r["a1"][...], 1, 0).astype(BF16)
            self.w[pl.ds(4 * c, 4), IN : IN + 6] = g.reshape(4, 6, 16, WIDTH)

    def grad_out(self, c):
        r = self.r
        g = dot(r["gattn"][:, c * 512 : (c + 1) * 512].T, r["scaled"][...], 1, 0).astype(BF16)
        self.w[pl.ds(16 * c, 16), OUT : OUT + 2] = g.reshape(16, 2, 16, WIDTH)

    def grad_small(self, small):
        r = self.r
        hsum = lax.dot_general(
            jnp.broadcast_to(r["gh"][0:1, :], (8, WIDTH)), head_columns(), (((1,), (1,)), ((), ())),
            precision=lax.Precision.HIGHEST, preferred_element_type=F32,
        )
        is13 = lax.broadcasted_iota(jnp.int32, (16, 128), 0) == 13
        heads = jnp.where(is13, jnp.concatenate([hsum, hsum], axis=0), 0.0)
        for d in range(32):
            a, b = (d // 4) * 128, d * 128
            small[d] = r["gd"][:, a : a + 128] + r["gm"][:, b : b + 128] + heads


class Scatter:
    def __init__(self, place, grads, small, sib, ssib, land, sland, back, send, recv, xsend, xrecv):
        self.p, self.grads, self.small = place, grads, small
        self.sib, self.ssib, self.land, self.sland, self.back = sib, ssib, land, sland, back
        self.send, self.recv, self.xsend, self.xrecv = send, recv, xsend, xrecv
        self.work = Work()

    def copy(self, k, slot, src, dst, to):
        return remote(src, dst, self.send.at[k], self.recv.at[k, slot], self.p.s, to)

    def go(self, k, slot, src, dst, to):
        self.copy(k, slot, src, dst, to).start()

    def got(self, k, slot, dst):
        self.copy(k, slot, dst, dst, self.p.sib).wait_recv()

    def block(self, k, of, og, half=None):
        d = self.p.dp(of, og)
        if k == AID:
            return piece_block(self.sib, None, DESK, d // 2, half)
        return piece_block(self.grads, self.small, SCATTER[k], d, half)

    def from_sib(self, k, slot, half=None):
        return piece_block(self.sib, self.ssib, SCATTER[k], slot, half)

    def landing(self, k, kind, slot):
        if k != AID and SCATTER[k] is SMALL:
            return self.sland[kind].at[slot]
        step = next((t for t, ks in enumerate(SCATTER_STEPS) if k in ks), len(SCATTER_STEPS))
        return self.land[kind].at[step % SHARE, slot]

    def landed(self, k, slot, kind, j=0):
        self.got(k, slot, self.landing(k, kind, pl.ds(2 * j, 2)))

    def to_sibling(self, k):
        p = self.p
        for i in (3, 1, 2, 0):
            for j in (3, 1, 2, 0):
                src = piece_block(self.grads, self.small, SCATTER[k], p.sib_dp(OFFS[j], OFFS[i]))
                self.go(k, 0 if i == 3 else 1, src, self.from_sib(k, i * 4 + j), p.sib)

    def lent_sum(self, i, j):
        p = self.p
        return remote(
            self.block(AWAY, OFFS[j], OFFS[i]), self.block(AID, OFFS[j], OFFS[i]), self.xsend.at[2],
            self.xrecv.at[X_SUMS + (2, 1, 1, 0)[i]], (p.s + 3) % 4, p.d,
        )

    def lend(self):
        for i in (3, 1, 2, 0):
            if i in (3, 1):
                self.arrived(AWAY, i == 3)
            for j in (3, 1, 2, 0):
                self.add(AWAY, self.block(AWAY, OFFS[j], OFFS[i]), [self.from_sib(AWAY, i * 4 + j)])
                self.lent_sum(i, j).start()

    def returned(self):
        p = self.p
        return remote(
            self.block(AID, 0, 0), self.back, self.xsend.at[3], self.xrecv.at[X_BACK], (p.s + 1) % 4, p.d
        )

    def arrived(self, k, far):
        first, count = (12, 4) if far else (0, 12)
        self.got(k, 0 if far else 1, blocks(self.sib, self.ssib, SCATTER[k], count, first))

    def lent_arrived(self, group):
        ref = blocks(self.sib, None, DESK, (4, 8, 4)[group])
        remote(ref, ref, self.xsend.at[2], self.xrecv.at[X_SUMS + group], self.p.s, self.p.sib).wait_recv()

    def add(self, k, dst, srcs, store=None):
        out = dst if store is None else store
        if store is None and not srcs:
            return
        if k != AID and SCATTER[k] is SMALL:
            out[...] = dst[...] + sum(src[...] for src in srcs)
            return

        @each(dst.shape[0])
        def _(u):
            acc = dst[u].astype(F32)
            for src in srcs:
                acc = acc + src[u].astype(F32)
            out[u] = acc.astype(out.dtype)

    def halves(self, k, j):
        p = self.p
        srcs = []
        if k == AID:
            if j == 3:
                self.lent_arrived(0)
        else:
            if j == 3:
                self.arrived(k, True)
            srcs = [self.from_sib(k, 12 + j)]
        self.add(k, self.block(k, OFFS[j], 2), srcs)
        for side, to in enumerate((p.dp(0, 1), p.dp(0, 3))):
            self.go(k, 2 + j, self.block(k, OFFS[j], 2, side), self.landing(k, 0, 2 * j + side), to)

    def wholes(self, k, j):
        p = self.p
        if j == 3:
            if k == AID:
                self.lent_arrived(1)
            else:
                self.arrived(k, False)
        self.landed(k, 2 + j, 0, j)
        for i, near, side in ((2, 1, 0), (1, 3, 1)):
            for half in range(2):
                srcs = [] if k == AID else [self.from_sib(k, i * 4 + j, half)]
                if half == side:
                    srcs.append(self.landing(k, 0, 2 * j + side))
                self.add(k, self.block(k, OFFS[j], near, half), srcs)
        for near, side in ((1, 0), (3, 1)):
            self.go(k, 6 + j, self.block(k, OFFS[j], near), self.landing(k, 1, 2 * j + side), p.dp(0, near))

    def far(self, k, j):
        p = self.p
        srcs = []
        if k != AID:
            srcs.append(self.from_sib(k, j))
        elif j == 3:
            self.lent_arrived(2)
        self.landed(k, 6 + j, 1, j)
        srcs += [self.landing(k, 1, 2 * j + side) for side in range(2)]
        self.add(k, self.block(k, OFFS[j], 0), srcs)
        if j == 3:
            self.go(k, 10, self.block(k, 2, 0, 0), self.landing(k, 2, 0), p.dp(1, 0))
            self.go(k, 10, self.block(k, 2, 0, 1), self.landing(k, 2, 1), p.dp(3, 0))

    def near(self, k):
        p = self.p
        self.landed(k, 10, 2)
        for near, side in ((1, 0), (3, 1)):
            self.add(k, self.block(k, near, 0, side), [self.landing(k, 2, side)])
        for near, side in ((1, 0), (3, 1)):
            self.go(k, 11, self.block(k, near, 0), self.landing(k, 3, side), p.dp(near, 0))

    def last(self, k, total, small_total):
        self.landed(k, 11, 3)
        srcs = [self.landing(k, 3, side) for side in range(2)]
        if k == AID:
            self.add(k, self.block(k, 0, 0), srcs)
            self.returned().start()
        elif SCATTER[k] is SMALL:
            self.add(k, self.block(k, 0, 0), srcs, store=small_total)
        else:
            u, n = SCATTER[k]
            self.add(k, self.block(k, 0, 0), srcs, store=total.at[pl.ds(u, n)])

    def aid(self):
        for step in (self.halves, self.wholes, self.far):
            for j in (3, 1, 2, 0):
                step(AID, j)
        self.near(AID)
        self.last(AID, None, None)

    def close(self):
        p = self.p

        def sent(k, count):
            if k == AID:
                ref = blocks(self.sib, None, DESK, count)
            else:
                ref = blocks(self.grads, self.small, SCATTER[k], count)
            self.copy(k, 0, ref, ref, p.sib).wait_send()

        for k in range(len(SCATTER)):
            if k != AWAY:
                sent(k, 31)

        @pl.when(p.s > 0)
        def _():
            sent(AWAY, 31)

        @pl.when(p.s == 0)
        def _():
            sent(AWAY, 16)
            ref = blocks(self.grads, None, LENT, 16)
            remote(ref, ref, self.xsend.at[2], self.xrecv.at[X_SUMS], p.s, p.sib).wait_send()

        @pl.when(p.s == 3)
        def _():
            sent(AID, 15)
            self.returned().wait_send()


HELD = dict(
    pd=((16, WIDTH), F32), pm=((16, FF), F32), pq=((1, QKV), F32), hs=((8, WIDTH), F32), ok=((TOK, TOK), F32),
    zin=((TOK, WIDTH), BF16), a1=((TOK, WIDTH), BF16), qkv=((TOK, QKV), BF16), p=((8 * 256, TOK), F32),
    mixed=((TOK, WIDTH), F32), scaled=((TOK, WIDTH), BF16), attn=((TOK, WIDTH), F32), z2=((TOK, WIDTH), F32),
    a2=((TOK, WIDTH), BF16), ff=((TOK, FF), F32), hat=((TOK, FF), BF16), slope=((TOK, FF), BF16), mid=((TOK, FF), BF16),
    gin=((TOK, WIDTH), BF16), ghid=((TOK, FF), BF16), gattn=((TOK, WIDTH), BF16), gqkv=((TOK, QKV), BF16),
    tw=((TOK, WIDTH), F32), gz2=((TOK, WIDTH), F32), gd=((16, WIDTH), F32), gm=((16, FF), F32), gh=((8, WIDTH), F32),
)
LANDING = ((8, 2), (8, 4), (2, 2), (2, 4))


def kernel(*refs):
    (tok, cot, live, seg, own_in, own_out, own_up, own_down, gains, vecs, mgain, mbias, hscale), refs = refs[:13], refs[13:]
    (out, gz, total, small_total), refs = refs[:4], refs[4:]
    (w, small, sib, ssib), refs = refs[:4], refs[4:]
    land, sland, refs = refs[:4], refs[4:8], refs[8:]
    back, refs = refs[0], refs[1:]
    r = dict(zip(HELD, refs), out=out, gz=gz)
    gsend, grecv, own_sem, xsend, xrecv, bsend, brecv, ssend, srecv, hsend, hrecv, sib_ok, lent_ok = refs[len(HELD) :]
    place = Place()
    layer = Layer(w, r)
    place.greet()

    loads = [
        pltpu.make_async_copy(
            own_down.at[:, :, pl.ds(q * 1024, 1024)], w.at[place.d, pl.ds(DOWN + 2 * q, 2)], own_sem.at[q]
        )
        for q in range(4)
    ] + [
        pltpu.make_async_copy(own_in, w.at[place.d, pl.ds(IN, 6)], own_sem.at[4]),
        pltpu.make_async_copy(own_out, w.at[place.d, pl.ds(OUT, 2)], own_sem.at[5]),
    ]
    for copy in loads:
        copy.start()
    token_load = pltpu.make_async_copy(tok, r["zin"], own_sem.at[6])
    cot_load = pltpu.make_async_copy(cot, r["gin"], own_sem.at[7])

    @pl.when(place.s == 0)
    def _():
        token_load.start()

    @pl.when(place.s == 3)
    def _():
        cot_load.start()

    mine = lax.broadcasted_iota(jnp.int32, (1, 128), 1) // 32 == place.d % 4

    def spot(x):
        x = x.astype(F32)
        return jnp.where(mine, jnp.concatenate([x, x, x, x], axis=1), 0.0)

    small[place.d, 0:3] = spot(gains[...])
    small[place.d, 3:10] = spot(vecs[...])
    small[place.d, 10:11] = mgain[...].astype(F32)
    small[place.d, 11:13] = mbias[...].astype(F32)
    small[place.d, 13:16] = jnp.zeros((3, 128), F32)
    place.barrier()

    def own(k):
        if k == 3:
            w[place.d, UP : UP + 8] = own_up[...].T.reshape(8, 16, WIDTH)
        for copy in {1: loads[4:5], 2: loads[5:6], 4: loads[2:4], 5: loads[:2]}.get(k, ()):
            copy.wait()

    def forward_copy(n):
        cols = pl.ds(n * 256, 256)
        return remote(
            out.at[:, cols], r["zin"].at[:, cols], xsend.at[n], xrecv.at[n], (place.s + 1) % 4, place.d
        )

    def send_forward(n):
        @pl.when(place.s < 3)
        def _():
            forward_copy(n).start()

    gather = Gather(place, w, small, sib, gsend, grecv, hsend, hrecv)

    def setup():
        for q in range(8):
            r["pd"][:, q * 128 : (q + 1) * 128] = small[4 * q] + small[4 * q + 1] + small[4 * q + 2] + small[4 * q + 3]
        for q in range(32):
            r["pm"][:, q * 128 : (q + 1) * 128] = small[q]
        r["pq"][:, :WIDTH] = r["pd"][4:5, :]
        r["pq"][:, WIDTH : 2 * WIDTH] = jnp.zeros((1, WIDTH), F32)
        r["pq"][:, 2 * WIDTH :] = r["pd"][5:6, :]
        heads = jnp.concatenate([hscale[...].astype(F32), jnp.zeros((1, 112), F32)], axis=1)
        r["hs"][...] = lax.dot_general(
            jnp.broadcast_to(heads, (8, 128)), head_columns(), (((1,), (0,)), ((), ())),
            precision=lax.Precision.HIGHEST, preferred_element_type=F32,
        )
        row = lax.broadcasted_iota(jnp.int32, (TOK, TOK), 0)
        col = lax.broadcasted_iota(jnp.int32, (TOK, TOK), 1)
        seg_key = jnp.broadcast_to(seg[...].astype(F32), (TOK, TOK))
        ok = (seg_key == seg_key.T) & (col <= row) & (row // 64 == col // 64)
        r["ok"][...] = jnp.where(ok, 1.0, 0.0)

    begins = place.s == 0

    def ready(k):
        work = gather.work
        if k == 0:
            setup()

            @pl.when(begins)
            def _():
                token_load.wait()
                layer.first_norm()
        elif k == 1:
            for c in range(2):
                work.add(lambda c=c: layer.qkv(2 * c, 2), begins)
            for c in range(4):
                work.add(lambda c=c: layer.attention(2 * c, 2), begins)
        elif k == 2:
            work.add(layer.project, begins)
            work.add(layer.middle_norms, begins)
        elif k == 3:
            for c in range(2):
                work.add(lambda c=c: layer.up(2 * c, 2), begins)
            for c in range(2):
                work.add(lambda c=c: layer.inner_norm(4 * c, 4), begins)

    gather.run(own, ready)

    @pl.when(begins)
    def _():
        layer.down(send_forward)

    @pl.when(place.s == 3)
    def _():
        cot_load.wait()

        @each(4)
        def _(i):
            at = rows_of(i, 32)
            row = lax.broadcasted_iota(jnp.int32, (32, WIDTH), 0) + 32 * i
            alive = row % 64 < jnp.where(row < 64, live[0], live[1])
            r["gin"][at, :] = jnp.where(alive, r["gin"][at, :].astype(F32), 0.0).astype(BF16)

    @pl.when(place.s > 0)
    def _():
        for n in range(4):
            forward_copy(n).wait_recv()
        layer.first_norm()
        layer.qkv()
        layer.attention()
        layer.project()
        layer.middle_norms()
        layer.up()
        layer.inner_norm()
        layer.down(send_forward)

    layer.prepare()
    gather.close()
    pl.semaphore_signal(sib_ok, inc=1, device_id=(place.s, place.sib), device_id_type=MESH)

    @pl.when(place.s < 3)
    def _():
        for n in range(4):
            forward_copy(n).wait_send()

    def backward_copy(i):
        at = pl.ds(i * 32, 32)
        return remote(gz.at[at], r["gin"].at[at], bsend.at[i], brecv.at[i], (place.s + 3) % 4, place.d)

    def send_backward(i):
        @pl.when(place.s > 0)
        def _():
            backward_copy(i).start()

    @pl.when(place.s < 3)
    def _():
        for i in range(4):
            backward_copy(i).wait_recv()

    @pl.when(place.s > 0)
    def _():
        layer.back_down(0, 1, 2, 3)
        layer.back_inner()
        layer.back_up()
        layer.back_middle()
        layer.back_project()
        layer.back_attention()
        layer.back_qkv()
        layer.back_first(send_backward)

    def first_section(*phases):
        @pl.when(place.s == 0)
        def _():
            for phase in phases:
                phase()

    scatter = Scatter(place, w, small, sib, ssib, land, sland, back, ssend, srecv, hsend, hrecv)
    n = len(SCATTER_STEPS)

    def stage(step, t):
        for k in SCATTER_STEPS[t] if 0 <= t < n else ():
            if k == AWAY:
                pl.when(place.s > 0)(lambda k=k: step(k))
            else:
                step(k)
        scatter.work.pop()

    def flow(t):
        for late, step in enumerate((scatter.halves, scatter.wholes, scatter.far)):
            for j in (3, 1, 2, 0):
                stage(lambda k, j=j, step=step: step(k, j), t - 1 - late)
        stage(scatter.near, t - 4)
        stage(lambda k: scatter.last(k, total, small_total), t - 5)

    work = scatter.work
    halfs = (slice(0, 512), slice(512, 1024))
    for c in range(2):
        work.add(lambda c=c: layer.back_inner(4 * c, 4), begins)
    for half in halfs:
        work.add(lambda half=half: layer.back_up(half), begins)
    for c in range(4):
        work.add(lambda c=c: layer.grad_up(2 * c, 2))
    work.add(lambda: scatter.to_sibling(1))
    work.add(lambda: scatter.to_sibling(2), tag="up")
    work.add(layer.back_middle, begins)
    work.add(layer.back_project, begins)
    for c in range(4):
        work.add(lambda c=c: layer.back_attention(2 * c, 2), begins)
    for half in halfs:
        work.add(lambda half=half: layer.back_qkv(half), begins)
    work.add(lambda: layer.back_first(send_backward), begins)
    for c in range(4):
        work.add(lambda c=c: layer.grad_in(2 * c, 2))
    for c in range(2):
        work.add(lambda c=c: layer.grad_out(c))
    work.add(lambda: scatter.to_sibling(3))
    work.add(lambda: scatter.to_sibling(5), tag="in")
    work.add(layer.inner_sums)
    work.add(layer.other_sums)
    work.add(lambda: layer.grad_small(small))
    work.add(lambda: scatter.to_sibling(4), tag="small")

    first_section(lambda: layer.back_down(2, 3))
    layer.grad_down(2, 3)
    pl.semaphore_wait(sib_ok, 1)
    scatter.to_sibling(0)
    first_section(lambda: layer.back_down(0, 1))
    layer.grad_down(0, 1)
    scatter.to_sibling(AWAY)
    flow(1)

    @pl.when(begins)
    def _():
        pl.semaphore_wait(lent_ok, 1)
        scatter.lend()

    work.until("up")
    flow(2)
    flow(3)

    @pl.when(place.s == 3)
    def _():
        pl.semaphore_signal(lent_ok, inc=1, device_id=(0, place.d), device_id_type=MESH)

    work.until("in")
    flow(4)
    work.until("small")
    for t in range(5, n + 5):
        flow(t)
    pl.when(place.s == 3)(scatter.aid)

    @pl.when(place.s == 0)
    def _():
        scatter.returned().wait_recv()
        u, count = LENT
        total[u : u + count] = back[...].astype(F32)

    scatter.close()

    @pl.when(place.s > 0)
    def _():
        for i in range(4):
            backward_copy(i).wait_send()


VSPEC = pl.BlockSpec(memory_space=pltpu.VMEM)
ASPEC = pl.BlockSpec(memory_space=pl.ANY)
SSPEC = pl.BlockSpec(memory_space=pltpu.SMEM)
DMA = pltpu.SemaphoreType.DMA


def run_layers(*args):
    g, s = (len(GATHER) + 1, 16), (len(SCATTER) + 1, 12)
    return pl.pallas_call(
        kernel,
        out_shape=[
            jax.ShapeDtypeStruct((TOK, WIDTH), BF16),
            jax.ShapeDtypeStruct((TOK, WIDTH), BF16),
            jax.ShapeDtypeStruct((UNITS, 16, WIDTH), F32),
            jax.ShapeDtypeStruct((16, 128), F32),
        ],
        in_specs=[ASPEC, ASPEC, SSPEC, VSPEC, ASPEC, ASPEC, VSPEC, ASPEC, VSPEC, VSPEC, VSPEC, VSPEC, VSPEC],
        out_specs=[VSPEC] * 4,
        scratch_shapes=[
            pltpu.VMEM((32, UNITS, 16, WIDTH), BF16),
            pltpu.VMEM((32, 16, 128), F32),
            pltpu.VMEM((16, UNITS, 16, WIDTH), BF16),
            pltpu.VMEM((16, 16, 128), F32),
        ]
        + [pltpu.VMEM((SHARE, slots, units, 16, WIDTH), BF16) for slots, units in LANDING]
        + [pltpu.VMEM((slots, 4 * units, 128), F32) for slots, units in LANDING]
        + [pltpu.VMEM((LENT[1], 16, WIDTH), BF16)]
        + [pltpu.VMEM(*v) for v in HELD.values()]
        + [DMA(g[:1]), DMA(g), DMA((8,)), DMA((4,)), DMA((4,)), DMA((4,)), DMA((4,)), DMA(s[:1]), DMA(s), DMA((4,)), DMA((9,))]
        + [pltpu.SemaphoreType.REGULAR] * 2,
        compiler_params=pltpu.CompilerParams(collective_id=1, has_side_effects=True, vmem_limit_bytes=VMEM_LIMIT),
        name="layers",
    )(*args)


def finish_kernel(out, gz, total, small, out2, gz2, g_in, g_out, g_up, g_down, g_gains, g_vecs, g_mgain, g_mbias, g_heads):
    out2[...] = out[...]
    gz2[...] = gz[...]
    g_in[...] = total[IN : IN + 6]
    g_out[...] = total[OUT : OUT + 2]
    for q in range(4):
        g_down[:, :, q * 1024 : (q + 1) * 1024] = total[DOWN + 2 * q : DOWN + 2 * q + 2]
    g_up[...] = total[UP : UP + 8].reshape(128, WIDTH).T
    lane = lax.axis_index("dp") % 4
    thin = jnp.zeros((10, 32), F32)
    for j in range(4):
        thin = jnp.where(lane == j, small[0:10, 32 * j : 32 * (j + 1)], thin)
    for i in range(3):
        g_gains[i] = thin[i : i + 1]
    for i in range(7):
        g_vecs[i] = thin[3 + i : 4 + i]
    g_mgain[...] = small[10:11, :]
    g_mbias[...] = small[11:13, :]
    g_heads[...] = small[13:14, :16]


def finish(*args):
    f = jax.ShapeDtypeStruct
    return pl.pallas_call(
        finish_kernel,
        out_shape=[
            f((TOK, WIDTH), BF16), f((TOK, WIDTH), BF16), f((6, 16, WIDTH), F32), f((2, 16, WIDTH), F32),
            f((WIDTH, 128), F32), f((2, 16, FF), F32), f((3, 1, 32), F32), f((7, 1, 32), F32), f((1, 128), F32),
            f((2, 128), F32), f((1, 16), F32),
        ],
        in_specs=[VSPEC] * 4,
        out_specs=[VSPEC] * 11,
        name="finish",
    )(*args)


def body(
    tokens, cotangent, live_counts, segments, attn_input, attn_output, feed_up, feed_down,
    norm_gains, vector_bias, mid_gain, mid_bias, head_scale,
):
    res = run_layers(
        tokens, cotangent, live_counts, segments[None, :], attn_input[0].T.reshape(6, 16, WIDTH),
        attn_output[0].T.reshape(2, 16, WIDTH), feed_up[0], feed_down[0].T.reshape(2, 16, FF), norm_gains[0],
        vector_bias[0], mid_gain, mid_bias[0], head_scale,
    )
    out, gz, g_in, g_out, g_up, g_down, g_gains, g_vecs, g_mgain, g_mbias, g_heads = finish(*res)
    return (
        out[None],
        gz[None],
        g_in.reshape(96, WIDTH).T[None],
        g_out.reshape(32, WIDTH).T[None],
        g_up[None],
        g_down.reshape(32, FF).T[None],
        g_gains.transpose(1, 0, 2),
        g_vecs.transpose(1, 0, 2),
        g_mgain,
        g_mbias[None],
        g_heads,
    )


def solution(mesh):
    return jax.shard_map(
        body,
        mesh=mesh,
        in_specs=(
            P("dp", None), P("dp", None), P("dp"), P("dp"),
            P("pipe", None, "dp"), P("pipe", None, "dp"), P("pipe", None, "dp"), P("pipe", None, "dp"),
            P("pipe", None, "dp"), P("pipe", None, "dp"), P("pipe", "dp"), P("pipe", None, "dp"), P("pipe", None),
        ),
        out_specs=(
            P("pipe", "dp", None), P("pipe", "dp", None),
            P("pipe", None, "dp"), P("pipe", None, "dp"), P("pipe", None, "dp"), P("pipe", None, "dp"),
            P("pipe", None, "dp"), P("pipe", None, "dp"), P("pipe", "dp"), P("pipe", None, "dp"), P("pipe", None),
        ),
        check_vma=False,
    )
```

```python
import jax
import jax.numpy as jnp
from jax import lax
from jax.experimental import pallas as pl
from jax.experimental.pallas import tpu as pltpu
from jax.sharding import PartitionSpec as P

MESH = pl.DeviceIdType.MESH
EPS = 1e-05
F32, BF16 = jnp.float32, jnp.bfloat16
VMEM_LIMIT = 61840 * 1024

TOK, WIDTH, FF, QKV = 128, 1024, 4096, 3072
IN, OUT, UP, DOWN, UNITS = 0, 6, 8, 16, 24
SMALL = "small"
GATHER = (SMALL, (IN, 6), (OUT, 2), (UP, 8), (DOWN + 4, 4), (DOWN, 4))
SCATTER_STEPS = ((0,), (1,), (2,), (3,), (4, 5), (6,))
SCATTER = ((DOWN + 4, 4), (UP, 4), (UP + 4, 4), (IN, 4), SMALL, (IN + 4, 4), (DOWN, 4))
LENT = (DOWN, 4)
LATE, HELP = 5, 6
AWAY, AID = 6, 7
DESK = (DOWN + 4, 4)
X_OWN, X_GIVE, X_SUMS, X_BACK = 0, 1, 5, 8
BACK_GROUPS = (
    ((1, 0), (2, 0), (3, 0)),
    ((0, 1), (0, 2), (1, 1), (1, 2)),
    ((2, 1), (2, 2), (3, 1), (3, 2)),
    ((0, 3), (1, 3), (2, 3), (3, 3)),
)
SHARE = 3
OFFS = (0, 3, 1, 2)


class Place:
    def __init__(self):
        self.s = lax.axis_index("pipe")
        d = lax.axis_index("dp")
        self.d = d
        self.c = d % 2
        y, z = (d // 2) % 4, d // 8
        self.f = y + self.c * (z - y)
        self.g = z + self.c * (y - z)
        self.sf = 2 + 6 * self.c
        self.sg = 8 - 6 * self.c
        self.sib = d + 1 - 2 * self.c
        rows = [((self.f + i) % 4) * self.sf for i in range(4)]
        columns = [((self.g + i) % 4) * self.sg for i in range(4)]
        self.table = [[row + column + self.c for column in columns] for row in rows]
        self.flip = 1 - 2 * self.c

    def dp(self, of, og):
        return self.table[of % 4][og % 4]

    def sib_dp(self, of, og):
        return self.table[og % 4][of % 4] + self.flip

    def greet(self):
        sem = pltpu.get_barrier_semaphore()
        near = [self.dp(1, 0), self.dp(3, 0), self.dp(0, 1), self.dp(0, 3), self.sib]
        near = [(self.s, to) for to in near] + [((self.s + by) % 4, self.d) for by in (1, 3)]
        for to in near:
            pl.semaphore_signal(sem, inc=1, device_id=to, device_id_type=MESH)

    def barrier(self):
        pl.semaphore_wait(pltpu.get_barrier_semaphore(), 7)


class Work:
    def __init__(self):
        self.items = []

    def add(self, slice_of_work, when=None, tag=None):
        self.items.append((slice_of_work, when, tag))

    def pop(self, count=1):
        for _ in range(min(count, len(self.items))):
            slice_of_work, when, _ = self.items.pop(0)
            if when is None:
                slice_of_work()
            else:
                pl.when(when)(slice_of_work)

    def until(self, tag):
        while any(tag == item[2] for item in self.items):
            self.pop()

    def drain(self):
        self.pop(len(self.items))


def remote(src, dst, send, recv, s, to):
    return pltpu.make_async_remote_copy(
        src_ref=src, dst_ref=dst, send_sem=send, recv_sem=recv, device_id=(s, to), device_id_type=MESH
    )


def piece_block(whole, small, piece, d, half=None):
    if piece is SMALL:
        return small.at[d] if half is None else small.at[d, pl.ds(8 * half, 8)]
    u, n = piece
    return whole.at[d, pl.ds(u, n)] if half is None else whole.at[d, pl.ds(u + half * (n // 2), n // 2)]


def blocks(whole, small, piece, count, first=0):
    if piece is SMALL:
        return small.at[pl.ds(first, count)]
    return whole.at[pl.ds(first, count), pl.ds(*piece)]


class Gather:
    def __init__(self, place, whole, small, lent, send, recv, xsend, xrecv):
        self.p, self.whole_ref, self.small, self.lent = place, whole, small, lent
        self.send, self.recv, self.xsend, self.xrecv = send, recv, xsend, xrecv
        self.work = Work()

    def ref(self, k, d, half=None):
        if k == HELP:
            u, n = LENT
            at = pl.ds(u, n) if half is None else pl.ds(u + half * (n // 2), n // 2)
            return self.lent.at[d // 2, at]
        return piece_block(self.whole_ref, self.small, GATHER[k], d, half)

    def put(self, k, slot, d, half, to):
        ref = self.ref(k, d, half)
        remote(ref, ref, self.send.at[k], self.recv.at[k, slot], self.p.s, to).start()

    def got(self, k, slot, d):
        ref = self.ref(k, d)
        remote(ref, ref, self.send.at[k], self.recv.at[k, slot], self.p.s, self.p.sib).wait_recv()

    def hand(self, k, j, i):
        p = self.p
        d = p.dp(OFFS[j], OFFS[i])
        if k != HELP:
            self.put(k, 15, d, None, p.sib)
        elif (j, i) != (0, 0):
            self.give(j, i).start()

    def give(self, j, i):
        p = self.p
        d = p.dp(OFFS[j], OFFS[i])
        group = next(g for g, group in enumerate(BACK_GROUPS) if (j, i) in group)
        return remote(
            self.ref(HELP, d), self.ref(LATE, d), self.xsend.at[1], self.xrecv.at[X_GIVE + group], (p.s + 1) % 4, p.d
        )

    def lend(self):
        p = self.p
        return remote(
            self.ref(LATE, p.d), self.ref(HELP, p.d), self.xsend.at[0], self.xrecv.at[X_OWN], (p.s + 3) % 4, p.d
        )

    def spread(self, k, j):
        p = self.p
        d = p.dp(OFFS[j], 0)
        self.put(k, 3 + 3 * j, d, None, p.dp(0, 1))
        self.put(k, 4 + 3 * j, d, None, p.dp(0, 3))
        self.hand(k, j, 0)

    def first(self, k):
        p = self.p
        self.put(k, 0, p.d, None, p.dp(1, 0))
        self.put(k, 1, p.d, None, p.dp(3, 0))
        self.spread(k, 0)

    def ring(self, k):
        p = self.p
        left, right = p.dp(3, 0), p.dp(1, 0)
        self.got(k, 0, left)
        self.put(k, 2, left, 0, right)
        self.spread(k, 1)
        self.got(k, 1, right)
        self.put(k, 2, right, 1, left)
        self.spread(k, 2)

    def far(self, k):
        self.got(k, 2, self.p.dp(2, 0))
        self.spread(k, 3)

    def second(self, k, j):
        p = self.p
        low, high = p.dp(OFFS[j], 3), p.dp(OFFS[j], 1)
        self.got(k, 3 + 3 * j, low)
        self.put(k, 5 + 3 * j, low, 0, p.dp(0, 1))
        self.hand(k, j, 1)
        self.got(k, 4 + 3 * j, high)
        self.put(k, 5 + 3 * j, high, 1, p.dp(0, 3))
        self.hand(k, j, 2)

    def last(self, k, j):
        self.got(k, 5 + 3 * j, self.p.dp(OFFS[j], 2))
        self.hand(k, j, 3)

    def relay(self, group):
        p = self.p
        ref = self.many(LATE, len(BACK_GROUPS[group]))
        remote(ref, ref, self.xsend.at[1], self.xrecv.at[X_GIVE + group], p.s, p.sib).wait_recv()
        for j, i in BACK_GROUPS[group]:
            self.hand(LATE, j, i)

    def many(self, k, count):
        if k == HELP:
            return blocks(self.lent, None, LENT, count)
        return blocks(self.whole_ref, self.small, GATHER[k], count)

    def whole(self, k):
        ref = self.many(k, 16)
        remote(ref, ref, self.send.at[k], self.recv.at[k, 15], self.p.s, self.p.sib).wait_recv()

    def close(self):
        p = self.p

        def sent(k, count):
            ref = self.many(k, count)
            remote(ref, ref, self.send.at[k], self.recv.at[k, 15], p.s, p.sib).wait_send()

        for k in range(len(GATHER)):
            if k != LATE:
                sent(k, 31)

        @pl.when(p.s > 0)
        def _():
            sent(LATE, 31)

        @pl.when(p.s == 0)
        def _():
            sent(LATE, 16)
            self.lend().wait_send()

        @pl.when(p.s == 3)
        def _():
            sent(HELP, 15)
            ref = self.many(HELP, 15)
            remote(ref, ref, self.xsend.at[1], self.xrecv.at[X_GIVE], p.s, p.sib).wait_send()

    def run(self, own, ready):
        n, begun = len(GATHER), 0
        s = self.p.s

        def stage(step, k):
            if k == LATE:
                pl.when(s > 0)(lambda: step(k))
            elif 0 <= k < n:
                step(k)

        own(LATE)

        @pl.when(s == 0)
        def _():
            self.lend().start()
            self.hand(LATE, 0, 0)

        @pl.when(s == 3)
        def _():
            self.lend().wait_recv()
            for step in (self.first, self.ring, self.far):
                step(HELP)
            for j in range(4):
                self.second(HELP, j)
            for j in range(4):
                self.last(HELP, j)

        for t in range(n + 3):
            while begun < min(n, t + 3):
                if begun != LATE:
                    own(begun)
                stage(self.first, begun)
                begun += 1
            stage(self.ring, t)
            self.work.pop()
            stage(self.far, t - 1)
            self.work.pop()
            for j in range(4):
                stage(lambda k, j=j: self.second(k, j), t - 2)
                self.work.pop()
            for j in range(4):
                stage(lambda k, j=j: self.last(k, j), t - 3)
                self.work.pop()
            if 4 <= t < 8:
                pl.when(s == 0)(lambda t=t: self.relay(t - 4))

            self.work.pop()
            if t >= 3:
                self.whole(t - 3)
                ready(t - 3)
        self.work.drain()


def dot(a, b, ca, cb):
    return lax.dot_general(a, b, (((ca,), (cb,)), ((), ())), preferred_element_type=F32)


def centered(x):
    c = x - jnp.mean(x, axis=-1, keepdims=True)
    r = lax.rsqrt(jnp.mean(c * c, axis=-1, keepdims=True) + EPS)
    return c, r


def norm(x, gain, bias):
    c, r = centered(x)
    return c * r * gain + bias


def norm_back(x, gain, gy):
    c, r = centered(x)
    hat = c * r
    gh = gy * gain
    gx = r * (gh - jnp.mean(gh, axis=-1, keepdims=True) - hat * jnp.mean(gh * hat, axis=-1, keepdims=True))
    return gx, gy * hat


def rows_of(i, n):
    return pl.ds(pl.multiple_of(i * n, n), n)


def col_sum(x):
    return jnp.sum(x, axis=0, keepdims=True)


def row_sum(x):
    return dot(jnp.full((16, x.shape[0]), 1.0, BF16), x, 1, 0)[:1]


K0, K1 = 0.7978845608028654, 0.044715


def gelu(x):
    return 0.5 * x * (1.0 + jnp.tanh(K0 * (x + K1 * x * x * x)))


def gelu_both(x):
    t = jnp.tanh(K0 * (x + K1 * x * x * x))
    u = 0.5 * x * (1.0 + t)
    du = 0.5 * (1.0 + t) + 0.5 * x * (1.0 - t * t) * K0 * (1.0 + 3.0 * K1 * x * x)
    return u, du


def head_masks():
    lane = lax.broadcasted_iota(jnp.int32, (1, 128), 1)
    even = jnp.where(lane < 64, 1.0, 0.0)
    return even.astype(BF16), (1.0 - even).astype(BF16)


def two_rows(x, even, odd):
    return jnp.concatenate([x * even, x * odd], axis=0)


def each(count, unroll=1):
    def run(body):
        def step(i, carry):
            body(i)
            return carry

        lax.fori_loop(0, count, step, 0, unroll=unroll)

    return run


def stack(w, d0, nd, u, nu, cols=slice(0, WIDTH)):
    return w[pl.ds(d0, nd), u : u + nu, :, cols].reshape(nd * nu * 16, cols.stop - cols.start)


def head_columns():
    col = lax.broadcasted_iota(jnp.int32, (128, WIDTH), 1)
    head = lax.broadcasted_iota(jnp.int32, (128, WIDTH), 0)
    return jnp.where(col // 64 == head, 1.0, 0.0)


class Layer:
    def __init__(self, w, r):
        self.w, self.r = w, r


    def first_norm(self):
        r, pd = self.r, self.r["pd"]

        @each(4, 2)
        def _(i):
            at = rows_of(i, 32)
            r["a1"][at, :] = norm(r["zin"][at, :].astype(F32), pd[0:1, :], pd[3:4, :]).astype(BF16)

    def qkv(self, first=0, count=4):
        r = self.r

        @each(count, 4 if count == 4 else 1)
        def _(c):
            c = c + first
            at = rows_of(c, 768)
            acc = dot(r["a1"][...], stack(self.w, 8 * c, 8, IN, 6), 1, 1) + r["pq"][0:1, at]
            r["qkv"][:, at] = acc.astype(BF16)

    def attention(self, first=0, count=8):
        r, qkv = self.r, self.r["qkv"]
        even, odd = head_masks()

        @each(count, 4 if count == 8 else 1)
        def _(p):
            p = p + first
            cols = rows_of(p, 128)
            q = qkv[:, cols]
            k = qkv[:, pl.ds(pl.multiple_of(WIDTH + p * 128, 128), 128)]
            v = qkv[:, pl.ds(pl.multiple_of(2 * WIDTH + p * 128, 128), 128)]
            ok = r["ok"][...]
            sc = dot(two_rows(q, even, odd), k, 1, 1) * 0.125
            sc = jnp.where(jnp.concatenate([ok, ok], axis=0) > 0.5, sc, -1000000000.0)
            e = jnp.exp(sc - jnp.max(sc, axis=-1, keepdims=True))
            pr = e / jnp.sum(e, axis=-1, keepdims=True)
            r["p"][rows_of(p, 256), :] = pr
            pb = pr.astype(BF16)
            both = jnp.concatenate([pb[:TOK], pb[TOK:]], axis=1)
            mixed = dot(both, two_rows(v, even, odd), 1, 0)
            r["mixed"][:, cols] = mixed
            r["scaled"][:, cols] = (mixed * r["hs"][0:1, cols]).astype(BF16)

    def project(self):
        r = self.r
        r["attn"][...] = dot(r["scaled"][...], stack(self.w, 0, 32, OUT, 2), 1, 1) + r["pd"][6:7, :]

    def middle_norms(self):
        r, pd = self.r, self.r["pd"]

        @each(4, 2)
        def _(i):
            at = rows_of(i, 32)
            z2 = r["zin"][at, :].astype(F32) + norm(r["attn"][at, :], pd[1:2, :], pd[7:8, :])
            r["z2"][at, :] = z2
            r["a2"][at, :] = norm(z2, pd[2:3, :], pd[8:9, :]).astype(BF16)

    def up(self, first=0, count=4):
        r = self.r

        @each(count)
        def _(c):
            c = c + first
            cols = rows_of(c, 1024)
            r["ff"][:, cols] = dot(r["a2"][...], stack(self.w, 8 * c, 8, UP, 8), 1, 1) + r["pm"][11:12, cols]

    def inner_norm(self, first=0, count=8):
        r, pm = self.r, self.r["pm"]

        @each(count, 2 if count == 8 else 1)
        def _(i):
            i = i + first
            at = rows_of(i, 16)
            r["mid"][at, :] = norm(gelu(r["ff"][at, :]), pm[10:11, :], pm[12:13, :]).astype(BF16)

    def down(self, send_out):
        r = self.r
        for n in range(4):
            cols = slice(n * 256, (n + 1) * 256)
            acc = r["z2"][:, cols] + r["pd"][9:10, cols]
            for q in range(4):
                w = stack(self.w, 8 * n, 8, DOWN + 2 * q, 2)
                acc = acc + dot(r["mid"][:, q * 1024 : (q + 1) * 1024], w, 1, 1)
            r["out"][:, cols] = acc.astype(BF16)
            send_out(n)

    def prepare(self):
        r = self.r

        @each(8, 2)
        def _(i):
            at = rows_of(i, 16)
            u, du = gelu_both(r["ff"][at, :])
            c, s = centered(u)
            r["hat"][at, :] = (c * s).astype(BF16)
            r["slope"][at, :] = (du * s).astype(BF16)

        for name in ("gd", "gm"):
            r[name][...] = jnp.zeros_like(r[name])


    def back_down(self, *chunks):
        r = self.r
        for q in chunks:
            w = stack(self.w, 0, 32, DOWN + 2 * q, 2)
            r["ff"][:, q * 1024 : (q + 1) * 1024] = dot(r["gin"][...], w, 1, 0)

    def back_inner(self, first=0, count=8):
        r, pm = self.r, self.r["pm"]

        @each(count, 2 if count == 8 else 1)
        def _(i):
            i = i + first
            at = rows_of(i, 16)
            gh = r["ff"][at, :] * pm[10:11, :]
            hat = r["hat"][at, :].astype(F32)
            m1 = jnp.mean(gh, axis=-1, keepdims=True)
            m2 = jnp.mean(gh * hat, axis=-1, keepdims=True)
            r["ghid"][at, :] = ((gh - m1 - hat * m2) * r["slope"][at, :].astype(F32)).astype(BF16)

    def back_up(self, cols=slice(0, WIDTH)):
        r = self.r
        r["tw"][:, cols] = dot(r["ghid"][...], stack(self.w, 0, 32, UP, 8, cols), 1, 0)

    def back_middle(self):
        r, gd, pd = self.r, self.r["gd"], self.r["pd"]

        @each(4, 2)
        def _(i):
            at = rows_of(i, 32)
            ga2 = r["tw"][at, :]
            gz, gg = norm_back(r["z2"][at, :], pd[2:3, :], ga2)
            gd[2:3, :] += col_sum(gg)
            gd[8:9, :] += col_sum(ga2)
            gz = gz + r["gin"][at, :].astype(F32)
            r["gz2"][at, :] = gz
            gat, gg = norm_back(r["attn"][at, :], pd[1:2, :], gz)
            gd[1:2, :] += col_sum(gg)
            gd[7:8, :] += col_sum(gz)
            r["gattn"][at, :] = gat.astype(BF16)

    def back_project(self):
        r = self.r
        r["tw"][...] = dot(r["gattn"][...], stack(self.w, 0, 32, OUT, 2), 1, 0)

    def back_attention(self, first=0, count=8):
        r = self.r
        even, odd = head_masks()

        @each(count, 4 if count == 8 else 1)
        def _(p):
            p = p + first
            cols = rows_of(p, 128)
            kcols = pl.ds(pl.multiple_of(WIDTH + p * 128, 128), 128)
            vcols = pl.ds(pl.multiple_of(2 * WIDTH + p * 128, 128), 128)
            gs = r["tw"][:, cols]
            r["gh"][0:1, cols] = col_sum(gs * r["mixed"][:, cols])
            gmx = (gs * r["hs"][0:1, cols]).astype(BF16)
            q, k, v = r["qkv"][:, cols], r["qkv"][:, kcols], r["qkv"][:, vcols]
            gmx2 = two_rows(gmx, even, odd)
            gp = dot(gmx2, v, 1, 1)
            pr = r["p"][rows_of(p, 256), :]
            gsc = (pr * (gp - jnp.sum(pr * gp, axis=-1, keepdims=True))).astype(BF16)
            both = jnp.concatenate([gsc[:TOK], gsc[TOK:]], axis=1)
            r["gqkv"][:, cols] = (dot(both, two_rows(k, even, odd), 1, 0) * 0.125).astype(BF16)
            r["gqkv"][:, kcols] = (dot(gsc, two_rows(q, even, odd), 0, 0) * 0.125).astype(BF16)
            r["gqkv"][:, vcols] = dot(pr.astype(BF16), gmx2, 0, 0).astype(BF16)

    def back_qkv(self, cols=slice(0, WIDTH)):
        r = self.r
        r["tw"][:, cols] = dot(r["gqkv"][...], stack(self.w, 0, 32, IN, 6, cols), 1, 0)

    def back_first(self, send_out):
        r, gd, pd = self.r, self.r["gd"], self.r["pd"]
        for i in range(4):
            at = slice(i * 32, (i + 1) * 32)
            ga1 = r["tw"][at, :]
            gz, gg = norm_back(r["zin"][at, :].astype(F32), pd[0:1, :], ga1)
            r["gz"][at, :] = (gz + r["gz2"][at, :]).astype(BF16)
            send_out(i)
            gd[0:1, :] += col_sum(gg)
            gd[3:4, :] += col_sum(ga1)

    def inner_sums(self):
        r, gm = self.r, self.r["gm"]

        @each(8)
        def _(i):
            at = rows_of(i, 16)
            g = r["ff"][at, :]
            gm[10:11, :] += col_sum(g * r["hat"][at, :].astype(F32))
            gm[12:13, :] += col_sum(g)

        gm[11:12, :] = row_sum(r["ghid"][...])

    def other_sums(self):
        r, gd = self.r, self.r["gd"]
        gd[9:10, :] = row_sum(r["gin"][...])
        gd[6:7, :] = row_sum(r["gattn"][...])
        gd[4:5, :] = row_sum(r["gqkv"][:, :WIDTH])
        gd[5:6, :] = row_sum(r["gqkv"][:, 2 * WIDTH :])


    def grad_down(self, *chunks):
        r = self.r

        @each(4)
        def _(c):
            gt = r["gin"][:, rows_of(c, 256)].T
            for q in chunks:
                g = dot(gt, r["mid"][:, q * 1024 : (q + 1) * 1024], 1, 0).astype(BF16)
                self.w[pl.ds(8 * c, 8), DOWN + 2 * q : DOWN + 2 * q + 2] = g.reshape(8, 2, 16, WIDTH)

    def grad_up(self, first, count):
        r = self.r

        @each(count)
        def _(c):
            c = c + first
            g = dot(r["ghid"][:, rows_of(c, 512)].T, r["a2"][...], 1, 0).astype(BF16)
            self.w[pl.ds(4 * c, 4), UP : UP + 8] = g.reshape(4, 8, 16, WIDTH)

    def grad_in(self, first, count):
        r = self.r

        @each(count)
        def _(c):
            c = c + first
            g = dot(r["gqkv"][:, rows_of(c, 384)].T, r["a1"][...], 1, 0).astype(BF16)
            self.w[pl.ds(4 * c, 4), IN : IN + 6] = g.reshape(4, 6, 16, WIDTH)

    def grad_out(self, c):
        r = self.r
        g = dot(r["gattn"][:, c * 512 : (c + 1) * 512].T, r["scaled"][...], 1, 0).astype(BF16)
        self.w[pl.ds(16 * c, 16), OUT : OUT + 2] = g.reshape(16, 2, 16, WIDTH)

    def grad_small(self, small):
        r = self.r
        hsum = lax.dot_general(
            jnp.broadcast_to(r["gh"][0:1, :], (8, WIDTH)), head_columns(), (((1,), (1,)), ((), ())),
            precision=lax.Precision.HIGHEST, preferred_element_type=F32,
        )
        is13 = lax.broadcasted_iota(jnp.int32, (16, 128), 0) == 13
        heads = jnp.where(is13, jnp.concatenate([hsum, hsum], axis=0), 0.0)
        for d in range(32):
            a, b = (d // 4) * 128, d * 128
            small[d] = r["gd"][:, a : a + 128] + r["gm"][:, b : b + 128] + heads


class Scatter:
    def __init__(self, place, grads, small, sib, ssib, land, sland, back, send, recv, xsend, xrecv):
        self.p, self.grads, self.small = place, grads, small
        self.sib, self.ssib, self.land, self.sland, self.back = sib, ssib, land, sland, back
        self.send, self.recv, self.xsend, self.xrecv = send, recv, xsend, xrecv
        self.work = Work()

    def copy(self, k, slot, src, dst, to):
        return remote(src, dst, self.send.at[k], self.recv.at[k, slot], self.p.s, to)

    def go(self, k, slot, src, dst, to):
        self.copy(k, slot, src, dst, to).start()

    def got(self, k, slot, dst):
        self.copy(k, slot, dst, dst, self.p.sib).wait_recv()

    def block(self, k, of, og, half=None):
        d = self.p.dp(of, og)
        if k == AID:
            return piece_block(self.sib, None, DESK, d // 2, half)
        return piece_block(self.grads, self.small, SCATTER[k], d, half)

    def from_sib(self, k, slot, half=None):
        return piece_block(self.sib, self.ssib, SCATTER[k], slot, half)

    def landing(self, k, kind, slot):
        if k != AID and SCATTER[k] is SMALL:
            return self.sland[kind].at[slot]
        step = next((t for t, ks in enumerate(SCATTER_STEPS) if k in ks), len(SCATTER_STEPS))
        return self.land[kind].at[step % SHARE, slot]

    def landed(self, k, slot, kind, j=0):
        self.got(k, slot, self.landing(k, kind, pl.ds(2 * j, 2)))

    def to_sibling(self, k):
        p = self.p
        for i in (3, 1, 2, 0):
            for j in (3, 1, 2, 0):
                src = piece_block(self.grads, self.small, SCATTER[k], p.sib_dp(OFFS[j], OFFS[i]))
                self.go(k, 0 if i == 3 else 1, src, self.from_sib(k, i * 4 + j), p.sib)

    def lent_sum(self, i, j):
        p = self.p
        return remote(
            self.block(AWAY, OFFS[j], OFFS[i]), self.block(AID, OFFS[j], OFFS[i]), self.xsend.at[2],
            self.xrecv.at[X_SUMS + (2, 1, 1, 0)[i]], (p.s + 3) % 4, p.d,
        )

    def lend(self):
        for i in (3, 1, 2, 0):
            if i in (3, 1):
                self.arrived(AWAY, i == 3)
            for j in (3, 1, 2, 0):
                self.add(AWAY, self.block(AWAY, OFFS[j], OFFS[i]), [self.from_sib(AWAY, i * 4 + j)])
                self.lent_sum(i, j).start()

    def returned(self):
        p = self.p
        return remote(
            self.block(AID, 0, 0), self.back, self.xsend.at[3], self.xrecv.at[X_BACK], (p.s + 1) % 4, p.d
        )

    def arrived(self, k, far):
        first, count = (12, 4) if far else (0, 12)
        self.got(k, 0 if far else 1, blocks(self.sib, self.ssib, SCATTER[k], count, first))

    def lent_arrived(self, group):
        ref = blocks(self.sib, None, DESK, (4, 8, 4)[group])
        remote(ref, ref, self.xsend.at[2], self.xrecv.at[X_SUMS + group], self.p.s, self.p.sib).wait_recv()

    def add(self, k, dst, srcs, store=None):
        out = dst if store is None else store
        if store is None and not srcs:
            return
        if k != AID and SCATTER[k] is SMALL:
            out[...] = dst[...] + sum(src[...] for src in srcs)
            return

        @each(dst.shape[0])
        def _(u):
            acc = dst[u].astype(out.dtype)
            for src in srcs:
                acc = acc + src[u].astype(out.dtype)
            out[u] = acc

    def halves(self, k, j):
        p = self.p
        srcs = []
        if k == AID:
            if j == 3:
                self.lent_arrived(0)
        else:
            if j == 3:
                self.arrived(k, True)
            srcs = [self.from_sib(k, 12 + j)]
        self.add(k, self.block(k, OFFS[j], 2), srcs)
        for side, to in enumerate((p.dp(0, 1), p.dp(0, 3))):
            self.go(k, 2 + j, self.block(k, OFFS[j], 2, side), self.landing(k, 0, 2 * j + side), to)

    def wholes(self, k, j):
        p = self.p
        if j == 3:
            if k == AID:
                self.lent_arrived(1)
            else:
                self.arrived(k, False)
        self.landed(k, 2 + j, 0, j)
        for i, near, side in ((2, 1, 0), (1, 3, 1)):
            for half in range(2):
                srcs = [] if k == AID else [self.from_sib(k, i * 4 + j, half)]
                if half == side:
                    srcs.append(self.landing(k, 0, 2 * j + side))
                self.add(k, self.block(k, OFFS[j], near, half), srcs)
        for near, side in ((1, 0), (3, 1)):
            self.go(k, 6 + j, self.block(k, OFFS[j], near), self.landing(k, 1, 2 * j + side), p.dp(0, near))

    def far(self, k, j):
        p = self.p
        srcs = []
        if k != AID:
            srcs.append(self.from_sib(k, j))
        elif j == 3:
            self.lent_arrived(2)
        self.landed(k, 6 + j, 1, j)
        srcs += [self.landing(k, 1, 2 * j + side) for side in range(2)]
        self.add(k, self.block(k, OFFS[j], 0), srcs)
        if j == 3:
            self.go(k, 10, self.block(k, 2, 0, 0), self.landing(k, 2, 0), p.dp(1, 0))
            self.go(k, 10, self.block(k, 2, 0, 1), self.landing(k, 2, 1), p.dp(3, 0))

    def near(self, k):
        p = self.p
        self.landed(k, 10, 2)
        for near, side in ((1, 0), (3, 1)):
            self.add(k, self.block(k, near, 0, side), [self.landing(k, 2, side)])
        for near, side in ((1, 0), (3, 1)):
            self.go(k, 11, self.block(k, near, 0), self.landing(k, 3, side), p.dp(near, 0))

    def last(self, k, total, small_total):
        self.landed(k, 11, 3)
        srcs = [self.landing(k, 3, side) for side in range(2)]
        if k == AID:
            self.add(k, self.block(k, 0, 0), srcs)
            self.returned().start()
        elif SCATTER[k] is SMALL:
            self.add(k, self.block(k, 0, 0), srcs, store=small_total)
        else:
            u, n = SCATTER[k]
            self.add(k, self.block(k, 0, 0), srcs, store=total.at[pl.ds(u, n)])

    def aid(self):
        for step in (self.halves, self.wholes, self.far):
            for j in (3, 1, 2, 0):
                step(AID, j)
        self.near(AID)
        self.last(AID, None, None)

    def close(self):
        p = self.p

        def sent(k, count):
            if k == AID:
                ref = blocks(self.sib, None, DESK, count)
            else:
                ref = blocks(self.grads, self.small, SCATTER[k], count)
            self.copy(k, 0, ref, ref, p.sib).wait_send()

        for k in range(len(SCATTER)):
            if k != AWAY:
                sent(k, 31)

        @pl.when(p.s > 0)
        def _():
            sent(AWAY, 31)

        @pl.when(p.s == 0)
        def _():
            sent(AWAY, 16)
            ref = blocks(self.grads, None, LENT, 16)
            remote(ref, ref, self.xsend.at[2], self.xrecv.at[X_SUMS], p.s, p.sib).wait_send()

        @pl.when(p.s == 3)
        def _():
            sent(AID, 15)
            self.returned().wait_send()


HELD = dict(
    pd=((16, WIDTH), F32), pm=((16, FF), F32), pq=((1, QKV), F32), hs=((8, WIDTH), F32), ok=((TOK, TOK), F32),
    zin=((TOK, WIDTH), BF16), a1=((TOK, WIDTH), BF16), qkv=((TOK, QKV), BF16), p=((8 * 256, TOK), F32),
    mixed=((TOK, WIDTH), F32), scaled=((TOK, WIDTH), BF16), attn=((TOK, WIDTH), F32), z2=((TOK, WIDTH), F32),
    a2=((TOK, WIDTH), BF16), ff=((TOK, FF), F32), hat=((TOK, FF), BF16), slope=((TOK, FF), BF16), mid=((TOK, FF), BF16),
    gin=((TOK, WIDTH), BF16), ghid=((TOK, FF), BF16), gattn=((TOK, WIDTH), BF16), gqkv=((TOK, QKV), BF16),
    tw=((TOK, WIDTH), F32), gz2=((TOK, WIDTH), F32), gd=((16, WIDTH), F32), gm=((16, FF), F32), gh=((8, WIDTH), F32),
)
LANDING = ((8, 2), (8, 4), (2, 2), (2, 4))


def kernel(*refs):
    (tok, cot, live, seg, own_in, own_out, own_up, own_down, gains, vecs, mgain, mbias, hscale), refs = refs[:13], refs[13:]
    (out, gz, total, small_total), refs = refs[:4], refs[4:]
    (w, small, sib, ssib), refs = refs[:4], refs[4:]
    land, sland, refs = refs[:4], refs[4:8], refs[8:]
    back, refs = refs[0], refs[1:]
    r = dict(zip(HELD, refs), out=out, gz=gz)
    gsend, grecv, own_sem, xsend, xrecv, bsend, brecv, ssend, srecv, hsend, hrecv, sib_ok, lent_ok = refs[len(HELD) :]
    place = Place()
    layer = Layer(w, r)
    place.greet()

    loads = [
        pltpu.make_async_copy(
            own_down.at[:, :, pl.ds(q * 1024, 1024)], w.at[place.d, pl.ds(DOWN + 2 * q, 2)], own_sem.at[q]
        )
        for q in range(4)
    ] + [
        pltpu.make_async_copy(own_in, w.at[place.d, pl.ds(IN, 6)], own_sem.at[4]),
        pltpu.make_async_copy(own_out, w.at[place.d, pl.ds(OUT, 2)], own_sem.at[5]),
    ]
    for copy in loads:
        copy.start()
    token_load = pltpu.make_async_copy(tok, r["zin"], own_sem.at[6])
    cot_load = pltpu.make_async_copy(cot, r["gin"], own_sem.at[7])

    @pl.when(place.s == 0)
    def _():
        token_load.start()

    @pl.when(place.s == 3)
    def _():
        cot_load.start()

    mine = lax.broadcasted_iota(jnp.int32, (1, 128), 1) // 32 == place.d % 4

    def spot(x):
        x = x.astype(F32)
        return jnp.where(mine, jnp.concatenate([x, x, x, x], axis=1), 0.0)

    small[place.d, 0:3] = spot(gains[...])
    small[place.d, 3:10] = spot(vecs[...])
    small[place.d, 10:11] = mgain[...].astype(F32)
    small[place.d, 11:13] = mbias[...].astype(F32)
    small[place.d, 13:16] = jnp.zeros((3, 128), F32)
    place.barrier()

    def own(k):
        if k == 3:
            w[place.d, UP : UP + 8] = own_up[...].T.reshape(8, 16, WIDTH)
        for copy in {1: loads[4:5], 2: loads[5:6], 4: loads[2:4], 5: loads[:2]}.get(k, ()):
            copy.wait()

    def forward_copy(n):
        cols = pl.ds(n * 256, 256)
        return remote(
            out.at[:, cols], r["zin"].at[:, cols], xsend.at[n], xrecv.at[n], (place.s + 1) % 4, place.d
        )

    def send_forward(n):
        @pl.when(place.s < 3)
        def _():
            forward_copy(n).start()

    gather = Gather(place, w, small, sib, gsend, grecv, hsend, hrecv)

    def setup():
        for q in range(8):
            r["pd"][:, q * 128 : (q + 1) * 128] = small[4 * q] + small[4 * q + 1] + small[4 * q + 2] + small[4 * q + 3]
        for q in range(32):
            r["pm"][:, q * 128 : (q + 1) * 128] = small[q]
        r["pq"][:, :WIDTH] = r["pd"][4:5, :]
        r["pq"][:, WIDTH : 2 * WIDTH] = jnp.zeros((1, WIDTH), F32)
        r["pq"][:, 2 * WIDTH :] = r["pd"][5:6, :]
        heads = jnp.concatenate([hscale[...].astype(F32), jnp.zeros((1, 112), F32)], axis=1)
        r["hs"][...] = lax.dot_general(
            jnp.broadcast_to(heads, (8, 128)), head_columns(), (((1,), (0,)), ((), ())),
            precision=lax.Precision.HIGHEST, preferred_element_type=F32,
        )
        row = lax.broadcasted_iota(jnp.int32, (TOK, TOK), 0)
        col = lax.broadcasted_iota(jnp.int32, (TOK, TOK), 1)
        seg_key = jnp.broadcast_to(seg[...].astype(F32), (TOK, TOK))
        ok = (seg_key == seg_key.T) & (col <= row) & (row // 64 == col // 64)
        r["ok"][...] = jnp.where(ok, 1.0, 0.0)

    begins = place.s == 0

    def ready(k):
        work = gather.work
        if k == 0:
            setup()

            @pl.when(begins)
            def _():
                token_load.wait()
                layer.first_norm()
        elif k == 1:
            for c in range(2):
                work.add(lambda c=c: layer.qkv(2 * c, 2), begins)
            for c in range(4):
                work.add(lambda c=c: layer.attention(2 * c, 2), begins)
        elif k == 2:
            work.add(layer.project, begins)
            work.add(layer.middle_norms, begins)
        elif k == 3:
            for c in range(2):
                work.add(lambda c=c: layer.up(2 * c, 2), begins)
            for c in range(2):
                work.add(lambda c=c: layer.inner_norm(4 * c, 4), begins)

    gather.run(own, ready)

    @pl.when(begins)
    def _():
        layer.down(send_forward)

    @pl.when(place.s == 3)
    def _():
        cot_load.wait()

        @each(4)
        def _(i):
            at = rows_of(i, 32)
            row = lax.broadcasted_iota(jnp.int32, (32, WIDTH), 0) + 32 * i
            alive = row % 64 < jnp.where(row < 64, live[0], live[1])
            r["gin"][at, :] = jnp.where(alive, r["gin"][at, :].astype(F32), 0.0).astype(BF16)

    @pl.when(place.s > 0)
    def _():
        for n in range(4):
            forward_copy(n).wait_recv()
        layer.first_norm()
        layer.qkv()
        layer.attention()
        layer.project()
        layer.middle_norms()
        layer.up()
        layer.inner_norm()
        layer.down(send_forward)

    layer.prepare()
    gather.close()
    pl.semaphore_signal(sib_ok, inc=1, device_id=(place.s, place.sib), device_id_type=MESH)

    @pl.when(place.s < 3)
    def _():
        for n in range(4):
            forward_copy(n).wait_send()

    def backward_copy(i):
        at = pl.ds(i * 32, 32)
        return remote(gz.at[at], r["gin"].at[at], bsend.at[i], brecv.at[i], (place.s + 3) % 4, place.d)

    def send_backward(i):
        @pl.when(place.s > 0)
        def _():
            backward_copy(i).start()

    @pl.when(place.s < 3)
    def _():
        for i in range(4):
            backward_copy(i).wait_recv()

    @pl.when(place.s > 0)
    def _():
        layer.back_down(0, 1, 2, 3)
        layer.back_inner()
        layer.back_up()
        layer.back_middle()
        layer.back_project()
        layer.back_attention()
        layer.back_qkv()
        layer.back_first(send_backward)

    def first_section(*phases):
        @pl.when(place.s == 0)
        def _():
            for phase in phases:
                phase()

    scatter = Scatter(place, w, small, sib, ssib, land, sland, back, ssend, srecv, hsend, hrecv)
    n = len(SCATTER_STEPS)

    def stage(step, t):
        for k in SCATTER_STEPS[t] if 0 <= t < n else ():
            if k == AWAY:
                pl.when(place.s > 0)(lambda k=k: step(k))
            else:
                step(k)
        scatter.work.pop()

    def flow(t):
        for late, step in enumerate((scatter.halves, scatter.wholes, scatter.far)):
            for j in (3, 1, 2, 0):
                stage(lambda k, j=j, step=step: step(k, j), t - 1 - late)
        stage(scatter.near, t - 4)
        stage(lambda k: scatter.last(k, total, small_total), t - 5)

    work = scatter.work
    halfs = (slice(0, 512), slice(512, 1024))
    for c in range(2):
        work.add(lambda c=c: layer.back_inner(4 * c, 4), begins)
    for half in halfs:
        work.add(lambda half=half: layer.back_up(half), begins)
    for c in range(8):
        work.add(lambda c=c: layer.grad_up(c, 1))
    work.add(lambda: scatter.to_sibling(1))
    work.add(lambda: scatter.to_sibling(2), tag="up")
    work.add(layer.back_middle, begins)
    work.add(layer.back_project, begins)
    for c in range(4):
        work.add(lambda c=c: layer.back_attention(2 * c, 2), begins)
    for half in halfs:
        work.add(lambda half=half: layer.back_qkv(half), begins)
    work.add(lambda: layer.back_first(send_backward), begins)
    for c in range(8):
        work.add(lambda c=c: layer.grad_in(c, 1))
    for c in range(2):
        work.add(lambda c=c: layer.grad_out(c))
    work.add(lambda: scatter.to_sibling(3))
    work.add(lambda: scatter.to_sibling(5), tag="in")
    work.add(layer.inner_sums)
    work.add(layer.other_sums)
    work.add(lambda: layer.grad_small(small))
    work.add(lambda: scatter.to_sibling(4), tag="small")

    first_section(lambda: layer.back_down(2, 3))
    layer.grad_down(2, 3)
    pl.semaphore_wait(sib_ok, 1)
    scatter.to_sibling(0)
    first_section(lambda: layer.back_down(0, 1))
    layer.grad_down(0, 1)
    scatter.to_sibling(AWAY)
    flow(1)

    @pl.when(begins)
    def _():
        pl.semaphore_wait(lent_ok, 1)
        scatter.lend()

    work.until("up")
    flow(2)
    flow(3)

    @pl.when(place.s == 3)
    def _():
        pl.semaphore_signal(lent_ok, inc=1, device_id=(0, place.d), device_id_type=MESH)

    work.until("in")
    flow(4)
    work.until("small")
    for t in range(5, n + 5):
        flow(t)
    pl.when(place.s == 3)(scatter.aid)

    @pl.when(place.s == 0)
    def _():
        scatter.returned().wait_recv()
        u, count = LENT
        total[u : u + count] = back[...].astype(F32)

    scatter.close()

    @pl.when(place.s > 0)
    def _():
        for i in range(4):
            backward_copy(i).wait_send()


VSPEC = pl.BlockSpec(memory_space=pltpu.VMEM)
ASPEC = pl.BlockSpec(memory_space=pl.ANY)
SSPEC = pl.BlockSpec(memory_space=pltpu.SMEM)
DMA = pltpu.SemaphoreType.DMA


def run_layers(*args):
    g, s = (len(GATHER) + 1, 16), (len(SCATTER) + 1, 12)
    return pl.pallas_call(
        kernel,
        out_shape=[
            jax.ShapeDtypeStruct((TOK, WIDTH), BF16),
            jax.ShapeDtypeStruct((TOK, WIDTH), BF16),
            jax.ShapeDtypeStruct((UNITS, 16, WIDTH), F32),
            jax.ShapeDtypeStruct((16, 128), F32),
        ],
        in_specs=[ASPEC, ASPEC, SSPEC, VSPEC, ASPEC, ASPEC, VSPEC, ASPEC, VSPEC, VSPEC, VSPEC, VSPEC, VSPEC],
        out_specs=[VSPEC] * 4,
        scratch_shapes=[
            pltpu.VMEM((32, UNITS, 16, WIDTH), BF16),
            pltpu.VMEM((32, 16, 128), F32),
            pltpu.VMEM((16, UNITS, 16, WIDTH), BF16),
            pltpu.VMEM((16, 16, 128), F32),
        ]
        + [pltpu.VMEM((SHARE, slots, units, 16, WIDTH), BF16) for slots, units in LANDING]
        + [pltpu.VMEM((slots, 4 * units, 128), F32) for slots, units in LANDING]
        + [pltpu.VMEM((LENT[1], 16, WIDTH), BF16)]
        + [pltpu.VMEM(*v) for v in HELD.values()]
        + [DMA(g[:1]), DMA(g), DMA((8,)), DMA((4,)), DMA((4,)), DMA((4,)), DMA((4,)), DMA(s[:1]), DMA(s), DMA((4,)), DMA((9,))]
        + [pltpu.SemaphoreType.REGULAR] * 2,
        compiler_params=pltpu.CompilerParams(collective_id=1, has_side_effects=True, vmem_limit_bytes=VMEM_LIMIT),
        name="layers",
    )(*args)


def finish_kernel(out, gz, total, small, out2, gz2, g_in, g_out, g_up, g_down, g_gains, g_vecs, g_mgain, g_mbias, g_heads):
    out2[...] = out[...]
    gz2[...] = gz[...]
    g_in[...] = total[IN : IN + 6]
    g_out[...] = total[OUT : OUT + 2]
    for q in range(4):
        g_down[:, :, q * 1024 : (q + 1) * 1024] = total[DOWN + 2 * q : DOWN + 2 * q + 2]
    g_up[...] = total[UP : UP + 8].reshape(128, WIDTH).T
    lane = lax.axis_index("dp") % 4
    thin = jnp.zeros((10, 32), F32)
    for j in range(4):
        thin = jnp.where(lane == j, small[0:10, 32 * j : 32 * (j + 1)], thin)
    for i in range(3):
        g_gains[i] = thin[i : i + 1]
    for i in range(7):
        g_vecs[i] = thin[3 + i : 4 + i]
    g_mgain[...] = small[10:11, :]
    g_mbias[...] = small[11:13, :]
    g_heads[...] = small[13:14, :16]


def finish(*args):
    f = jax.ShapeDtypeStruct
    return pl.pallas_call(
        finish_kernel,
        out_shape=[
            f((TOK, WIDTH), BF16), f((TOK, WIDTH), BF16), f((6, 16, WIDTH), F32), f((2, 16, WIDTH), F32),
            f((WIDTH, 128), F32), f((2, 16, FF), F32), f((3, 1, 32), F32), f((7, 1, 32), F32), f((1, 128), F32),
            f((2, 128), F32), f((1, 16), F32),
        ],
        in_specs=[VSPEC] * 4,
        out_specs=[VSPEC] * 11,
        name="finish",
    )(*args)


def body(
    tokens, cotangent, live_counts, segments, attn_input, attn_output, feed_up, feed_down,
    norm_gains, vector_bias, mid_gain, mid_bias, head_scale,
):
    res = run_layers(
        tokens, cotangent, live_counts, segments[None, :], attn_input[0].T.reshape(6, 16, WIDTH),
        attn_output[0].T.reshape(2, 16, WIDTH), feed_up[0], feed_down[0].T.reshape(2, 16, FF), norm_gains[0],
        vector_bias[0], mid_gain, mid_bias[0], head_scale,
    )
    out, gz, g_in, g_out, g_up, g_down, g_gains, g_vecs, g_mgain, g_mbias, g_heads = finish(*res)
    return (
        out[None],
        gz[None],
        g_in.reshape(96, WIDTH).T[None],
        g_out.reshape(32, WIDTH).T[None],
        g_up[None],
        g_down.reshape(32, FF).T[None],
        g_gains.transpose(1, 0, 2),
        g_vecs.transpose(1, 0, 2),
        g_mgain,
        g_mbias[None],
        g_heads,
    )


def solution(mesh):
    return jax.shard_map(
        body,
        mesh=mesh,
        in_specs=(
            P("dp", None), P("dp", None), P("dp"), P("dp"),
            P("pipe", None, "dp"), P("pipe", None, "dp"), P("pipe", None, "dp"), P("pipe", None, "dp"),
            P("pipe", None, "dp"), P("pipe", None, "dp"), P("pipe", "dp"), P("pipe", None, "dp"), P("pipe", None),
        ),
        out_specs=(
            P("pipe", "dp", None), P("pipe", "dp", None),
            P("pipe", None, "dp"), P("pipe", None, "dp"), P("pipe", None, "dp"), P("pipe", None, "dp"),
            P("pipe", None, "dp"), P("pipe", None, "dp"), P("pipe", "dp"), P("pipe", None, "dp"), P("pipe", None),
        ),
        check_vma=False,
    )
```

```python
import jax
import jax.numpy as jnp
from jax import lax
from jax.experimental import pallas as pl
from jax.experimental.pallas import tpu as pltpu
from jax.sharding import PartitionSpec as P

MESH = pl.DeviceIdType.MESH
EPS = 1e-05
F32, BF16 = jnp.float32, jnp.bfloat16
VMEM_LIMIT = 61840 * 1024

TOK, WIDTH, FF, QKV = 128, 1024, 4096, 3072
IN, OUT, UP, DOWN, UNITS = 0, 6, 8, 16, 24
SMALL = "small"
GATHER = (SMALL, (IN, 6), (OUT, 2), (UP, 8), (DOWN + 4, 4), (DOWN, 4))
SCATTER_STEPS = ((0,), (1,), (2,), (3,), (4, 5), (6,))
SCATTER = ((DOWN + 4, 4), (UP, 4), (UP + 4, 4), (IN, 4), SMALL, (IN + 4, 4), (DOWN, 4))
LENT = (DOWN, 4)
LATE, HELP = 5, 6
AWAY, AID = 6, 7
DESK = (DOWN + 4, 4)
X_OWN, X_GIVE, X_SUMS, X_BACK = 0, 1, 5, 8
BACK_GROUPS = (
    ((1, 0), (2, 0), (3, 0)),
    ((0, 1), (0, 2), (1, 1), (1, 2)),
    ((2, 1), (2, 2), (3, 1), (3, 2)),
    ((0, 3), (1, 3), (2, 3), (3, 3)),
)
SHARE = 3
OFFS = (0, 3, 1, 2)


class Place:
    def __init__(self):
        self.s = lax.axis_index("pipe")
        d = lax.axis_index("dp")
        self.d = d
        self.c = d % 2
        y, z = (d // 2) % 4, d // 8
        self.f = y + self.c * (z - y)
        self.g = z + self.c * (y - z)
        self.sf = 2 + 6 * self.c
        self.sg = 8 - 6 * self.c
        self.sib = d + 1 - 2 * self.c
        rows = [((self.f + i) % 4) * self.sf for i in range(4)]
        columns = [((self.g + i) % 4) * self.sg for i in range(4)]
        self.table = [[row + column + self.c for column in columns] for row in rows]
        self.flip = 1 - 2 * self.c

    def dp(self, of, og):
        return self.table[of % 4][og % 4]

    def sib_dp(self, of, og):
        return self.table[og % 4][of % 4] + self.flip

    def greet(self):
        sem = pltpu.get_barrier_semaphore()
        near = [self.dp(1, 0), self.dp(3, 0), self.dp(0, 1), self.dp(0, 3), self.sib]
        near = [(self.s, to) for to in near] + [((self.s + by) % 4, self.d) for by in (1, 3)]
        for to in near:
            pl.semaphore_signal(sem, inc=1, device_id=to, device_id_type=MESH)

    def barrier(self):
        pl.semaphore_wait(pltpu.get_barrier_semaphore(), 7)


class Work:
    def __init__(self):
        self.items = []

    def add(self, slice_of_work, when=None, tag=None):
        self.items.append((slice_of_work, when, tag))

    def pop(self, count=1):
        for _ in range(min(count, len(self.items))):
            slice_of_work, when, _ = self.items.pop(0)
            if when is None:
                slice_of_work()
            else:
                pl.when(when)(slice_of_work)

    def until(self, tag):
        while any(tag == item[2] for item in self.items):
            self.pop()

    def drain(self):
        self.pop(len(self.items))


def remote(src, dst, send, recv, s, to):
    return pltpu.make_async_remote_copy(
        src_ref=src, dst_ref=dst, send_sem=send, recv_sem=recv, device_id=(s, to), device_id_type=MESH
    )


def piece_block(whole, small, piece, d, half=None):
    if piece is SMALL:
        return small.at[d] if half is None else small.at[d, pl.ds(8 * half, 8)]
    u, n = piece
    return whole.at[d, pl.ds(u, n)] if half is None else whole.at[d, pl.ds(u + half * (n // 2), n // 2)]


def blocks(whole, small, piece, count, first=0):
    if piece is SMALL:
        return small.at[pl.ds(first, count)]
    return whole.at[pl.ds(first, count), pl.ds(*piece)]


class Gather:
    def __init__(self, place, whole, small, lent, send, recv, xsend, xrecv):
        self.p, self.whole_ref, self.small, self.lent = place, whole, small, lent
        self.send, self.recv, self.xsend, self.xrecv = send, recv, xsend, xrecv
        self.work = Work()

    def ref(self, k, d, half=None):
        if k == HELP:
            u, n = LENT
            at = pl.ds(u, n) if half is None else pl.ds(u + half * (n // 2), n // 2)
            return self.lent.at[d // 2, at]
        return piece_block(self.whole_ref, self.small, GATHER[k], d, half)

    def put(self, k, slot, d, half, to):
        ref = self.ref(k, d, half)
        remote(ref, ref, self.send.at[k], self.recv.at[k, slot], self.p.s, to).start()

    def got(self, k, slot, d):
        ref = self.ref(k, d)
        remote(ref, ref, self.send.at[k], self.recv.at[k, slot], self.p.s, self.p.sib).wait_recv()

    def hand(self, k, j, i):
        p = self.p
        d = p.dp(OFFS[j], OFFS[i])
        if k != HELP:
            self.put(k, 15, d, None, p.sib)
        elif (j, i) != (0, 0):
            self.give(j, i).start()

    def give(self, j, i):
        p = self.p
        d = p.dp(OFFS[j], OFFS[i])
        group = next(g for g, group in enumerate(BACK_GROUPS) if (j, i) in group)
        return remote(
            self.ref(HELP, d), self.ref(LATE, d), self.xsend.at[1], self.xrecv.at[X_GIVE + group], (p.s + 1) % 4, p.d
        )

    def lend(self):
        p = self.p
        return remote(
            self.ref(LATE, p.d), self.ref(HELP, p.d), self.xsend.at[0], self.xrecv.at[X_OWN], (p.s + 3) % 4, p.d
        )

    def spread(self, k, j):
        p = self.p
        d = p.dp(OFFS[j], 0)
        self.put(k, 3 + 3 * j, d, None, p.dp(0, 1))
        self.put(k, 4 + 3 * j, d, None, p.dp(0, 3))
        self.hand(k, j, 0)

    def first(self, k):
        p = self.p
        self.put(k, 0, p.d, None, p.dp(1, 0))
        self.put(k, 1, p.d, None, p.dp(3, 0))
        self.spread(k, 0)

    def ring(self, k):
        p = self.p
        left, right = p.dp(3, 0), p.dp(1, 0)
        self.got(k, 0, left)
        self.put(k, 2, left, 0, right)
        self.spread(k, 1)
        self.got(k, 1, right)
        self.put(k, 2, right, 1, left)
        self.spread(k, 2)

    def far(self, k):
        self.got(k, 2, self.p.dp(2, 0))
        self.spread(k, 3)

    def second(self, k, j):
        p = self.p
        low, high = p.dp(OFFS[j], 3), p.dp(OFFS[j], 1)
        self.got(k, 3 + 3 * j, low)
        self.put(k, 5 + 3 * j, low, 0, p.dp(0, 1))
        self.hand(k, j, 1)
        self.got(k, 4 + 3 * j, high)
        self.put(k, 5 + 3 * j, high, 1, p.dp(0, 3))
        self.hand(k, j, 2)

    def last(self, k, j):
        self.got(k, 5 + 3 * j, self.p.dp(OFFS[j], 2))
        self.hand(k, j, 3)

    def relay(self, group):
        p = self.p
        ref = self.many(LATE, len(BACK_GROUPS[group]))
        remote(ref, ref, self.xsend.at[1], self.xrecv.at[X_GIVE + group], p.s, p.sib).wait_recv()
        for j, i in BACK_GROUPS[group]:
            self.hand(LATE, j, i)

    def many(self, k, count):
        if k == HELP:
            return blocks(self.lent, None, LENT, count)
        return blocks(self.whole_ref, self.small, GATHER[k], count)

    def whole(self, k):
        ref = self.many(k, 16)
        remote(ref, ref, self.send.at[k], self.recv.at[k, 15], self.p.s, self.p.sib).wait_recv()

    def close(self):
        p = self.p

        def sent(k, count):
            ref = self.many(k, count)
            remote(ref, ref, self.send.at[k], self.recv.at[k, 15], p.s, p.sib).wait_send()

        for k in range(len(GATHER)):
            if k != LATE:
                sent(k, 31)

        @pl.when(p.s > 0)
        def _():
            sent(LATE, 31)

        @pl.when(p.s == 0)
        def _():
            sent(LATE, 16)
            self.lend().wait_send()

        @pl.when(p.s == 3)
        def _():
            sent(HELP, 15)
            ref = self.many(HELP, 15)
            remote(ref, ref, self.xsend.at[1], self.xrecv.at[X_GIVE], p.s, p.sib).wait_send()

    def run(self, own, ready):
        n, begun = len(GATHER), 0
        s = self.p.s

        def stage(step, k):
            if k == LATE:
                pl.when(s > 0)(lambda: step(k))
            elif 0 <= k < n:
                step(k)

        own(LATE)

        @pl.when(s == 0)
        def _():
            self.lend().start()
            self.hand(LATE, 0, 0)

        @pl.when(s == 3)
        def _():
            self.lend().wait_recv()
            for step in (self.first, self.ring, self.far):
                step(HELP)
            for j in range(4):
                self.second(HELP, j)
            for j in range(4):
                self.last(HELP, j)

        for t in range(n + 3):
            while begun < min(n, t + 3):
                if begun != LATE:
                    own(begun)
                stage(self.first, begun)
                begun += 1
            stage(self.ring, t)
            self.work.pop()
            count = 1 if t <= n else 0
            stage(self.far, t - 1)
            self.work.pop(count)
            for j in range(4):
                stage(lambda k, j=j: self.second(k, j), t - 2)
                self.work.pop(count)
            for j in range(4):
                stage(lambda k, j=j: self.last(k, j), t - 3)
                self.work.pop(count)
            if 4 <= t < 8:
                pl.when(s == 0)(lambda t=t: self.relay(t - 4))
            self.work.pop(1 if count else 8)
            if t >= 3:
                self.whole(t - 3)
                ready(t - 3)
        self.work.drain()


def dot(a, b, ca, cb):
    return lax.dot_general(a, b, (((ca,), (cb,)), ((), ())), preferred_element_type=F32)


def centered(x):
    c = x - jnp.mean(x, axis=-1, keepdims=True)
    r = lax.rsqrt(jnp.mean(c * c, axis=-1, keepdims=True) + EPS)
    return c, r


def norm(x, gain, bias):
    c, r = centered(x)
    return c * r * gain + bias


def norm_back(x, gain, gy):
    c, r = centered(x)
    hat = c * r
    gh = gy * gain
    gx = r * (gh - jnp.mean(gh, axis=-1, keepdims=True) - hat * jnp.mean(gh * hat, axis=-1, keepdims=True))
    return gx, gy * hat


def rows_of(i, n):
    return pl.ds(pl.multiple_of(i * n, n), n)


def col_sum(x):
    return jnp.sum(x, axis=0, keepdims=True)


def row_sum(x):
    return dot(jnp.full((16, x.shape[0]), 1.0, BF16), x, 1, 0)[:1]


K0, K1 = 0.7978845608028654, 0.044715


def gelu(x):
    return 0.5 * x * (1.0 + jnp.tanh(K0 * (x + K1 * x * x * x)))


def gelu_both(x):
    t = jnp.tanh(K0 * (x + K1 * x * x * x))
    u = 0.5 * x * (1.0 + t)
    du = 0.5 * (1.0 + t) + 0.5 * x * (1.0 - t * t) * K0 * (1.0 + 3.0 * K1 * x * x)
    return u, du


def head_masks():
    lane = lax.broadcasted_iota(jnp.int32, (1, 128), 1)
    even = jnp.where(lane < 64, 1.0, 0.0)
    return even.astype(BF16), (1.0 - even).astype(BF16)


def two_rows(x, even, odd):
    return jnp.concatenate([x * even, x * odd], axis=0)


def each(count, unroll=1):
    def run(body):
        def step(i, carry):
            body(i)
            return carry

        lax.fori_loop(0, count, step, 0, unroll=unroll)

    return run


def stack(w, d0, nd, u, nu, cols=slice(0, WIDTH)):
    return w[pl.ds(d0, nd), u : u + nu, :, cols].reshape(nd * nu * 16, cols.stop - cols.start)


def head_columns():
    col = lax.broadcasted_iota(jnp.int32, (128, WIDTH), 1)
    head = lax.broadcasted_iota(jnp.int32, (128, WIDTH), 0)
    return jnp.where(col // 64 == head, 1.0, 0.0)


class Layer:
    def __init__(self, w, r):
        self.w, self.r = w, r


    def first_norm(self):
        r, pd = self.r, self.r["pd"]

        @each(4, 2)
        def _(i):
            at = rows_of(i, 32)
            r["a1"][at, :] = norm(r["zin"][at, :].astype(F32), pd[0:1, :], pd[3:4, :]).astype(BF16)

    def qkv(self, first=0, count=4):
        r = self.r

        @each(count, 4 if count == 4 else 1)
        def _(c):
            c = c + first
            at = rows_of(c, 768)
            acc = dot(r["a1"][...], stack(self.w, 8 * c, 8, IN, 6), 1, 1) + r["pq"][0:1, at]
            r["qkv"][:, at] = acc.astype(BF16)

    def attention(self, first=0, count=8):
        r, qkv = self.r, self.r["qkv"]
        even, odd = head_masks()

        @each(count, 4 if count == 8 else 1)
        def _(p):
            p = p + first
            cols = rows_of(p, 128)
            q = qkv[:, cols]
            k = qkv[:, pl.ds(pl.multiple_of(WIDTH + p * 128, 128), 128)]
            v = qkv[:, pl.ds(pl.multiple_of(2 * WIDTH + p * 128, 128), 128)]
            ok = r["ok"][...]
            sc = dot(two_rows(q, even, odd), k, 1, 1) * 0.125
            sc = jnp.where(jnp.concatenate([ok, ok], axis=0) > 0.5, sc, -1000000000.0)
            e = jnp.exp(sc - jnp.max(sc, axis=-1, keepdims=True))
            pr = e / jnp.sum(e, axis=-1, keepdims=True)
            r["p"][rows_of(p, 256), :] = pr
            pb = pr.astype(BF16)
            both = jnp.concatenate([pb[:TOK], pb[TOK:]], axis=1)
            mixed = dot(both, two_rows(v, even, odd), 1, 0)
            r["mixed"][:, cols] = mixed
            r["scaled"][:, cols] = (mixed * r["hs"][0:1, cols]).astype(BF16)

    def project(self):
        r = self.r
        r["attn"][...] = dot(r["scaled"][...], stack(self.w, 0, 32, OUT, 2), 1, 1) + r["pd"][6:7, :]

    def middle_norms(self):
        r, pd = self.r, self.r["pd"]

        @each(4, 2)
        def _(i):
            at = rows_of(i, 32)
            z2 = r["zin"][at, :].astype(F32) + norm(r["attn"][at, :], pd[1:2, :], pd[7:8, :])
            r["z2"][at, :] = z2
            r["a2"][at, :] = norm(z2, pd[2:3, :], pd[8:9, :]).astype(BF16)

    def up(self, first=0, count=4):
        r = self.r

        @each(count)
        def _(c):
            c = c + first
            cols = rows_of(c, 1024)
            r["ff"][:, cols] = dot(r["a2"][...], stack(self.w, 8 * c, 8, UP, 8), 1, 1) + r["pm"][11:12, cols]

    def inner_norm(self, first=0, count=8):
        r, pm = self.r, self.r["pm"]

        @each(count, 2 if count == 8 else 1)
        def _(i):
            i = i + first
            at = rows_of(i, 16)
            r["mid"][at, :] = norm(gelu(r["ff"][at, :]), pm[10:11, :], pm[12:13, :]).astype(BF16)

    def down(self, send_out):
        r = self.r
        for n in range(4):
            cols = slice(n * 256, (n + 1) * 256)
            acc = r["z2"][:, cols] + r["pd"][9:10, cols]
            for q in range(4):
                w = stack(self.w, 8 * n, 8, DOWN + 2 * q, 2)
                acc = acc + dot(r["mid"][:, q * 1024 : (q + 1) * 1024], w, 1, 1)
            r["out"][:, cols] = acc.astype(BF16)
            send_out(n)

    def prepare(self):
        r = self.r

        @each(8, 2)
        def _(i):
            at = rows_of(i, 16)
            u, du = gelu_both(r["ff"][at, :])
            c, s = centered(u)
            r["hat"][at, :] = (c * s).astype(BF16)
            r["slope"][at, :] = (du * s).astype(BF16)

        for name in ("gd", "gm"):
            r[name][...] = jnp.zeros_like(r[name])


    def back_down(self, *chunks):
        r = self.r
        for q in chunks:
            w = stack(self.w, 0, 32, DOWN + 2 * q, 2)
            r["ff"][:, q * 1024 : (q + 1) * 1024] = dot(r["gin"][...], w, 1, 0)

    def back_inner(self, first=0, count=8):
        r, pm = self.r, self.r["pm"]

        @each(count, 2 if count == 8 else 1)
        def _(i):
            i = i + first
            at = rows_of(i, 16)
            gh = r["ff"][at, :] * pm[10:11, :]
            hat = r["hat"][at, :].astype(F32)
            m1 = jnp.mean(gh, axis=-1, keepdims=True)
            m2 = jnp.mean(gh * hat, axis=-1, keepdims=True)
            r["ghid"][at, :] = ((gh - m1 - hat * m2) * r["slope"][at, :].astype(F32)).astype(BF16)

    def back_up(self, cols=slice(0, WIDTH)):
        r = self.r
        r["tw"][:, cols] = dot(r["ghid"][...], stack(self.w, 0, 32, UP, 8, cols), 1, 0)

    def back_middle(self):
        r, gd, pd = self.r, self.r["gd"], self.r["pd"]

        @each(4, 2)
        def _(i):
            at = rows_of(i, 32)
            ga2 = r["tw"][at, :]
            gz, gg = norm_back(r["z2"][at, :], pd[2:3, :], ga2)
            gd[2:3, :] += col_sum(gg)
            gd[8:9, :] += col_sum(ga2)
            gz = gz + r["gin"][at, :].astype(F32)
            r["gz2"][at, :] = gz
            gat, gg = norm_back(r["attn"][at, :], pd[1:2, :], gz)
            gd[1:2, :] += col_sum(gg)
            gd[7:8, :] += col_sum(gz)
            r["gattn"][at, :] = gat.astype(BF16)

    def back_project(self):
        r = self.r
        r["tw"][...] = dot(r["gattn"][...], stack(self.w, 0, 32, OUT, 2), 1, 0)

    def back_attention(self, first=0, count=8):
        r = self.r
        even, odd = head_masks()

        @each(count, 4 if count == 8 else 1)
        def _(p):
            p = p + first
            cols = rows_of(p, 128)
            kcols = pl.ds(pl.multiple_of(WIDTH + p * 128, 128), 128)
            vcols = pl.ds(pl.multiple_of(2 * WIDTH + p * 128, 128), 128)
            gs = r["tw"][:, cols]
            r["gh"][0:1, cols] = col_sum(gs * r["mixed"][:, cols])
            gmx = (gs * r["hs"][0:1, cols]).astype(BF16)
            q, k, v = r["qkv"][:, cols], r["qkv"][:, kcols], r["qkv"][:, vcols]
            gmx2 = two_rows(gmx, even, odd)
            gp = dot(gmx2, v, 1, 1)
            pr = r["p"][rows_of(p, 256), :]
            gsc = (pr * (gp - jnp.sum(pr * gp, axis=-1, keepdims=True))).astype(BF16)
            both = jnp.concatenate([gsc[:TOK], gsc[TOK:]], axis=1)
            r["gqkv"][:, cols] = (dot(both, two_rows(k, even, odd), 1, 0) * 0.125).astype(BF16)
            r["gqkv"][:, kcols] = (dot(gsc, two_rows(q, even, odd), 0, 0) * 0.125).astype(BF16)
            r["gqkv"][:, vcols] = dot(pr.astype(BF16), gmx2, 0, 0).astype(BF16)

    def back_qkv(self, cols=slice(0, WIDTH)):
        r = self.r
        r["tw"][:, cols] = dot(r["gqkv"][...], stack(self.w, 0, 32, IN, 6, cols), 1, 0)

    def back_first(self, send_out):
        r, gd, pd = self.r, self.r["gd"], self.r["pd"]
        for i in range(4):
            at = slice(i * 32, (i + 1) * 32)
            ga1 = r["tw"][at, :]
            gz, gg = norm_back(r["zin"][at, :].astype(F32), pd[0:1, :], ga1)
            r["gz"][at, :] = (gz + r["gz2"][at, :]).astype(BF16)
            send_out(i)
            gd[0:1, :] += col_sum(gg)
            gd[3:4, :] += col_sum(ga1)

    def inner_sums(self):
        r, gm = self.r, self.r["gm"]

        @each(8)
        def _(i):
            at = rows_of(i, 16)
            g = r["ff"][at, :]
            gm[10:11, :] += col_sum(g * r["hat"][at, :].astype(F32))
            gm[12:13, :] += col_sum(g)

        gm[11:12, :] = row_sum(r["ghid"][...])

    def other_sums(self):
        r, gd = self.r, self.r["gd"]
        gd[9:10, :] = row_sum(r["gin"][...])
        gd[6:7, :] = row_sum(r["gattn"][...])
        gd[4:5, :] = row_sum(r["gqkv"][:, :WIDTH])
        gd[5:6, :] = row_sum(r["gqkv"][:, 2 * WIDTH :])


    def grad_down(self, *chunks):
        r = self.r

        @each(4)
        def _(c):
            gt = r["gin"][:, rows_of(c, 256)].T
            for q in chunks:
                g = dot(gt, r["mid"][:, q * 1024 : (q + 1) * 1024], 1, 0).astype(BF16)
                self.w[pl.ds(8 * c, 8), DOWN + 2 * q : DOWN + 2 * q + 2] = g.reshape(8, 2, 16, WIDTH)

    def grad_up(self, first, count):
        r = self.r

        @each(count)
        def _(c):
            c = c + first
            g = dot(r["ghid"][:, rows_of(c, 512)].T, r["a2"][...], 1, 0).astype(BF16)
            self.w[pl.ds(4 * c, 4), UP : UP + 8] = g.reshape(4, 8, 16, WIDTH)

    def grad_in(self, first, count):
        r = self.r

        @each(count)
        def _(c):
            c = c + first
            g = dot(r["gqkv"][:, rows_of(c, 384)].T, r["a1"][...], 1, 0).astype(BF16)
            self.w[pl.ds(4 * c, 4), IN : IN + 6] = g.reshape(4, 6, 16, WIDTH)

    def grad_out(self, c):
        r = self.r
        g = dot(r["gattn"][:, c * 512 : (c + 1) * 512].T, r["scaled"][...], 1, 0).astype(BF16)
        self.w[pl.ds(16 * c, 16), OUT : OUT + 2] = g.reshape(16, 2, 16, WIDTH)

    def grad_small(self, small):
        r = self.r
        hsum = lax.dot_general(
            jnp.broadcast_to(r["gh"][0:1, :], (8, WIDTH)), head_columns(), (((1,), (1,)), ((), ())),
            precision=lax.Precision.HIGHEST, preferred_element_type=F32,
        )
        is13 = lax.broadcasted_iota(jnp.int32, (16, 128), 0) == 13
        heads = jnp.where(is13, jnp.concatenate([hsum, hsum], axis=0), 0.0)
        for d in range(32):
            a, b = (d // 4) * 128, d * 128
            small[d] = r["gd"][:, a : a + 128] + r["gm"][:, b : b + 128] + heads


class Scatter:
    def __init__(self, place, grads, small, sib, ssib, land, sland, back, send, recv, xsend, xrecv):
        self.p, self.grads, self.small = place, grads, small
        self.sib, self.ssib, self.land, self.sland, self.back = sib, ssib, land, sland, back
        self.send, self.recv, self.xsend, self.xrecv = send, recv, xsend, xrecv
        self.work = Work()

    def copy(self, k, slot, src, dst, to):
        return remote(src, dst, self.send.at[k], self.recv.at[k, slot], self.p.s, to)

    def go(self, k, slot, src, dst, to):
        self.copy(k, slot, src, dst, to).start()

    def got(self, k, slot, dst):
        self.copy(k, slot, dst, dst, self.p.sib).wait_recv()

    def block(self, k, of, og, half=None):
        d = self.p.dp(of, og)
        if k == AID:
            return piece_block(self.sib, None, DESK, d // 2, half)
        return piece_block(self.grads, self.small, SCATTER[k], d, half)

    def from_sib(self, k, slot, half=None):
        return piece_block(self.sib, self.ssib, SCATTER[k], slot, half)

    def landing(self, k, kind, slot):
        if k != AID and SCATTER[k] is SMALL:
            return self.sland[kind].at[slot]
        step = next((t for t, ks in enumerate(SCATTER_STEPS) if k in ks), len(SCATTER_STEPS))
        return self.land[kind].at[step % SHARE, slot]

    def landed(self, k, slot, kind, j=0):
        self.got(k, slot, self.landing(k, kind, pl.ds(2 * j, 2)))

    def to_sibling(self, k):
        p = self.p
        for i in (3, 1, 2, 0):
            for j in (3, 1, 2, 0):
                src = piece_block(self.grads, self.small, SCATTER[k], p.sib_dp(OFFS[j], OFFS[i]))
                self.go(k, 0 if i == 3 else 1, src, self.from_sib(k, i * 4 + j), p.sib)

    def lent_sum(self, i, j):
        p = self.p
        return remote(
            self.block(AWAY, OFFS[j], OFFS[i]), self.block(AID, OFFS[j], OFFS[i]), self.xsend.at[2],
            self.xrecv.at[X_SUMS + (2, 1, 1, 0)[i]], (p.s + 3) % 4, p.d,
        )

    def lend(self):
        for i in (3, 1, 2, 0):
            if i in (3, 1):
                self.arrived(AWAY, i == 3)
            for j in (3, 1, 2, 0):
                self.add(AWAY, self.block(AWAY, OFFS[j], OFFS[i]), [self.from_sib(AWAY, i * 4 + j)])
                self.lent_sum(i, j).start()

    def returned(self):
        p = self.p
        return remote(
            self.block(AID, 0, 0), self.back, self.xsend.at[3], self.xrecv.at[X_BACK], (p.s + 1) % 4, p.d
        )

    def arrived(self, k, far):
        first, count = (12, 4) if far else (0, 12)
        self.got(k, 0 if far else 1, blocks(self.sib, self.ssib, SCATTER[k], count, first))

    def lent_arrived(self, group):
        ref = blocks(self.sib, None, DESK, (4, 8, 4)[group])
        remote(ref, ref, self.xsend.at[2], self.xrecv.at[X_SUMS + group], self.p.s, self.p.sib).wait_recv()

    def add(self, k, dst, srcs, store=None):
        out = dst if store is None else store
        if store is None and not srcs:
            return
        if k != AID and SCATTER[k] is SMALL:
            out[...] = dst[...] + sum(src[...] for src in srcs)
            return

        @each(dst.shape[0])
        def _(u):
            acc = dst[u].astype(out.dtype)
            for src in srcs:
                acc = acc + src[u].astype(out.dtype)
            out[u] = acc

    def halves(self, k, j):
        p = self.p
        srcs = []
        if k == AID:
            if j == 3:
                self.lent_arrived(0)
        else:
            if j == 3:
                self.arrived(k, True)
            srcs = [self.from_sib(k, 12 + j)]
        self.add(k, self.block(k, OFFS[j], 2), srcs)
        for side, to in enumerate((p.dp(0, 1), p.dp(0, 3))):
            self.go(k, 2 + j, self.block(k, OFFS[j], 2, side), self.landing(k, 0, 2 * j + side), to)

    def wholes(self, k, j):
        p = self.p
        if j == 3:
            if k == AID:
                self.lent_arrived(1)
            else:
                self.arrived(k, False)
        self.landed(k, 2 + j, 0, j)
        for i, near, side in ((2, 1, 0), (1, 3, 1)):
            for half in range(2):
                srcs = [] if k == AID else [self.from_sib(k, i * 4 + j, half)]
                if half == side:
                    srcs.append(self.landing(k, 0, 2 * j + side))
                self.add(k, self.block(k, OFFS[j], near, half), srcs)
        for near, side in ((1, 0), (3, 1)):
            self.go(k, 6 + j, self.block(k, OFFS[j], near), self.landing(k, 1, 2 * j + side), p.dp(0, near))

    def far(self, k, j):
        p = self.p
        srcs = []
        if k != AID:
            srcs.append(self.from_sib(k, j))
        elif j == 3:
            self.lent_arrived(2)
        self.landed(k, 6 + j, 1, j)
        srcs += [self.landing(k, 1, 2 * j + side) for side in range(2)]
        self.add(k, self.block(k, OFFS[j], 0), srcs)
        if j == 3:
            self.go(k, 10, self.block(k, 2, 0, 0), self.landing(k, 2, 0), p.dp(1, 0))
            self.go(k, 10, self.block(k, 2, 0, 1), self.landing(k, 2, 1), p.dp(3, 0))

    def near(self, k):
        p = self.p
        self.landed(k, 10, 2)
        for near, side in ((1, 0), (3, 1)):
            self.add(k, self.block(k, near, 0, side), [self.landing(k, 2, side)])
        for near, side in ((1, 0), (3, 1)):
            self.go(k, 11, self.block(k, near, 0), self.landing(k, 3, side), p.dp(near, 0))

    def last(self, k, total, small_total):
        self.landed(k, 11, 3)
        srcs = [self.landing(k, 3, side) for side in range(2)]
        if k == AID:
            self.add(k, self.block(k, 0, 0), srcs)
            self.returned().start()
        elif SCATTER[k] is SMALL:
            self.add(k, self.block(k, 0, 0), srcs, store=small_total)
        else:
            u, n = SCATTER[k]
            self.add(k, self.block(k, 0, 0), srcs, store=total.at[pl.ds(u, n)])

    def aid(self):
        for step in (self.halves, self.wholes, self.far):
            for j in (3, 1, 2, 0):
                step(AID, j)
        self.near(AID)
        self.last(AID, None, None)

    def close(self):
        p = self.p

        def sent(k, count):
            if k == AID:
                ref = blocks(self.sib, None, DESK, count)
            else:
                ref = blocks(self.grads, self.small, SCATTER[k], count)
            self.copy(k, 0, ref, ref, p.sib).wait_send()

        for k in range(len(SCATTER)):
            if k != AWAY:
                sent(k, 31)

        @pl.when(p.s > 0)
        def _():
            sent(AWAY, 31)

        @pl.when(p.s == 0)
        def _():
            sent(AWAY, 16)
            ref = blocks(self.grads, None, LENT, 16)
            remote(ref, ref, self.xsend.at[2], self.xrecv.at[X_SUMS], p.s, p.sib).wait_send()

        @pl.when(p.s == 3)
        def _():
            sent(AID, 15)
            self.returned().wait_send()


HELD = dict(
    pd=((16, WIDTH), F32), pm=((16, FF), F32), pq=((1, QKV), F32), hs=((8, WIDTH), F32), ok=((TOK, TOK), F32),
    zin=((TOK, WIDTH), BF16), a1=((TOK, WIDTH), BF16), qkv=((TOK, QKV), BF16), p=((8 * 256, TOK), F32),
    mixed=((TOK, WIDTH), F32), scaled=((TOK, WIDTH), BF16), attn=((TOK, WIDTH), F32), z2=((TOK, WIDTH), F32),
    a2=((TOK, WIDTH), BF16), ff=((TOK, FF), F32), hat=((TOK, FF), BF16), slope=((TOK, FF), BF16), mid=((TOK, FF), BF16),
    gin=((TOK, WIDTH), BF16), ghid=((TOK, FF), BF16), gattn=((TOK, WIDTH), BF16), gqkv=((TOK, QKV), BF16),
    tw=((TOK, WIDTH), F32), gz2=((TOK, WIDTH), F32), gd=((16, WIDTH), F32), gm=((16, FF), F32), gh=((8, WIDTH), F32),
)
LANDING = ((8, 2), (8, 4), (2, 2), (2, 4))


def kernel(*refs):
    (tok, cot, live, seg, own_in, own_out, own_up, own_down, gains, vecs, mgain, mbias, hscale), refs = refs[:13], refs[13:]
    (out, gz, total, small_total), refs = refs[:4], refs[4:]
    (w, small, sib, ssib), refs = refs[:4], refs[4:]
    land, sland, refs = refs[:4], refs[4:8], refs[8:]
    back, refs = refs[0], refs[1:]
    r = dict(zip(HELD, refs), out=out, gz=gz)
    gsend, grecv, own_sem, xsend, xrecv, bsend, brecv, ssend, srecv, hsend, hrecv, sib_ok, lent_ok = refs[len(HELD) :]
    place = Place()
    layer = Layer(w, r)
    place.greet()

    loads = [
        pltpu.make_async_copy(
            own_down.at[:, :, pl.ds(q * 1024, 1024)], w.at[place.d, pl.ds(DOWN + 2 * q, 2)], own_sem.at[q]
        )
        for q in range(4)
    ] + [
        pltpu.make_async_copy(own_in, w.at[place.d, pl.ds(IN, 6)], own_sem.at[4]),
        pltpu.make_async_copy(own_out, w.at[place.d, pl.ds(OUT, 2)], own_sem.at[5]),
    ]
    for copy in loads:
        copy.start()
    token_load = pltpu.make_async_copy(tok, r["zin"], own_sem.at[6])
    cot_load = pltpu.make_async_copy(cot, r["gin"], own_sem.at[7])

    @pl.when(place.s == 0)
    def _():
        token_load.start()

    @pl.when(place.s == 3)
    def _():
        cot_load.start()

    mine = lax.broadcasted_iota(jnp.int32, (1, 128), 1) // 32 == place.d % 4

    def spot(x):
        x = x.astype(F32)
        return jnp.where(mine, jnp.concatenate([x, x, x, x], axis=1), 0.0)

    small[place.d, 0:3] = spot(gains[...])
    small[place.d, 3:10] = spot(vecs[...])
    small[place.d, 10:11] = mgain[...].astype(F32)
    small[place.d, 11:13] = mbias[...].astype(F32)
    small[place.d, 13:16] = jnp.zeros((3, 128), F32)
    place.barrier()

    def own(k):
        if k == 3:
            w[place.d, UP : UP + 8] = own_up[...].T.reshape(8, 16, WIDTH)
        for copy in {1: loads[4:5], 2: loads[5:6], 4: loads[2:4], 5: loads[:2]}.get(k, ()):
            copy.wait()

    def forward_copy(n):
        cols = pl.ds(n * 256, 256)
        return remote(
            out.at[:, cols], r["zin"].at[:, cols], xsend.at[n], xrecv.at[n], (place.s + 1) % 4, place.d
        )

    def send_forward(n):
        @pl.when(place.s < 3)
        def _():
            forward_copy(n).start()

    gather = Gather(place, w, small, sib, gsend, grecv, hsend, hrecv)

    def setup():
        for q in range(8):
            r["pd"][:, q * 128 : (q + 1) * 128] = small[4 * q] + small[4 * q + 1] + small[4 * q + 2] + small[4 * q + 3]
        for q in range(32):
            r["pm"][:, q * 128 : (q + 1) * 128] = small[q]
        r["pq"][:, :WIDTH] = r["pd"][4:5, :]
        r["pq"][:, WIDTH : 2 * WIDTH] = jnp.zeros((1, WIDTH), F32)
        r["pq"][:, 2 * WIDTH :] = r["pd"][5:6, :]
        heads = jnp.concatenate([hscale[...].astype(F32), jnp.zeros((1, 112), F32)], axis=1)
        r["hs"][...] = lax.dot_general(
            jnp.broadcast_to(heads, (8, 128)), head_columns(), (((1,), (0,)), ((), ())),
            precision=lax.Precision.HIGHEST, preferred_element_type=F32,
        )
        row = lax.broadcasted_iota(jnp.int32, (TOK, TOK), 0)
        col = lax.broadcasted_iota(jnp.int32, (TOK, TOK), 1)
        seg_key = jnp.broadcast_to(seg[...].astype(F32), (TOK, TOK))
        ok = (seg_key == seg_key.T) & (col <= row) & (row // 64 == col // 64)
        r["ok"][...] = jnp.where(ok, 1.0, 0.0)

    begins = place.s == 0

    def ready(k):
        work = gather.work
        if k == 0:
            setup()

            @pl.when(begins)
            def _():
                token_load.wait()
                layer.first_norm()
        elif k == 1:
            for c in range(2):
                work.add(lambda c=c: layer.qkv(2 * c, 2), begins)
            for c in range(4):
                work.add(lambda c=c: layer.attention(2 * c, 2), begins)
        elif k == 2:
            work.add(layer.project, begins)
            work.add(layer.middle_norms, begins)
        elif k == 3:
            for c in range(2):
                work.add(lambda c=c: layer.up(2 * c, 2), begins)
            for c in range(2):
                work.add(lambda c=c: layer.inner_norm(4 * c, 4), begins)

    gather.run(own, ready)

    @pl.when(begins)
    def _():
        layer.down(send_forward)

    @pl.when(place.s == 3)
    def _():
        cot_load.wait()

        @each(4)
        def _(i):
            at = rows_of(i, 32)
            row = lax.broadcasted_iota(jnp.int32, (32, WIDTH), 0) + 32 * i
            alive = row % 64 < jnp.where(row < 64, live[0], live[1])
            r["gin"][at, :] = jnp.where(alive, r["gin"][at, :].astype(F32), 0.0).astype(BF16)

    @pl.when(place.s > 0)
    def _():
        for n in range(4):
            forward_copy(n).wait_recv()
        layer.first_norm()
        layer.qkv()
        layer.attention()
        layer.project()
        layer.middle_norms()
        layer.up()
        layer.inner_norm()
        layer.down(send_forward)

    layer.prepare()
    gather.close()
    pl.semaphore_signal(sib_ok, inc=1, device_id=(place.s, place.sib), device_id_type=MESH)

    @pl.when(place.s < 3)
    def _():
        for n in range(4):
            forward_copy(n).wait_send()

    def backward_copy(i):
        at = pl.ds(i * 32, 32)
        return remote(gz.at[at], r["gin"].at[at], bsend.at[i], brecv.at[i], (place.s + 3) % 4, place.d)

    def send_backward(i):
        @pl.when(place.s > 0)
        def _():
            backward_copy(i).start()

    @pl.when(place.s < 3)
    def _():
        for i in range(4):
            backward_copy(i).wait_recv()

    @pl.when(place.s > 0)
    def _():
        layer.back_down(0, 1, 2, 3)
        layer.back_inner()
        layer.back_up()
        layer.back_middle()
        layer.back_project()
        layer.back_attention()
        layer.back_qkv()
        layer.back_first(send_backward)

    def first_section(*phases):
        @pl.when(place.s == 0)
        def _():
            for phase in phases:
                phase()

    scatter = Scatter(place, w, small, sib, ssib, land, sland, back, ssend, srecv, hsend, hrecv)
    n = len(SCATTER_STEPS)

    def stage(step, t):
        for k in SCATTER_STEPS[t] if 0 <= t < n else ():
            if k == AWAY:
                pl.when(place.s > 0)(lambda k=k: step(k))
            else:
                step(k)
        scatter.work.pop()

    def flow(t):
        for late, step in enumerate((scatter.halves, scatter.wholes, scatter.far)):
            for j in (3, 1, 2, 0):
                stage(lambda k, j=j, step=step: step(k, j), t - 1 - late)
        stage(scatter.near, t - 4)
        stage(lambda k: scatter.last(k, total, small_total), t - 5)

    work = scatter.work
    halfs = (slice(0, 512), slice(512, 1024))
    for c in range(2):
        work.add(lambda c=c: layer.back_inner(4 * c, 4), begins)
    for half in halfs:
        work.add(lambda half=half: layer.back_up(half), begins)
    for c in range(8):
        work.add(lambda c=c: layer.grad_up(c, 1))
    work.add(lambda: scatter.to_sibling(1))
    work.add(lambda: scatter.to_sibling(2), tag="up")
    work.add(layer.back_middle, begins)
    work.add(layer.back_project, begins)
    for c in range(4):
        work.add(lambda c=c: layer.back_attention(2 * c, 2), begins)
    for half in halfs:
        work.add(lambda half=half: layer.back_qkv(half), begins)
    work.add(lambda: layer.back_first(send_backward), begins)
    for c in range(8):
        work.add(lambda c=c: layer.grad_in(c, 1))
    for c in range(2):
        work.add(lambda c=c: layer.grad_out(c))
    work.add(lambda: scatter.to_sibling(3))
    work.add(lambda: scatter.to_sibling(5), tag="in")
    work.add(layer.inner_sums)
    work.add(layer.other_sums)
    work.add(lambda: layer.grad_small(small))
    work.add(lambda: scatter.to_sibling(4), tag="small")

    first_section(lambda: layer.back_down(2, 3))
    layer.grad_down(2, 3)
    pl.semaphore_wait(sib_ok, 1)
    scatter.to_sibling(0)
    first_section(lambda: layer.back_down(0, 1))
    layer.grad_down(0, 1)
    scatter.to_sibling(AWAY)
    flow(1)

    @pl.when(begins)
    def _():
        pl.semaphore_wait(lent_ok, 1)
        scatter.lend()

    work.until("up")
    flow(2)
    flow(3)

    @pl.when(place.s == 3)
    def _():
        pl.semaphore_signal(lent_ok, inc=1, device_id=(0, place.d), device_id_type=MESH)

    work.until("in")
    flow(4)
    work.until("small")
    for t in range(5, n + 5):
        flow(t)
    pl.when(place.s == 3)(scatter.aid)

    @pl.when(place.s == 0)
    def _():
        scatter.returned().wait_recv()
        u, count = LENT
        total[u : u + count] = back[...].astype(F32)

    scatter.close()

    @pl.when(place.s > 0)
    def _():
        for i in range(4):
            backward_copy(i).wait_send()


VSPEC = pl.BlockSpec(memory_space=pltpu.VMEM)
ASPEC = pl.BlockSpec(memory_space=pl.ANY)
SSPEC = pl.BlockSpec(memory_space=pltpu.SMEM)
DMA = pltpu.SemaphoreType.DMA


def run_layers(*args):
    g, s = (len(GATHER) + 1, 16), (len(SCATTER) + 1, 12)
    return pl.pallas_call(
        kernel,
        out_shape=[
            jax.ShapeDtypeStruct((TOK, WIDTH), BF16),
            jax.ShapeDtypeStruct((TOK, WIDTH), BF16),
            jax.ShapeDtypeStruct((UNITS, 16, WIDTH), F32),
            jax.ShapeDtypeStruct((16, 128), F32),
        ],
        in_specs=[ASPEC, ASPEC, SSPEC, VSPEC, ASPEC, ASPEC, VSPEC, ASPEC, VSPEC, VSPEC, VSPEC, VSPEC, VSPEC],
        out_specs=[VSPEC] * 4,
        scratch_shapes=[
            pltpu.VMEM((32, UNITS, 16, WIDTH), BF16),
            pltpu.VMEM((32, 16, 128), F32),
            pltpu.VMEM((16, UNITS, 16, WIDTH), BF16),
            pltpu.VMEM((16, 16, 128), F32),
        ]
        + [pltpu.VMEM((SHARE, slots, units, 16, WIDTH), BF16) for slots, units in LANDING]
        + [pltpu.VMEM((slots, 4 * units, 128), F32) for slots, units in LANDING]
        + [pltpu.VMEM((LENT[1], 16, WIDTH), BF16)]
        + [pltpu.VMEM(*v) for v in HELD.values()]
        + [DMA(g[:1]), DMA(g), DMA((8,)), DMA((4,)), DMA((4,)), DMA((4,)), DMA((4,)), DMA(s[:1]), DMA(s), DMA((4,)), DMA((9,))]
        + [pltpu.SemaphoreType.REGULAR] * 2,
        compiler_params=pltpu.CompilerParams(collective_id=1, has_side_effects=True, vmem_limit_bytes=VMEM_LIMIT),
        name="layers",
    )(*args)


def finish_kernel(out, gz, total, small, out2, gz2, g_in, g_out, g_up, g_down, g_gains, g_vecs, g_mgain, g_mbias, g_heads):
    out2[...] = out[...]
    gz2[...] = gz[...]
    g_in[...] = total[IN : IN + 6]
    g_out[...] = total[OUT : OUT + 2]
    for q in range(4):
        g_down[:, :, q * 1024 : (q + 1) * 1024] = total[DOWN + 2 * q : DOWN + 2 * q + 2]
    g_up[...] = total[UP : UP + 8].reshape(128, WIDTH).T
    lane = lax.axis_index("dp") % 4
    thin = jnp.zeros((10, 32), F32)
    for j in range(4):
        thin = jnp.where(lane == j, small[0:10, 32 * j : 32 * (j + 1)], thin)
    for i in range(3):
        g_gains[i] = thin[i : i + 1]
    for i in range(7):
        g_vecs[i] = thin[3 + i : 4 + i]
    g_mgain[...] = small[10:11, :]
    g_mbias[...] = small[11:13, :]
    g_heads[...] = small[13:14, :16]


def finish(*args):
    f = jax.ShapeDtypeStruct
    return pl.pallas_call(
        finish_kernel,
        out_shape=[
            f((TOK, WIDTH), BF16), f((TOK, WIDTH), BF16), f((6, 16, WIDTH), F32), f((2, 16, WIDTH), F32),
            f((WIDTH, 128), F32), f((2, 16, FF), F32), f((3, 1, 32), F32), f((7, 1, 32), F32), f((1, 128), F32),
            f((2, 128), F32), f((1, 16), F32),
        ],
        in_specs=[VSPEC] * 4,
        out_specs=[VSPEC] * 11,
        name="finish",
    )(*args)


def body(
    tokens, cotangent, live_counts, segments, attn_input, attn_output, feed_up, feed_down,
    norm_gains, vector_bias, mid_gain, mid_bias, head_scale,
):
    res = run_layers(
        tokens, cotangent, live_counts, segments[None, :], attn_input[0].T.reshape(6, 16, WIDTH),
        attn_output[0].T.reshape(2, 16, WIDTH), feed_up[0], feed_down[0].T.reshape(2, 16, FF), norm_gains[0],
        vector_bias[0], mid_gain, mid_bias[0], head_scale,
    )
    out, gz, g_in, g_out, g_up, g_down, g_gains, g_vecs, g_mgain, g_mbias, g_heads = finish(*res)
    return (
        out[None],
        gz[None],
        g_in.reshape(96, WIDTH).T[None],
        g_out.reshape(32, WIDTH).T[None],
        g_up[None],
        g_down.reshape(32, FF).T[None],
        g_gains.transpose(1, 0, 2),
        g_vecs.transpose(1, 0, 2),
        g_mgain,
        g_mbias[None],
        g_heads,
    )


def solution(mesh):
    return jax.shard_map(
        body,
        mesh=mesh,
        in_specs=(
            P("dp", None), P("dp", None), P("dp"), P("dp"),
            P("pipe", None, "dp"), P("pipe", None, "dp"), P("pipe", None, "dp"), P("pipe", None, "dp"),
            P("pipe", None, "dp"), P("pipe", None, "dp"), P("pipe", "dp"), P("pipe", None, "dp"), P("pipe", None),
        ),
        out_specs=(
            P("pipe", "dp", None), P("pipe", "dp", None),
            P("pipe", None, "dp"), P("pipe", None, "dp"), P("pipe", None, "dp"), P("pipe", None, "dp"),
            P("pipe", None, "dp"), P("pipe", None, "dp"), P("pipe", "dp"), P("pipe", None, "dp"), P("pipe", None),
        ),
        check_vma=False,
    )
```
